256 devices in a mesh: row: 16 (over y, x), col: 16 (over z, core).
Axes of the slice: x: 4, y: 4, z: 8, core: 2. Of those that a mesh axis runs over, the one named last changes fastest.
Arguments:
- tiles: float32 [16, 16, 64, 128, 128], P('row', 'col'), may hold values from -0.125 to 0.125
- tile_rows: int32 [16, 16, 64], P('row', 'col'), may hold values from 0 to 63
- tile_cols: int32 [16, 16, 64], P('row', 'col'), may hold values from 0 to 127
- tile_count: int32 [16, 16], P('row', 'col'), may hold values from 32 to 64, as said below
- row_types: int32 [16, 64, 128], P('row', 'col'), may hold values from 0 to 1
- var_types: int32 [16, 128, 128], P('col', 'row'), may hold values from 0 to 1
- rhs: float32 [16, 64, 128], P('row', 'col'), may hold values from -6 to 6
- cost: float32 [16, 128, 128], P('col', 'row'), may hold values from -6 to 6
- primal_start: float32 [16, 128, 128], P('col', 'row'), may hold values from 0 to 1
- dual_start: float32 [16, 64, 128], P('row', 'col'), may hold values from -3 to 3
Outputs:
- primal_out: float32 [16, 128, 128], P('col', 'row')
- dual_out: float32 [16, 64, 128], P('row', 'col')
- primal_residual: float32 [2], replicated
- dual_residual: float32 [2], replicated
- gap: float32 [2], replicated
The draws below stay inside these ranges and needn't reach their ends.
Inputs may be any that keep to these rules, and one draw needn't show every extreme that they name: Slots from tile_count on hold entries that are not part of the matrix; in every draw some device uses all 64 slots.
All inputs are finite; a program needn't handle non-finite values.
Results may differ from the reference program's by a relative error of at most 0.0001.
Values sent between devices are 32-bit elements; how exact they have to be, the bound alone decides.
No kernel may reach another device: no remote copies, remote signals or barrier semaphores. Data moves between devices by JAX's collectives and lax.ppermute only.
A program may use at most 64 MiB of HBM per device.

```python
import jax
import jax.numpy as jnp
from jax import lax

TILE = 128
RB_DEV = 64
CB_DEV = 128
SLOTS = 64
ITERS = 2
NROWS = 131072
NCOLS = 262144
N_ROW = 16
N_COL = 16


def draw_tile_count(key, part):
    key = jax.random.fold_in(key, 7)
    count_key, chosen_key = jax.random.split(key)
    devices_all = N_ROW * N_COL
    filled = jax.random.randint(count_key, (devices_all,), SLOTS // 2, SLOTS + 1)
    chosen = jax.random.randint(chosen_key, (), 0, devices_all)
    filled = jnp.where(jnp.arange(devices_all) == chosen, SLOTS, filled)
    return filled.reshape(N_ROW, N_COL).astype(jnp.int32)


def place_ends(values, key, least, largest):
    extent = values.shape
    spot = [jax.random.randint(jax.random.fold_in(key, axis), (), 0, extent[axis]) for axis in range(len(extent))]
    values = values.at[tuple(spot)].set(least)
    longest = extent.index(max(extent))
    spot[longest] = (spot[longest] + 1) % extent[longest]
    return values.at[tuple(spot)].set(largest)


def level_of(key, shape, pieces, least, largest):
    loudness = 1.0
    for position, parts in pieces:
        heights = jax.random.uniform(jax.random.fold_in(jax.random.fold_in(key, 6), position), (parts,), jnp.float32, least / len(pieces), largest / len(pieces))
        loudness = loudness * jnp.repeat(jnp.exp(heights), shape[position] // parts).reshape((-1,) + (1,) * (len(shape) - 1 - position))
    return loudness


def scatter_about(stream_key, extent, scale, most, pieces=(), held_as=jnp.bfloat16):
    values = jax.random.normal(stream_key, extent, jnp.float32) * scale
    if len(pieces) > 0:
        values = level_of(stream_key, extent, pieces, -0.22, 0.18) * values
    return jnp.clip(values, min=-most, max=most).astype(held_as)


def setup_inputs(seed: int = 0) -> dict:
    splits = jax.random.split(jax.random.key(seed), 11)
    return {
        "tiles": scatter_about(splits[0], (N_ROW, N_COL, SLOTS, TILE, TILE), (SLOTS * N_COL * TILE // RB_DEV) ** -0.5, 0.125, ((0, 16), (1, 16)), jnp.float32),
        "tile_rows": place_ends(jax.random.randint(splits[1], (N_ROW, N_COL, SLOTS), 0, RB_DEV), jax.random.fold_in(splits[1], 1), 0, RB_DEV - 1).astype(jnp.int32),
        "tile_cols": place_ends(jax.random.randint(splits[2], (N_ROW, N_COL, SLOTS), 0, CB_DEV), jax.random.fold_in(splits[2], 1), 0, CB_DEV - 1).astype(jnp.int32),
        "tile_count": draw_tile_count(jax.random.fold_in(splits[10], 71), 0),
        "row_types": place_ends(jax.random.randint(splits[4], (N_ROW, RB_DEV, TILE), 0, 2), jax.random.fold_in(splits[4], 1), 0, 1).astype(jnp.int32),
        "var_types": place_ends(jax.random.randint(splits[5], (N_COL, CB_DEV, TILE), 0, 2), jax.random.fold_in(splits[5], 1), 0, 1).astype(jnp.int32),
        "rhs": scatter_about(splits[6], (N_ROW, RB_DEV, TILE), 1.0, 6.0, ((0, 16), (1, 16)), jnp.float32),
        "cost": scatter_about(splits[7], (N_COL, CB_DEV, TILE), 1.0, 6.0, ((0, 16), (1, 16)), jnp.float32),
        "primal_start": jnp.clip(1.0 * jax.random.uniform(splits[8], (N_COL, CB_DEV, TILE), jnp.float32) ** level_of(splits[8], (N_COL, CB_DEV, TILE), ((0, 16), (1, 16)), -0.2, 0.2), 0.0, 1.0),
        "dual_start": scatter_about(splits[9], (N_ROW, RB_DEV, TILE), 0.5, 3.0, ((0, 16), (1, 16)), jnp.float32),
    }


def clamp_primal(values, var_types):
    return jnp.where(var_types == 1, jnp.maximum(values, 0.0), jnp.clip(values, 0.0, 1.0))


def clamp_dual(values, row_types):
    return jnp.where(row_types == 1, jnp.maximum(values, 0.0), values)


def forward_all(flat_tiles, row_index, col_index, live_mask, vectors):
    picked = vectors[:, col_index, :]
    product = jnp.einsum("tij,vtj->vti", flat_tiles, picked, precision=lax.Precision.HIGHEST)
    product = product * live_mask[None, :, None].astype(vectors.dtype)
    result = jnp.zeros((vectors.shape[0], N_ROW * RB_DEV, TILE), vectors.dtype)
    return result.at[:, row_index, :].add(product)


def adjoint_all(flat_tiles, row_index, col_index, live_mask, vectors):
    picked = vectors[:, row_index, :]
    product = jnp.einsum("tij,vti->vtj", flat_tiles, picked, precision=lax.Precision.HIGHEST)
    product = product * live_mask[None, :, None].astype(vectors.dtype)
    result = jnp.zeros((vectors.shape[0], N_COL * CB_DEV, TILE), vectors.dtype)
    return result.at[:, col_index, :].add(product)


def reference(tiles, tile_rows, tile_cols, tile_count, row_types, var_types, rhs, cost, primal_start, dual_start):
    row_index = (jnp.arange(N_ROW, dtype=jnp.int32)[:, None, None] * RB_DEV + tile_rows).reshape(-1).astype(jnp.int32)
    col_index = (jnp.arange(N_COL, dtype=jnp.int32)[None, :, None] * CB_DEV + tile_cols).reshape(-1).astype(jnp.int32)
    live_mask = (jnp.arange(SLOTS, dtype=jnp.int32)[None, None, :] < tile_count[:, :, None]).reshape(-1)
    flat_tiles = tiles.reshape(-1, TILE, TILE)
    row_kind = row_types.reshape(1, N_ROW * RB_DEV, TILE)
    var_kind = var_types.reshape(1, N_COL * CB_DEV, TILE)
    rhs_flat = rhs.reshape(1, N_ROW * RB_DEV, TILE)
    cost_flat = cost.reshape(1, N_COL * CB_DEV, TILE)
    primal = primal_start.reshape(1, N_COL * CB_DEV, TILE)
    dual = dual_start.reshape(1, N_ROW * RB_DEV, TILE)
    history = []
    for turn in range(ITERS):
        gradient = adjoint_all(flat_tiles, row_index, col_index, live_mask, dual)
        primal_next = clamp_primal(primal - 0.4 * (cost_flat - gradient), var_kind)
        image = forward_all(flat_tiles, row_index, col_index, live_mask, 2.0 * primal_next - primal)
        dual_next = clamp_dual(dual + 0.4 * (rhs_flat - image), row_kind)
        primal, dual = primal_next, dual_next
        history.append((primal, dual))
    pair_primal = jnp.concatenate([primal, 0.5 * (history[0][0] + history[1][0])], 0)
    pair_dual = jnp.concatenate([dual, 0.5 * (history[0][1] + history[1][1])], 0)
    forward_pair = forward_all(flat_tiles, row_index, col_index, live_mask, pair_primal)
    adjoint_pair = adjoint_all(flat_tiles, row_index, col_index, live_mask, pair_dual)
    residual = rhs_flat - forward_pair
    residual = jnp.where(row_kind == 1, jnp.maximum(residual, 0.0), residual)
    reduced = cost_flat - adjoint_pair
    violation = jnp.where(var_kind == 1, jnp.minimum(reduced, 0.0), 0.0)
    box_term = jnp.sum(jnp.where(var_kind == 0, jnp.minimum(reduced, 0.0), 0.0), axis=(1, 2))
    primal_square = jnp.sum(residual * residual, axis=(1, 2))
    dual_square = jnp.sum(violation * violation, axis=(1, 2))
    cost_dot = jnp.sum(cost_flat * pair_primal, axis=(1, 2))
    rhs_dot = jnp.sum(rhs_flat * pair_dual, axis=(1, 2))
    primal_residual = primal_square / float(NROWS)
    dual_residual = dual_square / float(NCOLS)
    gap = (cost_dot - rhs_dot - box_term) / float(NCOLS)
    return primal.reshape(N_COL, CB_DEV, TILE), dual.reshape(N_ROW, RB_DEV, TILE), primal_residual, dual_residual, gap
```

```python
import jax
import jax.numpy as jnp
from jax import lax
from jax.experimental import pallas as pl
from jax.experimental.pallas import tpu as pltpu
from jax.sharding import PartitionSpec as P

N = 16
TILE = 128
ROW_BLOCKS = 64
COL_BLOCKS = 128
SLOTS = 64
ROWS_SHARE = ROW_BLOCKS // N
COLS_SHARE = COL_BLOCKS // N
NROWS = float(N * ROW_BLOCKS * TILE)
NCOLS = float(N * COL_BLOCKS * TILE)
UNROLL = 8
F32, BF16 = jnp.float32, jnp.bfloat16

ROW_MASKS = (1, 3, 4, 12)

VMEM = pl.BlockSpec(memory_space=pltpu.VMEM)
SMEM = pl.BlockSpec(memory_space=pltpu.SMEM)


def call(kernel, name, out_shapes, args, smem=0, smem_out=False, scratch=()):
    shapes = tuple(jax.ShapeDtypeStruct(s, d) for s, d in out_shapes)
    return pl.pallas_call(
        kernel,
        name=name,
        out_shape=shapes,
        in_specs=[SMEM] * smem + [VMEM] * (len(args) - smem),
        out_specs=tuple([SMEM if smem_out else VMEM] * len(shapes)),
        scratch_shapes=list(scratch),
        compiler_params=pltpu.CompilerParams(vmem_limit_bytes=32 * 2**20),
    )(*args)


def split(vector, copies):
    wide = jnp.broadcast_to(vector, (copies, TILE))
    lead = wide.astype(BF16).astype(F32)
    return [lead, wide - lead]


def adjoint_product(rows, cols, tile_pair, dual_ref, total):
    total[...] = jnp.zeros_like(total)

    def body(slot, carry):
        lhs = jnp.concatenate(split(dual_ref[pl.ds(rows[slot], 1), :], 8), 0).astype(BF16)
        lhs = jnp.concatenate([lhs, lhs], 1)
        product = jnp.dot(lhs, tile_pair(slot), preferred_element_type=F32)
        total[cols[slot]] += product[0:8] + product[8:16]
        return carry

    lax.fori_loop(0, SLOTS, body, 0, unroll=UNROLL)


def forward_product(rows, cols, tile_pair, primal_refs, total):
    total[...] = jnp.zeros_like(total)
    copies = 8 // len(primal_refs)

    def body(slot, carry):
        parts = [split(ref[pl.ds(cols[slot], 1), :], copies) for ref in primal_refs]
        lhs = jnp.concatenate([p[0] for p in parts] + [p[1] for p in parts], 0).astype(BF16)
        product = lax.dot_general(
            lhs, tile_pair(slot), (((1,), (1,)), ((), ())), preferred_element_type=F32
        )
        product = product[:, :TILE] + product[:, TILE:]
        total[rows[slot]] += product[0:8] + product[8:16]
        return carry

    lax.fori_loop(0, SLOTS, body, 0, unroll=UNROLL)


def clamp_primal(values, free):
    floor = jnp.maximum(values, 0.0)
    return jnp.where(free > 0.5, floor, jnp.minimum(floor, 1.0))


def clamp_dual(values, ineq):
    return jnp.where(ineq > 0.5, jnp.maximum(values, 0.0), values)


def first_adjoint(count, rows, cols, dual, tiles, gradient, pairs, total):
    def tile_pair(slot):
        tile = jnp.where(slot < count[0], tiles[slot], 0.0)
        lead = tile.astype(BF16)
        pair = jnp.concatenate([lead, (tile - lead.astype(F32)).astype(BF16)], 0)
        pairs[slot] = pair
        return pair

    adjoint_product(rows, cols, tile_pair, dual, total)
    gradient[...] = total[:, 0, :]


def first_forward(
    where, rows, cols, own, other, gathered, pairs, image, primal, start, cost, free, extended, total
):
    for place in range(N):
        device = where[0]
        for step, mask in enumerate(ROW_MASKS):
            if place >> step & 1:
                device = device ^ mask
        block = pl.ds(pl.multiple_of(device * COLS_SHARE, COLS_SHARE), COLS_SHARE)
        for k, ref in enumerate((start, cost, free)):
            ref[block, :] = gathered[place, k]
    gradient = own[...] + other[...]
    primal[...] = clamp_primal(start[...] - 0.4 * (cost[...] - gradient), free[...])
    extended[...] = 2.0 * primal[...] - start[...]
    forward_product(rows, cols, lambda slot: pairs[slot], [extended], total)
    image[...] = total[:, 0, :]


def second_adjoint(rows, cols, images, start, rhs, ineq, pairs, gradient, dual, total):
    image = jnp.sum(images[...], 0)
    dual[...] = clamp_dual(start[...] + 0.4 * (rhs[...] - image), ineq[...])
    adjoint_product(rows, cols, lambda slot: pairs[slot], dual, total)
    gradient[...] = total[:, 0, :]


def second_forward(
    where, rows, cols, own, other, before, cost, free, pairs, image, plain, primal, gradient, mine, extended, total
):
    gradient[...] = own[...] + other[...]
    primal[...] = clamp_primal(before[...] - 0.4 * (cost[...] - gradient[...]), free[...])
    extended[...] = 2.0 * primal[...] - before[...]
    mine[...] = primal[pl.ds(pl.multiple_of(where[0] * COLS_SHARE, COLS_SHARE), COLS_SHARE), :]
    forward_product(rows, cols, lambda slot: pairs[slot], [extended, primal], total)
    image[...] = total[:, 0, :]
    plain[...] = total[:, 4, :]


def third_adjoint(where, rows, cols, images, before, rhs, ineq, pairs, payload, mine, dual, total):
    image = images[0]
    plain = images[1]
    for k in range(1, N // 2):
        image = image + images[2 * k]
        plain = plain + images[2 * k + 1]
    earlier, bound, kind = before[...], rhs[...], ineq[...]
    dual[...] = clamp_dual(earlier + 0.4 * (bound - image), kind)
    mine[...] = dual[pl.ds(where[1] * ROWS_SHARE, ROWS_SHARE), :]
    adjoint_product(rows, cols, lambda slot: pairs[slot], dual, total)
    payload[0:COL_BLOCKS, :] = total[:, 0, :]
    terms = []
    for product in (plain, 0.5 * (3.0 * plain - image)):
        residual = bound - product
        residual = jnp.where(kind > 0.5, jnp.maximum(residual, 0.0), residual)
        terms.append(jnp.sum(residual * residual, 0, keepdims=True))
    for value in (dual[...], 0.5 * (earlier + dual[...])):
        terms.append(jnp.sum(bound * value, 0, keepdims=True))
    payload[COL_BLOCKS : COL_BLOCKS + 8, :] = jnp.concatenate(terms + terms, 0)


def column_terms(own, other, earlier, before, primal, cost, free, terms, row_terms):
    adjoint = own[0:COL_BLOCKS, :] + other[0:COL_BLOCKS, :]
    row_terms[...] = own[COL_BLOCKS:, :] + other[COL_BLOCKS:, :]
    price, kind = cost[...], free[...]
    rows = []
    for gradient, value in (
        (adjoint, primal[...]),
        (0.5 * (earlier[...] + adjoint), 0.5 * (before[...] + primal[...])),
    ):
        low = jnp.minimum(price - gradient, 0.0)
        violation = jnp.where(kind > 0.5, low, 0.0)
        box = jnp.where(kind > 0.5, 0.0, low)
        rows.append(jnp.sum(violation * violation, 0, keepdims=True))
        rows.append(jnp.sum(price * value, 0, keepdims=True))
        rows.append(jnp.sum(box, 0, keepdims=True))
    terms[...] = jnp.concatenate(rows + rows[:2], 0)


def measures(gathered, row_terms, primal_residual, dual_residual, gap):
    columns = jnp.sum(gathered[...], 0)
    rows = row_terms[...]
    for k in range(2):
        primal_residual[k] = jnp.sum(rows[k : k + 1]) * (1.0 / NROWS)
        dual_residual[k] = jnp.sum(columns[3 * k : 3 * k + 1]) * (1.0 / NCOLS)
        total = columns[3 * k + 1 : 3 * k + 2] - columns[3 * k + 2 : 3 * k + 3] - rows[2 + k : 3 + k]
        gap[k] = jnp.sum(total) * (1.0 / NCOLS)


def swap(values, axis, mask):
    return lax.ppermute(values, axis, [(i, i ^ mask) for i in range(N)])


def sum_over_row(values):
    for mask in ROW_MASKS[:-1]:
        values = values + swap(values, "row", mask)
    return values, swap(values, "row", ROW_MASKS[-1])


def shards(
    tiles, tile_rows, tile_cols, tile_count, row_types, var_types, rhs, cost, primal_start, dual_start
):
    tiles = tiles.reshape(SLOTS, TILE, TILE)
    rows, cols = tile_rows.reshape(-1), tile_cols.reshape(-1)
    count = tile_count.reshape(1)
    where = jnp.stack([lax.axis_index("row"), lax.axis_index("col")]).astype(jnp.int32)
    blocks = (ROW_BLOCKS, TILE)
    columns = (COL_BLOCKS, TILE)
    row_total = [pltpu.VMEM((ROW_BLOCKS, 8, TILE), F32)]
    col_total = [pltpu.VMEM((COL_BLOCKS, 8, TILE), F32)]

    row_side = jnp.concatenate([dual_start, rhs, row_types.astype(F32)], 0)
    row_side = lax.all_gather(row_side, "col", axis=1, tiled=True)
    dual0, rhs_full, ineq = row_side[0], row_side[1], row_side[2]

    gradient, pairs = call(
        first_adjoint,
        "first_adjoint",
        [(columns, F32), ((SLOTS, 2 * TILE, TILE), BF16)],
        (count, rows, cols, dual0, tiles),
        smem=3,
        scratch=col_total,
    )

    gathered = jnp.concatenate([primal_start, cost, var_types.astype(F32)], 0)
    gathered = gathered.reshape(3 * COLS_SHARE, TILE)
    for step, mask in enumerate(ROW_MASKS):
        other = swap(jnp.concatenate([gradient, gathered], 0), "row", mask)
        gathered = jnp.concatenate([gathered, other[COL_BLOCKS:]], 0)
        other = other[:COL_BLOCKS]
        if step < len(ROW_MASKS) - 1:
            gradient = gradient + other
    gathered = gathered.reshape(N, 3, COLS_SHARE, TILE)

    image, primal1, start_full, cost_full, free = call(
        first_forward,
        "first_forward",
        [(blocks, F32)] + [(columns, F32)] * 4,
        (where, rows, cols, gradient, other, gathered, pairs),
        smem=3,
        scratch=[pltpu.VMEM(columns, F32)] + row_total,
    )

    images = lax.all_gather(image, "col", axis=0, tiled=False)
    gradient, dual1 = call(
        second_adjoint,
        "second_adjoint",
        [(columns, F32), (blocks, F32)],
        (rows, cols, images, dual0, rhs_full, ineq, pairs),
        smem=2,
        scratch=col_total,
    )
    gradient, other = sum_over_row(gradient)

    image, plain, primal2, gradient2, primal_mine = call(
        second_forward,
        "second_forward",
        [(blocks, F32)] * 2 + [(columns, F32)] * 2 + [((COLS_SHARE, TILE), F32)],
        (where, rows, cols, gradient, other, primal1, cost_full, free, pairs),
        smem=3,
        scratch=[pltpu.VMEM(columns, F32)] + row_total,
    )

    second = where[1] % 2 == 1
    kept = jnp.where(second, plain, image)
    given = jnp.where(second, image, plain)
    images = lax.all_gather(kept + swap(given, "col", 1), "col", axis=0, tiled=False)

    payload, dual_mine, dual2 = call(
        third_adjoint,
        "third_adjoint",
        [((COL_BLOCKS + 8, TILE), F32), ((ROWS_SHARE, TILE), F32), (blocks, F32)],
        (where, rows, cols, images, dual1, rhs_full, ineq, pairs),
        smem=3,
        scratch=col_total,
    )
    payload, other = sum_over_row(payload)
    terms, row_terms = call(
        column_terms,
        "column_terms",
        [((8, TILE), F32)] * 2,
        (payload, other, gradient2, primal1, primal2, cost_full, free),
    )
    terms = lax.all_gather(terms, "col", axis=0, tiled=False)
    primal_residual, dual_residual, gap = call(
        measures, "measures", [((2,), F32)] * 3, (terms, row_terms), smem_out=True
    )
    return primal_mine[None], dual_mine[None], primal_residual, dual_residual, gap


def solution(mesh):
    in_specs = (
        P("row", "col", None, None, None),
        P("row", "col", None),
        P("row", "col", None),
        P("row", "col"),
        P("row", "col", None),
        P("col", "row", None),
        P("row", "col", None),
        P("col", "row", None),
        P("col", "row", None),
        P("row", "col", None),
    )
    out_specs = (P("col", "row", None), P("row", "col", None), P(), P(), P())
    return jax.shard_map(shards, mesh=mesh, in_specs=in_specs, out_specs=out_specs, check_vma=False)
```

```python
import jax
import jax.numpy as jnp
from jax import lax
from jax.experimental import pallas as pl
from jax.experimental.pallas import tpu as pltpu
from jax.sharding import Mesh
from jax.sharding import PartitionSpec as P

N = 16
TILE = 128
ROW_BLOCKS = 64
COL_BLOCKS = 128
SLOTS = 64
ROWS_SHARE = ROW_BLOCKS // N
COLS_SHARE = COL_BLOCKS // N
HALF = ROW_BLOCKS // 2
NROWS = float(N * ROW_BLOCKS * TILE)
NCOLS = float(N * COL_BLOCKS * TILE)
UNROLL = 8
F32, BF16 = jnp.float32, jnp.bfloat16

SLOT_ROWS, SLOT_COLS, COUNT, AT_Y, AT_X, AT_Z, AT_CORE = range(7)

VMEM = pl.BlockSpec(memory_space=pltpu.VMEM)
SMEM = pl.BlockSpec(memory_space=pltpu.SMEM)


def call(kernel, name, out_shapes, args, smem=0, smem_out=False, scratch=()):
    shapes = tuple(jax.ShapeDtypeStruct(s, d) for s, d in out_shapes)
    return pl.pallas_call(
        kernel,
        name=name,
        out_shape=shapes,
        in_specs=[SMEM] * smem + [VMEM] * (len(args) - smem),
        out_specs=tuple([SMEM if smem_out else VMEM] * len(shapes)),
        scratch_shapes=list(scratch),
        compiler_params=pltpu.CompilerParams(vmem_limit_bytes=8 * 2**20),
    )(*args)


def split(vector, copies):
    wide = jnp.broadcast_to(vector, (copies, TILE))
    lead = wide.astype(BF16).astype(F32)
    return [lead, wide - lead]


def adjoint_product(table, tile_pair, dual_ref, total):
    total[...] = jnp.zeros_like(total)

    def body(slot, carry):
        lhs = jnp.concatenate(split(dual_ref[pl.ds(table[SLOT_ROWS, slot], 1), :], 8), 0).astype(BF16)
        lhs = jnp.concatenate([lhs, lhs], 1)
        product = jnp.dot(lhs, tile_pair(slot), preferred_element_type=F32)
        total[table[SLOT_COLS, slot]] += product[0:8] + product[8:16]
        return carry

    lax.fori_loop(0, SLOTS, body, 0, unroll=UNROLL)


def forward_product(table, tile_pair, primal_refs, total):
    total[...] = jnp.zeros_like(total)
    copies = 8 // len(primal_refs)

    def body(slot, carry):
        parts = [split(ref[pl.ds(table[SLOT_COLS, slot], 1), :], copies) for ref in primal_refs]
        lhs = jnp.concatenate([p[0] for p in parts] + [p[1] for p in parts], 0).astype(BF16)
        product = lax.dot_general(
            lhs, tile_pair(slot), (((1,), (1,)), ((), ())), preferred_element_type=F32
        )
        product = product[:, :TILE] + product[:, TILE:]
        total[table[SLOT_ROWS, slot]] += product[0:8] + product[8:16]
        return carry

    lax.fori_loop(0, SLOTS, body, 0, unroll=UNROLL)


def clamp_primal(values, free):
    floor = jnp.maximum(values, 0.0)
    return jnp.where(free > 0.5, floor, jnp.minimum(floor, 1.0))


def clamp_dual(values, ineq):
    return jnp.where(ineq > 0.5, jnp.maximum(values, 0.0), values)


def index_row(table):
    return table[AT_Y, 0] * 4 + table[AT_X, 0]


def index_col(table):
    return table[AT_Z, 0] * 2 + table[AT_CORE, 0]


def sum_four(refs, rows):
    own, opposite, right, left = (ref[rows, :] for ref in refs)
    return (own + opposite) + (right + left)


def pack(place, count, rows, cols, kinds, rhs, start, table, row_side):
    table[...] = jnp.zeros_like(table)
    table[SLOT_ROWS : SLOT_ROWS + 1, 0:SLOTS] = rows[...]
    table[SLOT_COLS : SLOT_COLS + 1, 0:SLOTS] = cols[...]
    table[COUNT : COUNT + 1, :] = jnp.full((1, TILE), count[0], jnp.int32)
    for k in range(4):
        table[AT_Y + k : AT_Y + k + 1, :] = jnp.full((1, TILE), place[k], jnp.int32)
    side = jnp.concatenate(
        [start[...], rhs[...], kinds[...].astype(F32), jnp.zeros((ROWS_SHARE, TILE), F32)], 0
    )
    row_side[...] = jnp.broadcast_to(side[None], row_side.shape)


def first_adjoint(
    table, row_side, start, cost, kinds, tiles, payload, dual, rhs, ineq, pairs, total
):
    for k in range(N):
        block = slice(k * ROWS_SHARE, (k + 1) * ROWS_SHARE)
        for j, ref in enumerate((dual, rhs, ineq)):
            ref[block, :] = row_side[k, j * ROWS_SHARE : (j + 1) * ROWS_SHARE, :]

    def tile_pair(slot):
        tile = jnp.where(slot < table[COUNT, 0], tiles[slot], 0.0)
        lead = tile.astype(BF16)
        pair = jnp.concatenate([lead, (tile - lead.astype(F32)).astype(BF16)], 0)
        pairs[slot] = pair
        return pair

    adjoint_product(table, tile_pair, dual, total)
    payload[0:COL_BLOCKS, :] = total[:, 0, :]
    payload[COL_BLOCKS:, :] = jnp.concatenate(
        [start[...], cost[...], kinds[...].astype(F32)], 0
    )


def first_forward(
    table, own, opposite, right, left, pairs, kept, given, primal, start, cost, free, extended, total
):
    y, x = table[AT_Y, 0], table[AT_X, 0]
    for j, (ref, dy) in enumerate(((own, 0), (opposite, 2), (right, 3), (left, 1))):
        for k, dx in enumerate((0, 2, 3, 1)):
            device = ((y + dy) & 3) * 4 + ((x + dx) & 3)
            block = pl.ds(pl.multiple_of(device * COLS_SHARE, COLS_SHARE), COLS_SHARE)
            for m, out in enumerate((start, cost, free)):
                first = COL_BLOCKS + (3 * k + m) * COLS_SHARE
                out[block, :] = ref[first : first + COLS_SHARE, :]
    gradient = sum_four((own, opposite, right, left), slice(0, COL_BLOCKS))
    primal[...] = clamp_primal(start[...] - 0.4 * (cost[...] - gradient), free[...])
    extended[...] = 2.0 * primal[...] - start[...]
    forward_product(table, lambda slot: pairs[slot], [extended], total)
    mine = pl.multiple_of(table[AT_CORE, 0] * HALF, HALF)
    kept[...] = total[pl.ds(mine, HALF), 0, :]
    given[...] = total[pl.ds(HALF - mine, HALF), 0, :]


def second_adjoint(
    table, half, other, start, rhs, ineq, pairs, gradient, dual, image, total
):
    mine = pl.multiple_of(table[AT_CORE, 0] * HALF, HALF)
    image[pl.ds(mine, HALF), :] = half[...]
    image[pl.ds(HALF - mine, HALF), :] = other[...]
    dual[...] = clamp_dual(start[...] + 0.4 * (rhs[...] - image[...]), ineq[...])
    adjoint_product(table, lambda slot: pairs[slot], dual, total)
    gradient[...] = total[:, 0, :]


def second_forward(
    table, own, opposite, right, left, before, cost, free, pairs, kept, given, primal, gradient, mine, extended, total
):
    gradient[...] = sum_four((own, opposite, right, left), slice(0, COL_BLOCKS))
    primal[...] = clamp_primal(before[...] - 0.4 * (cost[...] - gradient[...]), free[...])
    extended[...] = 2.0 * primal[...] - before[...]
    mine[...] = primal[
        pl.ds(pl.multiple_of(index_row(table) * COLS_SHARE, COLS_SHARE), COLS_SHARE), :
    ]
    forward_product(table, lambda slot: pairs[slot], [extended, primal], total)
    first = table[AT_CORE, 0] == 0
    image, plain = total[:, 0, :], total[:, 4, :]
    kept[...] = jnp.where(first, image, plain)
    given[...] = jnp.where(first, plain, image)


def third_adjoint(
    table, held, other, before, rhs, ineq, pairs, payload, mine, dual, total
):
    first = table[AT_CORE, 0] == 0
    image = jnp.where(first, held[...], other[...])
    plain = jnp.where(first, other[...], held[...])
    earlier, bound, kind = before[...], rhs[...], ineq[...]
    dual[...] = clamp_dual(earlier + 0.4 * (bound - image), kind)
    mine[...] = dual[pl.ds(index_col(table) * ROWS_SHARE, ROWS_SHARE), :]
    adjoint_product(table, lambda slot: pairs[slot], dual, total)
    payload[0:COL_BLOCKS, :] = total[:, 0, :]
    terms = []
    for product in (plain, 0.5 * (3.0 * plain - image)):
        residual = bound - product
        residual = jnp.where(kind > 0.5, jnp.maximum(residual, 0.0), residual)
        terms.append(jnp.sum(residual * residual, 0, keepdims=True))
    for value in (dual[...], 0.5 * (earlier + dual[...])):
        terms.append(jnp.sum(bound * value, 0, keepdims=True))
    payload[COL_BLOCKS : COL_BLOCKS + 8, :] = jnp.concatenate(terms + terms, 0)


def column_terms(
    own, opposite, right, left, earlier, before, primal, cost, free, terms, row_terms
):
    four = (own, opposite, right, left)
    adjoint = sum_four(four, slice(0, COL_BLOCKS))
    row_terms[...] = sum_four(four, slice(COL_BLOCKS, COL_BLOCKS + 8))
    price, kind = cost[...], free[...]
    rows = []
    for gradient, value in (
        (adjoint, primal[...]),
        (0.5 * (earlier[...] + adjoint), 0.5 * (before[...] + primal[...])),
    ):
        low = jnp.minimum(price - gradient, 0.0)
        violation = jnp.where(kind > 0.5, low, 0.0)
        box = jnp.where(kind > 0.5, 0.0, low)
        rows.append(jnp.sum(violation * violation, 0, keepdims=True))
        rows.append(jnp.sum(price * value, 0, keepdims=True))
        rows.append(jnp.sum(box, 0, keepdims=True))
    rows = jnp.concatenate(rows + rows[:2], 0)
    terms[...] = jnp.broadcast_to(rows[None], terms.shape)


def measures(gathered, row_terms, primal_residual, dual_residual, gap):
    columns = jnp.sum(gathered[...], 0)
    rows = row_terms[...]
    for k in range(2):
        primal_residual[k] = jnp.sum(rows[k : k + 1]) * (1.0 / NROWS)
        dual_residual[k] = jnp.sum(columns[3 * k : 3 * k + 1]) * (1.0 / NCOLS)
        total = columns[3 * k + 1 : 3 * k + 2] - columns[3 * k + 2 : 3 * k + 3] - rows[2 + k : 3 + k]
        gap[k] = jnp.sum(total) * (1.0 / NCOLS)


def shift(values, axis, step):
    return lax.ppermute(values, axis, [(k, (k + step) % 4) for k in range(4)])


def four_of(values, axis):
    return values, shift(values, axis, 2), shift(values, axis, 1), shift(values, axis, -1)


def four_over_row(values):
    own, opposite, right, left = four_of(values, "x")
    return four_of((own + opposite) + (right + left), "y")


def swap_cores(values):
    return lax.ppermute(values, "core", [(0, 1), (1, 0)])


def exchange(copies, axes):
    return lax.all_to_all(copies, axes, 0, 0)


def sum_over_z(values):
    copies = jnp.broadcast_to(values[None], (8,) + values.shape)
    return jnp.sum(exchange(copies, "z"), 0)


def shards(
    tiles, tile_rows, tile_cols, tile_count, row_types, var_types, rhs, cost, primal_start, dual_start
):
    tiles = tiles.reshape(SLOTS, TILE, TILE)
    place = jnp.stack([lax.axis_index(a) for a in ("y", "x", "z", "core")]).astype(jnp.int32)
    blocks, columns, half = (ROW_BLOCKS, TILE), (COL_BLOCKS, TILE), (HALF, TILE)
    row_total = [pltpu.VMEM((ROW_BLOCKS, 8, TILE), F32)]
    col_total = [pltpu.VMEM((COL_BLOCKS, 8, TILE), F32)]

    table, row_side = call(
        pack,
        "pack",
        [((8, TILE), jnp.int32), ((N, 4 * ROWS_SHARE, TILE), F32)],
        (
            place,
            tile_count.reshape(1),
            tile_rows.reshape(1, SLOTS),
            tile_cols.reshape(1, SLOTS),
            row_types[0],
            rhs[0],
            dual_start[0],
        ),
        smem=2,
    )
    row_side = exchange(row_side, ("z", "core"))

    payload, dual0, rhs_full, ineq, pairs = call(
        first_adjoint,
        "first_adjoint",
        [((COL_BLOCKS + 3 * COLS_SHARE, TILE), F32)]
        + [(blocks, F32)] * 3
        + [((SLOTS, 2 * TILE, TILE), BF16)],
        (table, row_side, primal_start[0], cost[0], var_types[0], tiles),
        smem=1,
        scratch=col_total,
    )
    four = four_of(payload, "x")
    gradient = (four[0] + four[1]) + (four[2] + four[3])
    payload = jnp.concatenate([gradient[:COL_BLOCKS]] + [p[COL_BLOCKS:] for p in four], 0)
    four = four_of(payload, "y")

    kept, given, primal1, start_full, cost_full, free = call(
        first_forward,
        "first_forward",
        [(half, F32)] * 2 + [(columns, F32)] * 4,
        (table, *four, pairs),
        smem=1,
        scratch=[pltpu.VMEM(columns, F32)] + row_total,
    )
    held = sum_over_z(kept + swap_cores(given))

    gradient, dual1 = call(
        second_adjoint,
        "second_adjoint",
        [(columns, F32), (blocks, F32)],
        (table, held, swap_cores(held), dual0, rhs_full, ineq, pairs),
        smem=1,
        scratch=[pltpu.VMEM(blocks, F32)] + col_total,
    )

    kept, given, primal2, gradient2, primal_mine = call(
        second_forward,
        "second_forward",
        [(blocks, F32)] * 2 + [(columns, F32)] * 2 + [((COLS_SHARE, TILE), F32)],
        (table, *four_over_row(gradient), primal1, cost_full, free, pairs),
        smem=1,
        scratch=[pltpu.VMEM(columns, F32)] + row_total,
    )
    held = sum_over_z(kept + swap_cores(given))

    payload, dual_mine = call(
        third_adjoint,
        "third_adjoint",
        [((COL_BLOCKS + 8, TILE), F32), ((ROWS_SHARE, TILE), F32)],
        (table, held, swap_cores(held), dual1, rhs_full, ineq, pairs),
        smem=1,
        scratch=[pltpu.VMEM(blocks, F32)] + col_total,
    )
    terms, row_terms = call(
        column_terms,
        "column_terms",
        [((N, 8, TILE), F32), ((8, TILE), F32)],
        (*four_over_row(payload), gradient2, primal1, primal2, cost_full, free),
    )
    primal_residual, dual_residual, gap = call(
        measures,
        "measures",
        [((2,), F32)] * 3,
        (exchange(terms, ("z", "core")), row_terms),
        smem_out=True,
    )
    return primal_mine[None], dual_mine[None], primal_residual, dual_residual, gap


def solution(mesh):
    rings = Mesh(mesh.devices.reshape(4, 4, 8, 2), ("y", "x", "z", "core"))
    row, col = ("y", "x"), ("z", "core")
    in_specs = (
        P(row, col, None, None, None),
        P(row, col, None),
        P(row, col, None),
        P(row, col),
        P(row, col, None),
        P(col, row, None),
        P(row, col, None),
        P(col, row, None),
        P(col, row, None),
        P(row, col, None),
    )
    out_specs = (P(col, row, None), P(row, col, None), P(), P(), P())
    return jax.shard_map(shards, mesh=rings, in_specs=in_specs, out_specs=out_specs, check_vma=False)
```

```python
import jax
import jax.numpy as jnp
from jax import lax
from jax.experimental import pallas as pl
from jax.experimental.pallas import tpu as pltpu
from jax.sharding import Mesh
from jax.sharding import PartitionSpec as P

N = 16
TILE = 128
ROW_BLOCKS = 64
COL_BLOCKS = 128
SLOTS = 64
ROWS_SHARE = ROW_BLOCKS // N
COLS_SHARE = COL_BLOCKS // N
HALF = ROW_BLOCKS // 2
NROWS = float(N * ROW_BLOCKS * TILE)
NCOLS = float(N * COL_BLOCKS * TILE)
UNROLL = 8
PACK_VMEM = 60 * 2**20
FIRST_VMEM = 48 * 2**20
CHUNKS = 8
CHUNK = SLOTS // CHUNKS
F32, BF16 = jnp.float32, jnp.bfloat16

SLOT_ROWS, SLOT_COLS, COUNT, AT_Y, AT_X, AT_Z, AT_CORE = range(7)

VMEM = pl.BlockSpec(memory_space=pltpu.VMEM)
SMEM = pl.BlockSpec(memory_space=pltpu.SMEM)
HBM = pl.BlockSpec(memory_space=pltpu.HBM)


def call(kernel, name, out_shapes, args, smem=0, hbm=0, smem_out=False, scratch=(), vmem=8 * 2**20):
    shapes = tuple(jax.ShapeDtypeStruct(s, d) for s, d in out_shapes)
    return pl.pallas_call(
        kernel,
        name=name,
        out_shape=shapes,
        in_specs=[SMEM] * smem + [HBM] * hbm + [VMEM] * (len(args) - smem - hbm),
        out_specs=tuple([SMEM if smem_out else VMEM] * len(shapes)),
        scratch_shapes=list(scratch),
        compiler_params=pltpu.CompilerParams(vmem_limit_bytes=vmem),
    )(*args)


def split(vector, copies):
    wide = jnp.broadcast_to(vector, (copies, TILE))
    lead = wide.astype(BF16).astype(F32)
    return [lead, wide - lead]


def adjoint_product(table, tile_pair, dual_ref, total):
    total[...] = jnp.zeros_like(total)
    adjoint_slots(table, tile_pair, dual_ref, total, 0, SLOTS)


def adjoint_slots(table, tile_pair, dual_ref, total, first, slots):
    def body(slot, carry):
        lhs = jnp.concatenate(split(dual_ref[pl.ds(table[SLOT_ROWS, slot], 1), :], 8), 0).astype(BF16)
        lhs = jnp.concatenate([lhs, lhs], 1)
        product = jnp.dot(lhs, tile_pair(slot), preferred_element_type=F32)
        total[table[SLOT_COLS, slot]] += product[0:8] + product[8:16]
        return carry

    lax.fori_loop(first, first + slots, body, 0, unroll=UNROLL)


def forward_product(table, tile_pair, primal_refs, total):
    total[...] = jnp.zeros_like(total)
    copies = 8 // len(primal_refs)

    def body(slot, carry):
        parts = [split(ref[pl.ds(table[SLOT_COLS, slot], 1), :], copies) for ref in primal_refs]
        lhs = jnp.concatenate([p[0] for p in parts] + [p[1] for p in parts], 0).astype(BF16)
        product = lax.dot_general(
            lhs, tile_pair(slot), (((1,), (1,)), ((), ())), preferred_element_type=F32
        )
        product = product[:, :TILE] + product[:, TILE:]
        total[table[SLOT_ROWS, slot]] += product[0:8] + product[8:16]
        return carry

    lax.fori_loop(0, SLOTS, body, 0, unroll=UNROLL)


def clamp_primal(values, free):
    floor = jnp.maximum(values, 0.0)
    return jnp.where(free > 0.5, floor, jnp.minimum(floor, 1.0))


def clamp_dual(values, ineq):
    return jnp.where(ineq > 0.5, jnp.maximum(values, 0.0), values)


def index_row(table):
    return table[AT_Y, 0] * 4 + table[AT_X, 0]


def index_col(table):
    return table[AT_Z, 0] * 2 + table[AT_CORE, 0]


def sum_four(refs, rows):
    own, opposite, right, left = (ref[rows, :] for ref in refs)
    return (own + opposite) + (right + left)


def pack(
    count, rows, cols, row_kinds, rhs, dual, col_kinds, cost, primal,
    table, row_side, column_side, places, side, kinds, done,
):
    copies = [
        pltpu.make_async_copy(source, target, done.at[k])
        for k, (source, target) in enumerate(
            (
                (rows.at[0], places.at[0:1]),
                (cols.at[0], places.at[1:2]),
                (dual.at[0], side.at[0]),
                (rhs.at[0], side.at[1]),
                (row_kinds.at[0], kinds.at[0:ROWS_SHARE]),
                (primal.at[0], column_side.at[0:COLS_SHARE]),
                (cost.at[0], column_side.at[COLS_SHARE : 2 * COLS_SHARE]),
                (col_kinds.at[0], kinds.at[COLS_SHARE : 2 * COLS_SHARE]),
            )
        )
    ]
    for copy in copies:
        copy.start()
    table[...] = jnp.zeros_like(table)
    table[COUNT : COUNT + 1, :] = jnp.full((1, TILE), count[0, 0], jnp.int32)
    for k, axis in ((AT_Y, "y"), (AT_X, "x"), (AT_Z, "z"), (AT_CORE, "core")):
        table[k : k + 1, :] = jnp.full((1, TILE), lax.axis_index(axis), jnp.int32)
    for copy in copies:
        copy.wait()
    table[SLOT_ROWS : SLOT_ROWS + 1, 0:SLOTS] = places[0:1, :]
    table[SLOT_COLS : SLOT_COLS + 1, 0:SLOTS] = places[1:2, :]
    packed = jnp.concatenate(
        [
            side[0],
            side[1],
            kinds[0:ROWS_SHARE, :].astype(F32),
            jnp.zeros((ROWS_SHARE, TILE), F32),
        ],
        0,
    )
    column_side[2 * COLS_SHARE :, :] = kinds[COLS_SHARE:, :].astype(F32)
    row_side[...] = jnp.broadcast_to(packed[None], row_side.shape)


def x_sums(own, opposite, right, left, payload):
    four = (own, opposite, right, left)
    payload[0:COL_BLOCKS, :] = sum_four(four, slice(0, COL_BLOCKS))
    share = 3 * COLS_SHARE
    for k, ref in enumerate(four):
        first = COL_BLOCKS + k * share
        payload[first : first + share, :] = ref[COL_BLOCKS : COL_BLOCKS + share, :]


def sums(own, opposite, right, left, total):
    total[...] = sum_four((own, opposite, right, left), slice(None))


def add_copies(kept, received, copies):
    copies[...] = jnp.broadcast_to((kept[...] + received[...])[None], copies.shape)


def sum_copies(pieces, total):
    total[...] = jnp.sum(pieces[...], 0)


def first_adjoint(
    table, tiles, row_side, column_side, payload, dual, rhs, ineq, pairs, chunks, done, total
):
    copies = []
    for k in range(CHUNKS):
        part = pl.ds(k * CHUNK, CHUNK)
        copies.append(pltpu.make_async_copy(tiles.at[part], chunks.at[part], done.at[k]))
        copies[k].start()
    for k in range(N):
        block = slice(k * ROWS_SHARE, (k + 1) * ROWS_SHARE)
        for j, ref in enumerate((dual, rhs, ineq)):
            ref[block, :] = row_side[k, j * ROWS_SHARE : (j + 1) * ROWS_SHARE, :]

    def tile_pair(slot):
        tile = jnp.where(slot < table[COUNT, 0], chunks[slot], 0.0)
        lead = tile.astype(BF16)
        pair = jnp.concatenate([lead, (tile - lead.astype(F32)).astype(BF16)], 0)
        pairs[slot] = pair
        return pair

    total[...] = jnp.zeros_like(total)
    for k in range(CHUNKS):
        copies[k].wait()
        adjoint_slots(table, tile_pair, dual, total, k * CHUNK, CHUNK)
    payload[0:COL_BLOCKS, :] = total[:, 0, :]
    payload[COL_BLOCKS:, :] = column_side[...]


def first_forward(
    table, own, opposite, right, left, pairs, kept, given, primal, start, cost, free, extended, total
):
    y, x = table[AT_Y, 0], table[AT_X, 0]
    for j, (ref, dy) in enumerate(((own, 0), (opposite, 2), (right, 3), (left, 1))):
        for k, dx in enumerate((0, 2, 3, 1)):
            device = ((y + dy) & 3) * 4 + ((x + dx) & 3)
            block = pl.ds(pl.multiple_of(device * COLS_SHARE, COLS_SHARE), COLS_SHARE)
            for m, out in enumerate((start, cost, free)):
                first = COL_BLOCKS + (3 * k + m) * COLS_SHARE
                out[block, :] = ref[first : first + COLS_SHARE, :]
    gradient = sum_four((own, opposite, right, left), slice(0, COL_BLOCKS))
    primal[...] = clamp_primal(start[...] - 0.4 * (cost[...] - gradient), free[...])
    extended[...] = 2.0 * primal[...] - start[...]
    forward_product(table, lambda slot: pairs[slot], [extended], total)
    mine = pl.multiple_of(table[AT_CORE, 0] * HALF, HALF)
    kept[...] = total[pl.ds(mine, HALF), 0, :]
    given[...] = total[pl.ds(HALF - mine, HALF), 0, :]


def second_adjoint(
    table, half, other, start, rhs, ineq, pairs, gradient, dual, image, total
):
    mine = pl.multiple_of(table[AT_CORE, 0] * HALF, HALF)
    image[pl.ds(mine, HALF), :] = half[...]
    image[pl.ds(HALF - mine, HALF), :] = other[...]
    dual[...] = clamp_dual(start[...] + 0.4 * (rhs[...] - image[...]), ineq[...])
    adjoint_product(table, lambda slot: pairs[slot], dual, total)
    gradient[...] = total[:, 0, :]


def second_forward(
    table, own, opposite, right, left, before, cost, free, pairs, kept, given, primal, gradient, mine, extended, total
):
    gradient[...] = sum_four((own, opposite, right, left), slice(0, COL_BLOCKS))
    primal[...] = clamp_primal(before[...] - 0.4 * (cost[...] - gradient[...]), free[...])
    extended[...] = 2.0 * primal[...] - before[...]
    mine[...] = primal[
        pl.ds(pl.multiple_of(index_row(table) * COLS_SHARE, COLS_SHARE), COLS_SHARE), :
    ]
    forward_product(table, lambda slot: pairs[slot], [extended, primal], total)
    first = table[AT_CORE, 0] == 0
    image, plain = total[:, 0, :], total[:, 4, :]
    kept[...] = jnp.where(first, image, plain)
    given[...] = jnp.where(first, plain, image)


def third_adjoint(
    table, held, other, before, rhs, ineq, pairs, payload, mine, dual, total
):
    first = table[AT_CORE, 0] == 0
    image = jnp.where(first, held[...], other[...])
    plain = jnp.where(first, other[...], held[...])
    earlier, bound, kind = before[...], rhs[...], ineq[...]
    dual[...] = clamp_dual(earlier + 0.4 * (bound - image), kind)
    mine[...] = dual[pl.ds(index_col(table) * ROWS_SHARE, ROWS_SHARE), :]
    adjoint_product(table, lambda slot: pairs[slot], dual, total)
    payload[0:COL_BLOCKS, :] = total[:, 0, :]
    terms = []
    for product in (plain, 0.5 * (3.0 * plain - image)):
        residual = bound - product
        residual = jnp.where(kind > 0.5, jnp.maximum(residual, 0.0), residual)
        terms.append(jnp.sum(residual * residual, 0, keepdims=True))
    for value in (dual[...], 0.5 * (earlier + dual[...])):
        terms.append(jnp.sum(bound * value, 0, keepdims=True))
    payload[COL_BLOCKS : COL_BLOCKS + 8, :] = jnp.concatenate(terms + terms, 0)


def column_terms(
    own, opposite, right, left, earlier, before, primal, cost, free, terms, row_terms
):
    four = (own, opposite, right, left)
    adjoint = sum_four(four, slice(0, COL_BLOCKS))
    row_terms[...] = sum_four(four, slice(COL_BLOCKS, COL_BLOCKS + 8))
    price, kind = cost[...], free[...]
    rows = []
    for gradient, value in (
        (adjoint, primal[...]),
        (0.5 * (earlier[...] + adjoint), 0.5 * (before[...] + primal[...])),
    ):
        low = jnp.minimum(price - gradient, 0.0)
        violation = jnp.where(kind > 0.5, low, 0.0)
        box = jnp.where(kind > 0.5, 0.0, low)
        rows.append(jnp.sum(violation * violation, 0, keepdims=True))
        rows.append(jnp.sum(price * value, 0, keepdims=True))
        rows.append(jnp.sum(box, 0, keepdims=True))
    rows = jnp.concatenate(rows + rows[:2], 0)
    terms[...] = jnp.broadcast_to(rows[None], terms.shape)


def measures(gathered, row_terms, primal_residual, dual_residual, gap):
    columns = jnp.sum(gathered[...], 0)
    rows = row_terms[...]
    for k in range(2):
        primal_residual[k] = jnp.sum(rows[k : k + 1]) * (1.0 / NROWS)
        dual_residual[k] = jnp.sum(columns[3 * k : 3 * k + 1]) * (1.0 / NCOLS)
        total = columns[3 * k + 1 : 3 * k + 2] - columns[3 * k + 2 : 3 * k + 3] - rows[2 + k : 3 + k]
        gap[k] = jnp.sum(total) * (1.0 / NCOLS)


def shift(values, axis, step):
    return lax.ppermute(values, axis, [(k, (k + step) % 4) for k in range(4)])


def four_of(values, axis):
    return values, shift(values, axis, 2), shift(values, axis, 1), shift(values, axis, -1)


def four_over_row(values):
    total = call(sums, "sums", [(values.shape, F32)], four_of(values, "x"))
    return four_of(total[0], "y")


def swap_cores(values):
    return lax.ppermute(values, "core", [(0, 1), (1, 0)])


def exchange(copies, axes):
    return lax.all_to_all(copies, axes, 0, 0)


def sum_over_col(kept, given):
    copies = call(add_copies, "add_copies", [((8,) + kept.shape, F32)], (kept, swap_cores(given)))
    total = call(sum_copies, "sum_copies", [(kept.shape, F32)], (exchange(copies[0], "z"),))
    return total[0]


def shards(
    tiles, tile_rows, tile_cols, tile_count, row_types, var_types, rhs, cost, primal_start, dual_start
):
    tiles = tiles.reshape(SLOTS, TILE, TILE)
    blocks, columns, half = (ROW_BLOCKS, TILE), (COL_BLOCKS, TILE), (HALF, TILE)
    row_total = [pltpu.VMEM((ROW_BLOCKS, 8, TILE), F32)]
    col_total = [pltpu.VMEM((COL_BLOCKS, 8, TILE), F32)]

    table, row_side, column_side = call(
        pack,
        "pack",
        [
            ((8, TILE), jnp.int32),
            ((N, 4 * ROWS_SHARE, TILE), F32),
            ((3 * COLS_SHARE, TILE), F32),
        ],
        (tile_count, tile_rows, tile_cols, row_types, rhs, dual_start, var_types, cost, primal_start),
        smem=1,
        hbm=8,
        scratch=[
            pltpu.VMEM((2, SLOTS), jnp.int32),
            pltpu.VMEM((2, ROWS_SHARE, TILE), F32),
            pltpu.VMEM((2 * COLS_SHARE, TILE), jnp.int32),
            pltpu.SemaphoreType.DMA((8,)),
        ],
        vmem=PACK_VMEM,
    )
    row_side = exchange(row_side, ("z", "core"))

    payload, dual0, rhs_full, ineq, pairs = call(
        first_adjoint,
        "first_adjoint",
        [((COL_BLOCKS + 3 * COLS_SHARE, TILE), F32)]
        + [(blocks, F32)] * 3
        + [((SLOTS, 2 * TILE, TILE), BF16)],
        (table, tiles, row_side, column_side),
        smem=1,
        hbm=1,
        scratch=[pltpu.VMEM((SLOTS, TILE, TILE), F32), pltpu.SemaphoreType.DMA((CHUNKS,))] + col_total,
        vmem=FIRST_VMEM,
    )
    four = four_of(payload, "x")
    payload = call(x_sums, "x_sums", [((COL_BLOCKS + 12 * COLS_SHARE, TILE), F32)], four)
    four = four_of(payload[0], "y")

    kept, given, primal1, start_full, cost_full, free = call(
        first_forward,
        "first_forward",
        [(half, F32)] * 2 + [(columns, F32)] * 4,
        (table, *four, pairs),
        smem=1,
        scratch=[pltpu.VMEM(columns, F32)] + row_total,
    )
    held = sum_over_col(kept, given)

    gradient, dual1 = call(
        second_adjoint,
        "second_adjoint",
        [(columns, F32), (blocks, F32)],
        (table, held, swap_cores(held), dual0, rhs_full, ineq, pairs),
        smem=1,
        scratch=[pltpu.VMEM(blocks, F32)] + col_total,
    )

    kept, given, primal2, gradient2, primal_mine = call(
        second_forward,
        "second_forward",
        [(blocks, F32)] * 2 + [(columns, F32)] * 2 + [((COLS_SHARE, TILE), F32)],
        (table, *four_over_row(gradient), primal1, cost_full, free, pairs),
        smem=1,
        scratch=[pltpu.VMEM(columns, F32)] + row_total,
    )
    held = sum_over_col(kept, given)

    payload, dual_mine = call(
        third_adjoint,
        "third_adjoint",
        [((COL_BLOCKS + 8, TILE), F32), ((ROWS_SHARE, TILE), F32)],
        (table, held, swap_cores(held), dual1, rhs_full, ineq, pairs),
        smem=1,
        scratch=[pltpu.VMEM(blocks, F32)] + col_total,
    )
    terms, row_terms = call(
        column_terms,
        "column_terms",
        [((N, 8, TILE), F32), ((8, TILE), F32)],
        (*four_over_row(payload), gradient2, primal1, primal2, cost_full, free),
    )
    primal_residual, dual_residual, gap = call(
        measures,
        "measures",
        [((2,), F32)] * 3,
        (exchange(terms, ("z", "core")), row_terms),
        smem_out=True,
    )
    return primal_mine[None], dual_mine[None], primal_residual, dual_residual, gap


def solution(mesh):
    rings = Mesh(mesh.devices.reshape(4, 4, 8, 2), ("y", "x", "z", "core"))
    row, col = ("y", "x"), ("z", "core")
    in_specs = (
        P(row, col, None, None, None),
        P(row, col, None),
        P(row, col, None),
        P(row, col),
        P(row, col, None),
        P(col, row, None),
        P(row, col, None),
        P(col, row, None),
        P(col, row, None),
        P(row, col, None),
    )
    out_specs = (P(col, row, None), P(row, col, None), P(), P(), P())
    return jax.shard_map(shards, mesh=rings, in_specs=in_specs, out_specs=out_specs, check_vma=False)
```

```python
import jax
import jax.numpy as jnp
from jax import lax
from jax.experimental import pallas as pl
from jax.experimental.pallas import tpu as pltpu
from jax.sharding import Mesh
from jax.sharding import PartitionSpec as P

N = 16
TILE = 128
ROW_BLOCKS = 64
COL_BLOCKS = 128
SLOTS = 64
ROWS_SHARE = ROW_BLOCKS // N
COLS_SHARE = COL_BLOCKS // N
HALF = ROW_BLOCKS // 2
NROWS = float(N * ROW_BLOCKS * TILE)
NCOLS = float(N * COL_BLOCKS * TILE)
PACK_VMEM = 60 * 2**20
FIRST_VMEM = 48 * 2**20
PIECES = (4, 12, 16, 32)
F32, BF16 = jnp.float32, jnp.bfloat16

SLOT_ROWS, SLOT_COLS, COUNT, AT_Y, AT_X, AT_Z, AT_CORE = range(7)
COL_SIDE, ROW_SIDE, TABLE, SIDE = 0, 24, 32, 40

VMEM = pl.BlockSpec(memory_space=pltpu.VMEM)
SMEM = pl.BlockSpec(memory_space=pltpu.SMEM)
HBM = pl.BlockSpec(memory_space=pltpu.HBM)


def call(kernel, name, out_shapes, args, smem=0, hbm=0, smem_out=False, scratch=(), vmem=8 * 2**20):
    shapes = tuple(jax.ShapeDtypeStruct(s, d) for s, d in out_shapes)
    return pl.pallas_call(
        kernel,
        name=name,
        out_shape=shapes,
        in_specs=[SMEM] * smem + [HBM] * hbm + [VMEM] * (len(args) - smem - hbm),
        out_specs=tuple([SMEM if smem_out else VMEM] * len(shapes)),
        scratch_shapes=list(scratch),
        compiler_params=pltpu.CompilerParams(vmem_limit_bytes=vmem),
    )(*args)


def split(vector, copies):
    wide = jnp.broadcast_to(vector, (copies, TILE))
    lead = wide.astype(BF16).astype(F32)
    return [lead, wide - lead]


def adjoint_product(table, tile_pair, dual_ref, total):
    total[...] = jnp.zeros_like(total)
    adjoint_slots(table, tile_pair, dual_ref, total, 0, SLOTS)


def adjoint_slots(table, tile_pair, dual_ref, total, first, slots):
    def body(slot, carry):
        lhs = jnp.concatenate(split(dual_ref[pl.ds(table[SLOT_ROWS, slot], 1), :], 8), 0).astype(BF16)
        lhs = jnp.concatenate([lhs, lhs], 1)
        product = jnp.dot(lhs, tile_pair(slot), preferred_element_type=F32)
        total[table[SLOT_COLS, slot]] += product[0:8] + product[8:16]
        return carry

    lax.fori_loop(first, first + slots, body, 0, unroll=slots)


def forward_product(table, tile_pair, primal_refs, total):
    total[...] = jnp.zeros_like(total)
    copies = 8 // len(primal_refs)

    def body(slot, carry):
        parts = [split(ref[pl.ds(table[SLOT_COLS, slot], 1), :], copies) for ref in primal_refs]
        lhs = jnp.concatenate([p[0] for p in parts] + [p[1] for p in parts], 0).astype(BF16)
        product = lax.dot_general(
            lhs, tile_pair(slot), (((1,), (1,)), ((), ())), preferred_element_type=F32
        )
        product = product[:, :TILE] + product[:, TILE:]
        total[table[SLOT_ROWS, slot]] += product[0:8] + product[8:16]
        return carry

    lax.fori_loop(0, SLOTS, body, 0, unroll=SLOTS)


def clamp_primal(values, free):
    floor = jnp.maximum(values, 0.0)
    return jnp.where(free > 0.5, floor, jnp.minimum(floor, 1.0))


def clamp_dual(values, ineq):
    return jnp.where(ineq > 0.5, jnp.maximum(values, 0.0), values)


def index_row(table):
    return table[AT_Y, 0] * 4 + table[AT_X, 0]


def index_col(table):
    return table[AT_Z, 0] * 2 + table[AT_CORE, 0]


def sum_four(refs, rows):
    own, opposite, right, left = (ref[rows, :] for ref in refs)
    return (own + opposite) + (right + left)


def pack(
    count, rows, cols, row_kinds, rhs, dual, col_kinds, cost, primal, duals, side, places, kinds, start, done
):
    copies = [
        pltpu.make_async_copy(source, target, done.at[k])
        for k, (source, target) in enumerate(
            (
                (rows.at[0], places.at[0:1]),
                (cols.at[0], places.at[1:2]),
                (dual.at[0], start),
                (rhs.at[0], side.at[ROW_SIDE : ROW_SIDE + ROWS_SHARE]),
                (row_kinds.at[0], kinds.at[0:ROWS_SHARE]),
                (primal.at[0], side.at[0:COLS_SHARE]),
                (cost.at[0], side.at[COLS_SHARE : 2 * COLS_SHARE]),
                (col_kinds.at[0], kinds.at[COLS_SHARE : 2 * COLS_SHARE]),
            )
        )
    ]
    for copy in copies:
        copy.start()
    side[TABLE + COUNT :, :] = jnp.zeros((SIDE - TABLE - COUNT, TILE), F32)
    for k, value in (
        (COUNT, count[0, 0]),
        (AT_Y, lax.axis_index("y")),
        (AT_X, lax.axis_index("x")),
        (AT_Z, lax.axis_index("z")),
        (AT_CORE, lax.axis_index("core")),
    ):
        side[TABLE + k : TABLE + k + 1, :] = jnp.full((1, TILE), value, jnp.int32).astype(F32)
    side[TABLE : TABLE + COUNT, :] = jnp.zeros((COUNT, TILE), F32)
    for copy in copies:
        copy.wait()
    side[TABLE : TABLE + COUNT, 0:SLOTS] = places[...].astype(F32)
    side[2 * COLS_SHARE : ROW_SIDE, :] = kinds[COLS_SHARE:, :].astype(F32)
    side[ROW_SIDE + ROWS_SHARE : TABLE, :] = kinds[0:ROWS_SHARE, :].astype(F32)
    duals[...] = jnp.broadcast_to(start[...][None], duals.shape)


def x_sums(own, opposite, right, left, payload):
    four = (own, opposite, right, left)
    payload[0:COL_BLOCKS, :] = sum_four(four, slice(0, COL_BLOCKS))
    share = 3 * COLS_SHARE
    for k, ref in enumerate(four):
        first = COL_BLOCKS + k * share
        payload[first : first + share, :] = ref[COL_BLOCKS : COL_BLOCKS + share, :]


def sums(own, opposite, right, left, total):
    total[...] = sum_four((own, opposite, right, left), slice(None))


def image_copies(kept, received, side, copies):
    block = jnp.concatenate([kept[...] + received[...], side[ROW_SIDE:TABLE, :]], 0)
    copies[...] = jnp.broadcast_to(block[None], copies.shape)


def image_sums(pieces, held):
    held[0:HALF, :] = jnp.sum(pieces[:, 0:HALF, :], 0)
    for k in range(8):
        for j in range(2):
            first = HALF + j * ROWS_SHARE
            into = HALF * (1 + j) + k * ROWS_SHARE
            held[into : into + ROWS_SHARE, :] = pieces[k, first : first + ROWS_SHARE, :]


def pair_copies(kept, received, copies):
    both = kept[...] + received[...]
    for k in range(8):
        first = HALF + k * ROWS_SHARE
        copies[k, 0:HALF, :] = both[0:HALF]
        copies[k, HALF : HALF + 8, :] = jnp.concatenate(
            [both[first : first + ROWS_SHARE], jnp.zeros((8 - ROWS_SHARE, TILE), F32)], 0
        )


def pair_sums(pieces, held):
    held[...] = jnp.sum(pieces[...], 0)


def first_adjoint(
    tiles, duals, side, payload, dual, table_out, pairs, chunks, table, done, total
):
    copies, first = [], 0
    for k, slots in enumerate(PIECES):
        part = pl.ds(first, slots)
        copies.append(pltpu.make_async_copy(tiles.at[part], chunks.at[part], done.at[k]))
        copies[k].start()
        first += slots
    table_out[...] = side[TABLE:, :].astype(jnp.int32)
    read = pltpu.make_async_copy(table_out, table, done.at[len(PIECES)])
    read.start()
    for k in range(N):
        dual[k * ROWS_SHARE : (k + 1) * ROWS_SHARE, :] = duals[k]
    total[...] = jnp.zeros_like(total)
    payload[COL_BLOCKS:, :] = side[COL_SIDE:ROW_SIDE, :]
    read.wait()

    def tile_pair(slot):
        tile = jnp.where(slot < table[COUNT, 0], chunks[slot], 0.0)
        lead = tile.astype(BF16)
        pair = jnp.concatenate([lead, (tile - lead.astype(F32)).astype(BF16)], 0)
        pairs[slot] = pair
        return pair

    first = 0
    for k, slots in enumerate(PIECES):
        copies[k].wait()
        adjoint_slots(table, tile_pair, dual, total, first, slots)
        first += slots
    payload[0:COL_BLOCKS, :] = total[:, 0, :]


def first_forward(
    table, own, opposite, right, left, pairs, kept, given, primal, start, cost, free, extended, total
):
    y, x = table[AT_Y, 0], table[AT_X, 0]
    for j, (ref, dy) in enumerate(((own, 0), (opposite, 2), (right, 3), (left, 1))):
        for k, dx in enumerate((0, 2, 3, 1)):
            device = ((y + dy) & 3) * 4 + ((x + dx) & 3)
            block = pl.ds(pl.multiple_of(device * COLS_SHARE, COLS_SHARE), COLS_SHARE)
            for m, out in enumerate((start, cost, free)):
                first = COL_BLOCKS + (3 * k + m) * COLS_SHARE
                out[block, :] = ref[first : first + COLS_SHARE, :]
    gradient = sum_four((own, opposite, right, left), slice(0, COL_BLOCKS))
    primal[...] = clamp_primal(start[...] - 0.4 * (cost[...] - gradient), free[...])
    extended[...] = 2.0 * primal[...] - start[...]
    forward_product(table, lambda slot: pairs[slot], [extended], total)
    mine = pl.multiple_of(table[AT_CORE, 0] * HALF, HALF)
    kept[...] = total[pl.ds(mine, HALF), 0, :]
    given[...] = total[pl.ds(HALF - mine, HALF), 0, :]


def second_adjoint(table, held, other, start, pairs, gradient, dual, rhs, ineq, image, total):
    first = table[AT_CORE, 0] == 0
    mine, theirs = held[...], other[...]
    for core, half in enumerate((jnp.where(first, mine, theirs), jnp.where(first, theirs, mine))):
        image[core * HALF : (core + 1) * HALF, :] = half[0:HALF]
        for k in range(8):
            block = slice((2 * k + core) * ROWS_SHARE, (2 * k + core + 1) * ROWS_SHARE)
            share = slice(k * ROWS_SHARE, (k + 1) * ROWS_SHARE)
            rhs[block, :] = half[HALF : 2 * HALF][share]
            ineq[block, :] = half[2 * HALF :][share]
    dual[...] = clamp_dual(start[...] + 0.4 * (rhs[...] - image[...]), ineq[...])
    adjoint_product(table, lambda slot: pairs[slot], dual, total)
    gradient[...] = total[:, 0, :]


def second_forward(
    table, own, opposite, right, left, before, cost, free, pairs, kept, given, primal, gradient, primal_mine, extended, total
):
    gradient[...] = sum_four((own, opposite, right, left), slice(0, COL_BLOCKS))
    primal[...] = clamp_primal(before[...] - 0.4 * (cost[...] - gradient[...]), free[...])
    extended[...] = 2.0 * primal[...] - before[...]
    primal_mine[...] = primal[
        pl.ds(pl.multiple_of(index_row(table) * COLS_SHARE, COLS_SHARE), COLS_SHARE), :
    ]
    forward_product(table, lambda slot: pairs[slot], [extended, primal], total)
    mine = pl.multiple_of(table[AT_CORE, 0] * HALF, HALF)
    for k, part in enumerate((0, 4)):
        rows = slice(k * HALF, (k + 1) * HALF)
        kept[rows, :] = total[pl.ds(mine, HALF), part, :]
        given[rows, :] = total[pl.ds(HALF - mine, HALF), part, :]


def third_adjoint(
    table, held, other, before, rhs, ineq, pairs, payload, mine, dual, image, total
):
    half = pl.multiple_of(table[AT_CORE, 0] * HALF, HALF)
    image[pl.ds(half, HALF), :] = held[0:HALF, :]
    image[pl.ds(HALF - half, HALF), :] = other[0:HALF, :]
    dual[...] = clamp_dual(before[...] + 0.4 * (rhs[...] - image[...]), ineq[...])
    mine[...] = dual[pl.ds(index_col(table) * ROWS_SHARE, ROWS_SHARE), :]
    adjoint_product(table, lambda slot: pairs[slot], dual, total)
    payload[0:COL_BLOCKS, :] = total[:, 0, :]
    share = pl.ds(half + table[AT_Z, 0] * ROWS_SHARE, ROWS_SHARE)
    plain = held[HALF : HALF + ROWS_SHARE, :]
    bound, kind, last = rhs[share, :], ineq[share, :], dual[share, :]
    terms = []
    for product in (plain, 0.5 * (3.0 * plain - image[share, :])):
        residual = bound - product
        residual = jnp.where(kind > 0.5, jnp.maximum(residual, 0.0), residual)
        terms.append(jnp.sum(residual * residual, 0, keepdims=True))
    for value in (last, 0.5 * (before[share, :] + last)):
        terms.append(jnp.sum(bound * value, 0, keepdims=True))
    payload[COL_BLOCKS : COL_BLOCKS + 8, :] = jnp.concatenate(terms + terms, 0)


def column_terms(own, opposite, right, left, earlier, before, primal, cost, free, terms):
    four = (own, opposite, right, left)
    adjoint = sum_four(four, slice(0, COL_BLOCKS))
    row_terms = sum_four(four, slice(COL_BLOCKS, COL_BLOCKS + 8))
    price, kind = cost[...], free[...]
    squares, gaps = [], []
    for k, (gradient, value) in enumerate(
        (
            (adjoint, primal[...]),
            (0.5 * (earlier[...] + adjoint), 0.5 * (before[...] + primal[...])),
        )
    ):
        low = jnp.minimum(price - gradient, 0.0)
        violation = jnp.where(kind > 0.5, low, 0.0)
        box = jnp.where(kind > 0.5, 0.0, low)
        squares.append(jnp.sum(violation * violation, 0, keepdims=True))
        column = jnp.sum(price * value, 0, keepdims=True) - jnp.sum(box, 0, keepdims=True)
        gaps.append(column - row_terms[2 + k : 3 + k])
    rows = jnp.concatenate([row_terms[0:2]] + squares + gaps + squares, 0)
    sums = jnp.broadcast_to(jnp.sum(rows, 1, keepdims=True), rows.shape)
    places = [lax.broadcasted_iota(jnp.int32, rows.shape, k) for k in range(2)]
    line = jnp.sum(jnp.where(places[0] == places[1], sums, 0.0), 0, keepdims=True)
    terms[...] = jnp.broadcast_to(line[None], terms.shape)


def measures(gathered, primal_residual, dual_residual, gap):
    line = jnp.sum(gathered[...], 0)
    lane = lax.broadcasted_iota(jnp.int32, line.shape, 1)
    for k, (out, size) in enumerate(
        ((primal_residual, NROWS), (dual_residual, NCOLS), (gap, NCOLS))
    ):
        for j in range(2):
            out[j] = jnp.sum(jnp.where(lane == 2 * k + j, line, 0.0)) * (1.0 / size)


def shift(values, axis, step):
    return lax.ppermute(values, axis, [(k, (k + step) % 4) for k in range(4)])


def four_of(values, axis):
    return values, shift(values, axis, 2), shift(values, axis, 1), shift(values, axis, -1)


def four_over_row(values):
    total = call(sums, "sums", [(values.shape, F32)], four_of(values, "x"))
    return four_of(total[0], "y")


def swap_cores(values):
    return lax.ppermute(values, "core", [(0, 1), (1, 0)])


def exchange(copies, axes):
    return lax.all_to_all(copies, axes, 0, 0)


def shards(
    tiles, tile_rows, tile_cols, tile_count, row_types, var_types, rhs, cost, primal_start, dual_start
):
    tiles = tiles.reshape(SLOTS, TILE, TILE)
    blocks, columns, half = (ROW_BLOCKS, TILE), (COL_BLOCKS, TILE), (HALF, TILE)
    row_total = [pltpu.VMEM((ROW_BLOCKS, 8, TILE), F32)]
    col_total = [pltpu.VMEM((COL_BLOCKS, 8, TILE), F32)]

    duals, side = call(
        pack,
        "pack",
        [((N, ROWS_SHARE, TILE), F32), ((SIDE, TILE), F32)],
        (tile_count, tile_rows, tile_cols, row_types, rhs, dual_start, var_types, cost, primal_start),
        smem=1,
        hbm=8,
        scratch=[
            pltpu.VMEM((2, SLOTS), jnp.int32),
            pltpu.VMEM((2 * COLS_SHARE, TILE), jnp.int32),
            pltpu.VMEM((ROWS_SHARE, TILE), F32),
            pltpu.SemaphoreType.DMA((8,)),
        ],
        vmem=PACK_VMEM,
    )

    payload, dual0, table, pairs = call(
        first_adjoint,
        "first_adjoint",
        [
            ((COL_BLOCKS + 3 * COLS_SHARE, TILE), F32),
            (blocks, F32),
            ((8, TILE), jnp.int32),
            ((SLOTS, 2 * TILE, TILE), BF16),
        ],
        (tiles, exchange(duals, ("z", "core")), side),
        hbm=1,
        scratch=[
            pltpu.VMEM((SLOTS, TILE, TILE), F32),
            pltpu.SMEM((8, TILE), jnp.int32),
            pltpu.SemaphoreType.DMA((len(PIECES) + 1,)),
        ]
        + col_total,
        vmem=FIRST_VMEM,
    )
    payload = call(
        x_sums, "x_sums", [((COL_BLOCKS + 12 * COLS_SHARE, TILE), F32)], four_of(payload, "x")
    )

    kept, given, primal1, start_full, cost_full, free = call(
        first_forward,
        "first_forward",
        [(half, F32)] * 2 + [(columns, F32)] * 4,
        (table, *four_of(payload[0], "y"), pairs),
        smem=1,
        scratch=[pltpu.VMEM(columns, F32)] + row_total,
    )
    copies = call(
        image_copies,
        "image_copies",
        [((8, HALF + 2 * ROWS_SHARE, TILE), F32)],
        (kept, swap_cores(given), side),
    )
    held = call(
        image_sums, "image_sums", [((3 * HALF, TILE), F32)], (exchange(copies[0], "z"),)
    )[0]

    gradient, dual1, rhs_full, ineq = call(
        second_adjoint,
        "second_adjoint",
        [(columns, F32)] + [(blocks, F32)] * 3,
        (table, held, swap_cores(held), dual0, pairs),
        smem=1,
        scratch=[pltpu.VMEM(blocks, F32)] + col_total,
    )

    kept, given, primal2, gradient2, primal_mine = call(
        second_forward,
        "second_forward",
        [(blocks, F32)] * 2 + [(columns, F32)] * 2 + [((COLS_SHARE, TILE), F32)],
        (table, *four_over_row(gradient), primal1, cost_full, free, pairs),
        smem=1,
        scratch=[pltpu.VMEM(columns, F32)] + row_total,
    )
    copies = call(
        pair_copies, "pair_copies", [((8, HALF + 8, TILE), F32)], (kept, swap_cores(given))
    )
    held = call(pair_sums, "pair_sums", [((HALF + 8, TILE), F32)], (exchange(copies[0], "z"),))[0]

    payload, dual_mine = call(
        third_adjoint,
        "third_adjoint",
        [((COL_BLOCKS + 8, TILE), F32), ((ROWS_SHARE, TILE), F32)],
        (table, held, swap_cores(held), dual1, rhs_full, ineq, pairs),
        smem=1,
        scratch=[pltpu.VMEM(blocks, F32)] * 2 + col_total,
    )
    terms = call(
        column_terms,
        "column_terms",
        [((N, 1, TILE), F32)],
        (*four_over_row(payload), gradient2, primal1, primal2, cost_full, free),
    )
    primal_residual, dual_residual, gap = call(
        measures,
        "measures",
        [((2,), F32)] * 3,
        (exchange(terms[0], ("z", "core")),),
        smem_out=True,
    )
    return primal_mine[None], dual_mine[None], primal_residual, dual_residual, gap


def solution(mesh):
    rings = Mesh(mesh.devices.reshape(4, 4, 8, 2), ("y", "x", "z", "core"))
    row, col = ("y", "x"), ("z", "core")
    in_specs = (
        P(row, col, None, None, None),
        P(row, col, None),
        P(row, col, None),
        P(row, col),
        P(row, col, None),
        P(col, row, None),
        P(row, col, None),
        P(col, row, None),
        P(col, row, None),
        P(row, col, None),
    )
    out_specs = (P(col, row, None), P(row, col, None), P(), P(), P())
    return jax.shard_map(shards, mesh=rings, in_specs=in_specs, out_specs=out_specs, check_vma=False)
```

```python
import jax
import jax.numpy as jnp
from jax import lax
from jax.experimental import pallas as pl
from jax.experimental.pallas import tpu as pltpu
from jax.sharding import Mesh
from jax.sharding import PartitionSpec as P

N = 16
TILE = 128
ROW_BLOCKS = 64
COL_BLOCKS = 128
SLOTS = 64
ROWS_SHARE = ROW_BLOCKS // N
COLS_SHARE = COL_BLOCKS // N
HALF = ROW_BLOCKS // 2
NROWS = float(N * ROW_BLOCKS * TILE)
NCOLS = float(N * COL_BLOCKS * TILE)
PACK_VMEM = 60 * 2**20
FIRST_VMEM = 48 * 2**20
PIECES = (4, 12, 16, 32)
F32, BF16 = jnp.float32, jnp.bfloat16

SLOT_ROWS, SLOT_COLS, COUNT, AT_Y, AT_X, AT_Z, AT_CORE = range(7)
COL_SIDE, ROW_SIDE, TABLE, SIDE = 0, 24, 32, 40

VMEM = pl.BlockSpec(memory_space=pltpu.VMEM)
SMEM = pl.BlockSpec(memory_space=pltpu.SMEM)
HBM = pl.BlockSpec(memory_space=pltpu.HBM)


def call(kernel, name, out_shapes, args, smem=0, hbm=0, smem_out=False, scratch=(), vmem=8 * 2**20):
    shapes = tuple(jax.ShapeDtypeStruct(s, d) for s, d in out_shapes)
    return pl.pallas_call(
        kernel,
        name=name,
        out_shape=shapes,
        in_specs=[SMEM] * smem + [HBM] * hbm + [VMEM] * (len(args) - smem - hbm),
        out_specs=tuple([SMEM if smem_out else VMEM] * len(shapes)),
        scratch_shapes=list(scratch),
        compiler_params=pltpu.CompilerParams(vmem_limit_bytes=vmem),
    )(*args)


def split(vector, copies):
    wide = jnp.broadcast_to(vector, (copies, TILE))
    lead = wide.astype(BF16).astype(F32)
    return [lead, wide - lead]


def adjoint_product(table, tile_pair, dual_ref, total):
    total[...] = jnp.zeros_like(total)
    adjoint_slots(table, tile_pair, dual_ref, total, 0, SLOTS)


def adjoint_slots(table, tile_pair, dual_ref, total, first, slots):
    def body(slot, carry):
        lhs = jnp.concatenate(split(dual_ref[pl.ds(table[SLOT_ROWS, slot], 1), :], 8), 0).astype(BF16)
        lhs = jnp.concatenate([lhs, lhs], 1)
        product = jnp.dot(lhs, tile_pair(slot), preferred_element_type=F32)
        total[table[SLOT_COLS, slot]] += product[0:8] + product[8:16]
        return carry

    lax.fori_loop(first, first + slots, body, 0, unroll=slots)


def forward_product(table, tile_pair, primal_refs, total):
    total[...] = jnp.zeros_like(total)
    copies = 8 // len(primal_refs)

    def body(slot, carry):
        parts = [split(ref[pl.ds(table[SLOT_COLS, slot], 1), :], copies) for ref in primal_refs]
        lhs = jnp.concatenate([p[0] for p in parts] + [p[1] for p in parts], 0).astype(BF16)
        product = lax.dot_general(
            lhs, tile_pair(slot), (((1,), (1,)), ((), ())), preferred_element_type=F32
        )
        product = product[:, :TILE] + product[:, TILE:]
        total[table[SLOT_ROWS, slot]] += product[0:8] + product[8:16]
        return carry

    lax.fori_loop(0, SLOTS, body, 0, unroll=SLOTS)


def clamp_primal(values, free):
    floor = jnp.maximum(values, 0.0)
    return jnp.where(free > 0.5, floor, jnp.minimum(floor, 1.0))


def clamp_dual(values, ineq):
    return jnp.where(ineq > 0.5, jnp.maximum(values, 0.0), values)


def index_row(table):
    return table[AT_Y, 0] * 4 + table[AT_X, 0]


def index_col(table):
    return table[AT_Z, 0] * 2 + table[AT_CORE, 0]


def sum_four(refs, rows):
    own, right, left, opposite = (ref[rows, :] for ref in refs)
    return (own + opposite) + (right + left)


def pack(
    count, rows, cols, row_kinds, rhs, dual, col_kinds, cost, primal, duals, side, places, kinds, start, done
):
    copies = [
        pltpu.make_async_copy(source, target, done.at[k])
        for k, (source, target) in enumerate(
            (
                (rows.at[0], places.at[0:1]),
                (cols.at[0], places.at[1:2]),
                (dual.at[0], start),
                (rhs.at[0], side.at[ROW_SIDE : ROW_SIDE + ROWS_SHARE]),
                (row_kinds.at[0], kinds.at[0:ROWS_SHARE]),
                (primal.at[0], side.at[0:COLS_SHARE]),
                (cost.at[0], side.at[COLS_SHARE : 2 * COLS_SHARE]),
                (col_kinds.at[0], kinds.at[COLS_SHARE : 2 * COLS_SHARE]),
            )
        )
    ]
    for copy in copies:
        copy.start()
    side[TABLE + COUNT :, :] = jnp.zeros((SIDE - TABLE - COUNT, TILE), F32)
    for k, value in (
        (COUNT, count[0, 0]),
        (AT_Y, lax.axis_index("y")),
        (AT_X, lax.axis_index("x")),
        (AT_Z, lax.axis_index("z")),
        (AT_CORE, lax.axis_index("core")),
    ):
        side[TABLE + k : TABLE + k + 1, :] = jnp.full((1, TILE), value, jnp.int32).astype(F32)
    side[TABLE : TABLE + COUNT, :] = jnp.zeros((COUNT, TILE), F32)
    for copy in copies:
        copy.wait()
    side[TABLE : TABLE + COUNT, 0:SLOTS] = places[...].astype(F32)
    side[2 * COLS_SHARE : ROW_SIDE, :] = kinds[COLS_SHARE:, :].astype(F32)
    side[ROW_SIDE + ROWS_SHARE : TABLE, :] = kinds[0:ROWS_SHARE, :].astype(F32)
    duals[...] = jnp.broadcast_to(start[...][None], duals.shape)


def x_sums(own, right, left, opposite, payload):
    four = (own, right, left, opposite)
    payload[0:COL_BLOCKS, :] = sum_four(four, slice(0, COL_BLOCKS))
    share = 3 * COLS_SHARE
    for k, ref in enumerate(four):
        first = COL_BLOCKS + k * share
        payload[first : first + share, :] = ref[COL_BLOCKS : COL_BLOCKS + share, :]


def sums(own, right, left, opposite, total):
    total[...] = sum_four((own, right, left, opposite), slice(None))


def image_copies(kept, received, side, copies):
    block = jnp.concatenate([kept[...] + received[...], side[ROW_SIDE:TABLE, :]], 0)
    copies[...] = jnp.broadcast_to(block[None], copies.shape)


def image_sums(pieces, held):
    held[0:HALF, :] = jnp.sum(pieces[:, 0:HALF, :], 0)
    for k in range(8):
        for j in range(2):
            first = HALF + j * ROWS_SHARE
            into = HALF * (1 + j) + k * ROWS_SHARE
            held[into : into + ROWS_SHARE, :] = pieces[k, first : first + ROWS_SHARE, :]


def pair_copies(kept, received, copies):
    both = kept[...] + received[...]
    for k in range(8):
        first = HALF + k * ROWS_SHARE
        copies[k, 0:HALF, :] = both[0:HALF]
        copies[k, HALF : HALF + 8, :] = jnp.concatenate(
            [both[first : first + ROWS_SHARE], jnp.zeros((8 - ROWS_SHARE, TILE), F32)], 0
        )


def pair_sums(pieces, held):
    held[...] = jnp.sum(pieces[...], 0)


def first_adjoint(
    tiles, duals, side, payload, dual, table_out, pairs, chunks, table, done, total
):
    copies, first = [], 0
    for k, slots in enumerate(PIECES):
        part = pl.ds(first, slots)
        copies.append(pltpu.make_async_copy(tiles.at[part], chunks.at[part], done.at[k]))
        copies[k].start()
        first += slots
    table_out[...] = side[TABLE:, :].astype(jnp.int32)
    read = pltpu.make_async_copy(table_out, table, done.at[len(PIECES)])
    read.start()
    for k in range(N):
        dual[k * ROWS_SHARE : (k + 1) * ROWS_SHARE, :] = duals[k]
    total[...] = jnp.zeros_like(total)
    payload[COL_BLOCKS:, :] = side[COL_SIDE:ROW_SIDE, :]
    read.wait()

    def tile_pair(slot):
        tile = jnp.where(slot < table[COUNT, 0], chunks[slot], 0.0)
        lead = tile.astype(BF16)
        pair = jnp.concatenate([lead, (tile - lead.astype(F32)).astype(BF16)], 0)
        pairs[slot] = pair
        return pair

    first = 0
    for k, slots in enumerate(PIECES):
        copies[k].wait()
        adjoint_slots(table, tile_pair, dual, total, first, slots)
        first += slots
    payload[0:COL_BLOCKS, :] = total[:, 0, :]


def first_forward(
    table, own, right, left, opposite, pairs, kept, given, primal, start, cost, free, extended, total
):
    y, x = table[AT_Y, 0], table[AT_X, 0]
    for j, (ref, dy) in enumerate(((own, 0), (right, 3), (left, 1), (opposite, 2))):
        for k, dx in enumerate((0, 3, 1, 2)):
            device = ((y + dy) & 3) * 4 + ((x + dx) & 3)
            block = pl.ds(pl.multiple_of(device * COLS_SHARE, COLS_SHARE), COLS_SHARE)
            for m, out in enumerate((start, cost, free)):
                first = COL_BLOCKS + (3 * k + m) * COLS_SHARE
                out[block, :] = ref[first : first + COLS_SHARE, :]
    gradient = sum_four((own, right, left, opposite), slice(0, COL_BLOCKS))
    primal[...] = clamp_primal(start[...] - 0.4 * (cost[...] - gradient), free[...])
    extended[...] = 2.0 * primal[...] - start[...]
    forward_product(table, lambda slot: pairs[slot], [extended], total)
    mine = pl.multiple_of(table[AT_CORE, 0] * HALF, HALF)
    kept[...] = total[pl.ds(mine, HALF), 0, :]
    given[...] = total[pl.ds(HALF - mine, HALF), 0, :]


def second_adjoint(table, held, other, start, pairs, gradient, dual, rhs, ineq, image, total):
    first = table[AT_CORE, 0] == 0
    mine, theirs = held[...], other[...]
    for core, half in enumerate((jnp.where(first, mine, theirs), jnp.where(first, theirs, mine))):
        image[core * HALF : (core + 1) * HALF, :] = half[0:HALF]
        for k in range(8):
            block = slice((2 * k + core) * ROWS_SHARE, (2 * k + core + 1) * ROWS_SHARE)
            share = slice(k * ROWS_SHARE, (k + 1) * ROWS_SHARE)
            rhs[block, :] = half[HALF : 2 * HALF][share]
            ineq[block, :] = half[2 * HALF :][share]
    dual[...] = clamp_dual(start[...] + 0.4 * (rhs[...] - image[...]), ineq[...])
    adjoint_product(table, lambda slot: pairs[slot], dual, total)
    gradient[...] = total[:, 0, :]


def second_forward(
    table, own, right, left, opposite, before, cost, free, pairs, kept, given, primal, gradient, primal_mine, extended, total
):
    gradient[...] = sum_four((own, right, left, opposite), slice(0, COL_BLOCKS))
    primal[...] = clamp_primal(before[...] - 0.4 * (cost[...] - gradient[...]), free[...])
    extended[...] = 2.0 * primal[...] - before[...]
    primal_mine[...] = primal[
        pl.ds(pl.multiple_of(index_row(table) * COLS_SHARE, COLS_SHARE), COLS_SHARE), :
    ]
    forward_product(table, lambda slot: pairs[slot], [extended, primal], total)
    mine = pl.multiple_of(table[AT_CORE, 0] * HALF, HALF)
    for k, part in enumerate((0, 4)):
        rows = slice(k * HALF, (k + 1) * HALF)
        kept[rows, :] = total[pl.ds(mine, HALF), part, :]
        given[rows, :] = total[pl.ds(HALF - mine, HALF), part, :]


def third_adjoint(
    table, held, other, before, rhs, ineq, pairs, payload, mine, dual, image, total
):
    half = pl.multiple_of(table[AT_CORE, 0] * HALF, HALF)
    image[pl.ds(half, HALF), :] = held[0:HALF, :]
    image[pl.ds(HALF - half, HALF), :] = other[0:HALF, :]
    dual[...] = clamp_dual(before[...] + 0.4 * (rhs[...] - image[...]), ineq[...])
    mine[...] = dual[pl.ds(index_col(table) * ROWS_SHARE, ROWS_SHARE), :]
    adjoint_product(table, lambda slot: pairs[slot], dual, total)
    payload[0:COL_BLOCKS, :] = total[:, 0, :]
    share = pl.ds(half + table[AT_Z, 0] * ROWS_SHARE, ROWS_SHARE)
    plain = held[HALF : HALF + ROWS_SHARE, :]
    bound, kind, last = rhs[share, :], ineq[share, :], dual[share, :]
    terms = []
    for product in (plain, 0.5 * (3.0 * plain - image[share, :])):
        residual = bound - product
        residual = jnp.where(kind > 0.5, jnp.maximum(residual, 0.0), residual)
        terms.append(jnp.sum(residual * residual, 0, keepdims=True))
    for value in (last, 0.5 * (before[share, :] + last)):
        terms.append(jnp.sum(bound * value, 0, keepdims=True))
    payload[COL_BLOCKS : COL_BLOCKS + 8, :] = jnp.concatenate(terms + terms, 0)


def column_terms(own, right, left, opposite, earlier, before, primal, cost, free, terms):
    four = (own, right, left, opposite)
    adjoint = sum_four(four, slice(0, COL_BLOCKS))
    row_terms = sum_four(four, slice(COL_BLOCKS, COL_BLOCKS + 8))
    price, kind = cost[...], free[...]
    squares, gaps = [], []
    for k, (gradient, value) in enumerate(
        (
            (adjoint, primal[...]),
            (0.5 * (earlier[...] + adjoint), 0.5 * (before[...] + primal[...])),
        )
    ):
        low = jnp.minimum(price - gradient, 0.0)
        violation = jnp.where(kind > 0.5, low, 0.0)
        box = jnp.where(kind > 0.5, 0.0, low)
        squares.append(jnp.sum(violation * violation, 0, keepdims=True))
        column = jnp.sum(price * value, 0, keepdims=True) - jnp.sum(box, 0, keepdims=True)
        gaps.append(column - row_terms[2 + k : 3 + k])
    rows = jnp.concatenate([row_terms[0:2]] + squares + gaps + squares, 0)
    sums = jnp.broadcast_to(jnp.sum(rows, 1, keepdims=True), rows.shape)
    places = [lax.broadcasted_iota(jnp.int32, rows.shape, k) for k in range(2)]
    line = jnp.sum(jnp.where(places[0] == places[1], sums, 0.0), 0, keepdims=True)
    terms[...] = jnp.broadcast_to(line[None], terms.shape)


def measures(gathered, primal_residual, dual_residual, gap):
    line = jnp.sum(gathered[...], 0)
    lane = lax.broadcasted_iota(jnp.int32, line.shape, 1)
    for k, (out, size) in enumerate(
        ((primal_residual, NROWS), (dual_residual, NCOLS), (gap, NCOLS))
    ):
        for j in range(2):
            out[j] = jnp.sum(jnp.where(lane == 2 * k + j, line, 0.0)) * (1.0 / size)


def shift(values, axis, step):
    return lax.ppermute(values, axis, [(k, (k + step) % 4) for k in range(4)])


def four_of(values, axis):
    return values, shift(values, axis, 1), shift(values, axis, -1), shift(values, axis, 2)


def four_over_row(values):
    total = call(sums, "sums", [(values.shape, F32)], four_of(values, "x"))
    return four_of(total[0], "y")


def swap_cores(values):
    return lax.ppermute(values, "core", [(0, 1), (1, 0)])


def exchange(copies, axes):
    return lax.all_to_all(copies, axes, 0, 0)


def shards(
    tiles, tile_rows, tile_cols, tile_count, row_types, var_types, rhs, cost, primal_start, dual_start
):
    tiles = tiles.reshape(SLOTS, TILE, TILE)
    blocks, columns, half = (ROW_BLOCKS, TILE), (COL_BLOCKS, TILE), (HALF, TILE)
    row_total = [pltpu.VMEM((ROW_BLOCKS, 8, TILE), F32)]
    col_total = [pltpu.VMEM((COL_BLOCKS, 8, TILE), F32)]

    duals, side = call(
        pack,
        "pack",
        [((N, ROWS_SHARE, TILE), F32), ((SIDE, TILE), F32)],
        (tile_count, tile_rows, tile_cols, row_types, rhs, dual_start, var_types, cost, primal_start),
        smem=1,
        hbm=8,
        scratch=[
            pltpu.VMEM((2, SLOTS), jnp.int32),
            pltpu.VMEM((2 * COLS_SHARE, TILE), jnp.int32),
            pltpu.VMEM((ROWS_SHARE, TILE), F32),
            pltpu.SemaphoreType.DMA((8,)),
        ],
        vmem=PACK_VMEM,
    )

    payload, dual0, table, pairs = call(
        first_adjoint,
        "first_adjoint",
        [
            ((COL_BLOCKS + 3 * COLS_SHARE, TILE), F32),
            (blocks, F32),
            ((8, TILE), jnp.int32),
            ((SLOTS, 2 * TILE, TILE), BF16),
        ],
        (tiles, exchange(duals, ("z", "core")), side),
        hbm=1,
        scratch=[
            pltpu.VMEM((SLOTS, TILE, TILE), F32),
            pltpu.SMEM((8, TILE), jnp.int32),
            pltpu.SemaphoreType.DMA((len(PIECES) + 1,)),
        ]
        + col_total,
        vmem=FIRST_VMEM,
    )
    payload = call(
        x_sums, "x_sums", [((COL_BLOCKS + 12 * COLS_SHARE, TILE), F32)], four_of(payload, "x")
    )

    kept, given, primal1, start_full, cost_full, free = call(
        first_forward,
        "first_forward",
        [(half, F32)] * 2 + [(columns, F32)] * 4,
        (table, *four_of(payload[0], "y"), pairs),
        smem=1,
        scratch=[pltpu.VMEM(columns, F32)] + row_total,
    )
    copies = call(
        image_copies,
        "image_copies",
        [((8, HALF + 2 * ROWS_SHARE, TILE), F32)],
        (kept, swap_cores(given), side),
    )
    held = call(
        image_sums, "image_sums", [((3 * HALF, TILE), F32)], (exchange(copies[0], "z"),)
    )[0]

    gradient, dual1, rhs_full, ineq = call(
        second_adjoint,
        "second_adjoint",
        [(columns, F32)] + [(blocks, F32)] * 3,
        (table, held, swap_cores(held), dual0, pairs),
        smem=1,
        scratch=[pltpu.VMEM(blocks, F32)] + col_total,
    )

    kept, given, primal2, gradient2, primal_mine = call(
        second_forward,
        "second_forward",
        [(blocks, F32)] * 2 + [(columns, F32)] * 2 + [((COLS_SHARE, TILE), F32)],
        (table, *four_over_row(gradient), primal1, cost_full, free, pairs),
        smem=1,
        scratch=[pltpu.VMEM(columns, F32)] + row_total,
    )
    copies = call(
        pair_copies, "pair_copies", [((8, HALF + 8, TILE), F32)], (kept, swap_cores(given))
    )
    held = call(pair_sums, "pair_sums", [((HALF + 8, TILE), F32)], (exchange(copies[0], "z"),))[0]

    payload, dual_mine = call(
        third_adjoint,
        "third_adjoint",
        [((COL_BLOCKS + 8, TILE), F32), ((ROWS_SHARE, TILE), F32)],
        (table, held, swap_cores(held), dual1, rhs_full, ineq, pairs),
        smem=1,
        scratch=[pltpu.VMEM(blocks, F32)] * 2 + col_total,
    )
    terms = call(
        column_terms,
        "column_terms",
        [((N, 1, TILE), F32)],
        (*four_over_row(payload), gradient2, primal1, primal2, cost_full, free),
    )
    primal_residual, dual_residual, gap = call(
        measures,
        "measures",
        [((2,), F32)] * 3,
        (exchange(terms[0], ("z", "core")),),
        smem_out=True,
    )
    return primal_mine[None], dual_mine[None], primal_residual, dual_residual, gap


def solution(mesh):
    rings = Mesh(mesh.devices.reshape(4, 4, 8, 2), ("y", "x", "z", "core"))
    row, col = ("y", "x"), ("z", "core")
    in_specs = (
        P(row, col, None, None, None),
        P(row, col, None),
        P(row, col, None),
        P(row, col),
        P(row, col, None),
        P(col, row, None),
        P(row, col, None),
        P(col, row, None),
        P(col, row, None),
        P(row, col, None),
    )
    out_specs = (P(col, row, None), P(row, col, None), P(), P(), P())
    return jax.shard_map(shards, mesh=rings, in_specs=in_specs, out_specs=out_specs, check_vma=False)
```

```python
import jax
import jax.numpy as jnp
from jax import lax
from jax.experimental import pallas as pl
from jax.experimental.pallas import tpu as pltpu
from jax.sharding import Mesh
from jax.sharding import PartitionSpec as P

N = 16
TILE = 128
ROW_BLOCKS = 64
COL_BLOCKS = 128
SLOTS = 64
ROWS_SHARE = ROW_BLOCKS // N
COLS_SHARE = COL_BLOCKS // N
HALF = ROW_BLOCKS // 2
NROWS = float(N * ROW_BLOCKS * TILE)
NCOLS = float(N * COL_BLOCKS * TILE)
PACK_VMEM = 60 * 2**20
FIRST_VMEM = 48 * 2**20
PIECES = (4, 12, 16, 32)
F32, BF16 = jnp.float32, jnp.bfloat16

SLOT_ROWS, SLOT_COLS, COUNT, AT_Y, AT_X, AT_Z, AT_CORE = range(7)
COL_KINDS, COST, ROW_SIDE, TABLE, SIDE = 8, 16, 24, 32, 40
STEP = 0.4

VMEM = pl.BlockSpec(memory_space=pltpu.VMEM)
SMEM = pl.BlockSpec(memory_space=pltpu.SMEM)
HBM = pl.BlockSpec(memory_space=pltpu.HBM)


def call(kernel, name, out_shapes, args, smem=0, hbm=0, smem_out=False, scratch=(), vmem=8 * 2**20):
    shapes = tuple(jax.ShapeDtypeStruct(s, d) for s, d in out_shapes)
    return pl.pallas_call(
        kernel,
        name=name,
        out_shape=shapes,
        in_specs=[SMEM] * smem + [HBM] * hbm + [VMEM] * (len(args) - smem - hbm),
        out_specs=tuple([SMEM if smem_out else VMEM] * len(shapes)),
        scratch_shapes=list(scratch),
        compiler_params=pltpu.CompilerParams(vmem_limit_bytes=vmem),
    )(*args)


def split(vector, copies):
    wide = jnp.broadcast_to(vector, (copies, TILE))
    lead = wide.astype(BF16).astype(F32)
    return [lead, wide - lead]


def adjoint_product(table, tile_pair, dual_ref, total):
    total[...] = jnp.zeros_like(total)
    adjoint_slots(table, tile_pair, dual_ref, total, 0, SLOTS)


def adjoint_slots(table, tile_pair, dual_ref, total, first, slots):
    def body(slot, carry):
        lhs = jnp.concatenate(split(dual_ref[pl.ds(table[SLOT_ROWS, slot], 1), :], 8), 0).astype(BF16)
        lhs = jnp.concatenate([lhs, lhs], 1)
        product = jnp.dot(lhs, tile_pair(slot), preferred_element_type=F32)
        total[table[SLOT_COLS, slot]] += product[0:8] + product[8:16]
        return carry

    lax.fori_loop(first, first + slots, body, 0, unroll=slots)


def forward_product(table, tile_pair, primal_refs, total):
    total[...] = jnp.zeros_like(total)
    copies = 8 // len(primal_refs)

    def body(slot, carry):
        parts = [split(ref[pl.ds(table[SLOT_COLS, slot], 1), :], copies) for ref in primal_refs]
        lhs = jnp.concatenate([p[0] for p in parts] + [p[1] for p in parts], 0).astype(BF16)
        product = lax.dot_general(
            lhs, tile_pair(slot), (((1,), (1,)), ((), ())), preferred_element_type=F32
        )
        product = product[:, :TILE] + product[:, TILE:]
        total[table[SLOT_ROWS, slot]] += product[0:8] + product[8:16]
        return carry

    lax.fori_loop(0, SLOTS, body, 0, unroll=SLOTS)


def clamp_primal(values, free):
    floor = jnp.maximum(values, 0.0)
    return jnp.where(free > 0.5, floor, jnp.minimum(floor, 1.0))


def clamp_dual(values, ineq):
    return jnp.where(ineq > 0.5, jnp.maximum(values, 0.0), values)


def own_columns(table):
    index = table[AT_Y, 0] * 4 + table[AT_X, 0]
    return pl.ds(pl.multiple_of(index * COLS_SHARE, COLS_SHARE), COLS_SHARE)


def index_col(table):
    return table[AT_Z, 0] * 2 + table[AT_CORE, 0]


def sum_four(refs, rows):
    own, right, left, opposite = (ref[rows, :] for ref in refs)
    return (own + opposite) + (right + left)


def pack(
    count, rows, cols, row_kinds, rhs, dual, col_kinds, cost, primal, duals, side, places, kinds, start, done
):
    copies = [
        pltpu.make_async_copy(source, target, done.at[k])
        for k, (source, target) in enumerate(
            (
                (rows.at[0], places.at[0:1]),
                (cols.at[0], places.at[1:2]),
                (dual.at[0], start),
                (rhs.at[0], side.at[ROW_SIDE : ROW_SIDE + ROWS_SHARE]),
                (row_kinds.at[0], kinds.at[0:ROWS_SHARE]),
                (primal.at[0], side.at[0:COLS_SHARE]),
                (cost.at[0], side.at[COST:ROW_SIDE]),
                (col_kinds.at[0], kinds.at[COLS_SHARE : 2 * COLS_SHARE]),
            )
        )
    ]
    for copy in copies:
        copy.start()
    side[TABLE + COUNT :, :] = jnp.zeros((SIDE - TABLE - COUNT, TILE), F32)
    for k, value in (
        (COUNT, count[0, 0]),
        (AT_Y, lax.axis_index("y")),
        (AT_X, lax.axis_index("x")),
        (AT_Z, lax.axis_index("z")),
        (AT_CORE, lax.axis_index("core")),
    ):
        side[TABLE + k : TABLE + k + 1, :] = jnp.full((1, TILE), value, jnp.int32).astype(F32)
    side[TABLE : TABLE + COUNT, :] = jnp.zeros((COUNT, TILE), F32)
    for copy in copies:
        copy.wait()
    side[TABLE : TABLE + COUNT, 0:SLOTS] = places[...].astype(F32)
    side[COL_KINDS:COST, :] = kinds[COLS_SHARE:, :].astype(F32)
    side[ROW_SIDE + ROWS_SHARE : TABLE, :] = kinds[0:ROWS_SHARE, :].astype(F32)
    duals[...] = jnp.broadcast_to(start[...][None], duals.shape)


def x_sums(own, right, left, opposite, payload):
    four = (own, right, left, opposite)
    payload[0:COL_BLOCKS, :] = sum_four(four, slice(0, COL_BLOCKS))
    share = 2 * COLS_SHARE
    for k, ref in enumerate(four):
        first = COL_BLOCKS + k * share
        payload[first : first + share, :] = ref[COL_BLOCKS : COL_BLOCKS + share, :]


def sums(own, right, left, opposite, total):
    total[...] = sum_four((own, right, left, opposite), slice(None))


def image_copies(kept, received, side, copies):
    block = jnp.concatenate([kept[...] + received[...], side[ROW_SIDE:TABLE, :]], 0)
    copies[...] = jnp.broadcast_to(block[None], copies.shape)


def image_sums(pieces, held):
    held[0:HALF, :] = jnp.sum(pieces[:, 0:HALF, :], 0)
    for k in range(8):
        for j in range(2):
            first = HALF + j * ROWS_SHARE
            into = HALF * (1 + j) + k * ROWS_SHARE
            held[into : into + ROWS_SHARE, :] = pieces[k, first : first + ROWS_SHARE, :]


def pair_copies(kept, received, copies):
    both = kept[...] + received[...]
    for k in range(8):
        first = HALF + k * ROWS_SHARE
        copies[k, 0:HALF, :] = both[0:HALF]
        copies[k, HALF : HALF + 8, :] = jnp.concatenate(
            [both[first : first + ROWS_SHARE], jnp.zeros((8 - ROWS_SHARE, TILE), F32)], 0
        )


def pair_sums(pieces, held):
    held[...] = jnp.sum(pieces[...], 0)


def first_adjoint(
    tiles, duals, side, payload, dual, table_out, pairs, chunks, table, done, total
):
    copies, first = [], 0
    for k, slots in enumerate(PIECES):
        part = pl.ds(first, slots)
        copies.append(pltpu.make_async_copy(tiles.at[part], chunks.at[part], done.at[k]))
        copies[k].start()
        first += slots
    table_out[...] = side[TABLE:, :].astype(jnp.int32)
    read = pltpu.make_async_copy(table_out, table, done.at[len(PIECES)])
    read.start()
    for k in range(N):
        dual[k * ROWS_SHARE : (k + 1) * ROWS_SHARE, :] = duals[k]
    total[...] = jnp.zeros_like(total)
    payload[COL_BLOCKS:, :] = side[0:COST, :]
    read.wait()

    def tile_pair(slot):
        tile = jnp.where(slot < table[COUNT, 0], chunks[slot], 0.0)
        lead = tile.astype(BF16)
        pair = jnp.concatenate([lead, (tile - lead.astype(F32)).astype(BF16)], 0)
        pairs[slot] = pair
        return pair

    first = 0
    for k, slots in enumerate(PIECES):
        copies[k].wait()
        adjoint_slots(table, tile_pair, dual, total, first, slots)
        first += slots
    payload[0:COL_BLOCKS, :] = total[:, 0, :]
    mine = own_columns(table)
    payload[mine, :] += side[0:COLS_SHARE, :] * (1.0 / STEP) - side[COST:ROW_SIDE, :]


def first_forward(
    table, own, right, left, opposite, pairs, kept, given, primal, start, free, extended, total
):
    y, x = table[AT_Y, 0], table[AT_X, 0]
    for j, (ref, dy) in enumerate(((own, 0), (right, 3), (left, 1), (opposite, 2))):
        for k, dx in enumerate((0, 3, 1, 2)):
            device = ((y + dy) & 3) * 4 + ((x + dx) & 3)
            block = pl.ds(pl.multiple_of(device * COLS_SHARE, COLS_SHARE), COLS_SHARE)
            for m, out in enumerate((start, free)):
                first = COL_BLOCKS + (2 * k + m) * COLS_SHARE
                out[block, :] = ref[first : first + COLS_SHARE, :]
    ascent = sum_four((own, right, left, opposite), slice(0, COL_BLOCKS))
    primal[...] = clamp_primal(STEP * ascent, free[...])
    extended[...] = 2.0 * primal[...] - start[...]
    forward_product(table, lambda slot: pairs[slot], [extended], total)
    mine = pl.multiple_of(table[AT_CORE, 0] * HALF, HALF)
    kept[...] = total[pl.ds(mine, HALF), 0, :]
    given[...] = total[pl.ds(HALF - mine, HALF), 0, :]


def second_adjoint(table, held, other, start, side, pairs, gradient, dual, rhs, ineq, image, total):
    first = table[AT_CORE, 0] == 0
    mine, theirs = held[...], other[...]
    for core, half in enumerate((jnp.where(first, mine, theirs), jnp.where(first, theirs, mine))):
        image[core * HALF : (core + 1) * HALF, :] = half[0:HALF]
        for k in range(8):
            block = slice((2 * k + core) * ROWS_SHARE, (2 * k + core + 1) * ROWS_SHARE)
            share = slice(k * ROWS_SHARE, (k + 1) * ROWS_SHARE)
            rhs[block, :] = half[HALF : 2 * HALF][share]
            ineq[block, :] = half[2 * HALF :][share]
    dual[...] = clamp_dual(start[...] + STEP * (rhs[...] - image[...]), ineq[...])
    adjoint_product(table, lambda slot: pairs[slot], dual, total)
    gradient[...] = total[:, 0, :]
    gradient[own_columns(table), :] -= side[COST:ROW_SIDE, :]


def second_forward(
    table, own, right, left, opposite, before, free, pairs, kept, given, primal, ascent, primal_mine, extended, total
):
    ascent[...] = sum_four((own, right, left, opposite), slice(0, COL_BLOCKS))
    primal[...] = clamp_primal(before[...] + STEP * ascent[...], free[...])
    extended[...] = 2.0 * primal[...] - before[...]
    primal_mine[...] = primal[own_columns(table), :]
    forward_product(table, lambda slot: pairs[slot], [extended, primal], total)
    mine = pl.multiple_of(table[AT_CORE, 0] * HALF, HALF)
    for k, part in enumerate((0, 4)):
        rows = slice(k * HALF, (k + 1) * HALF)
        kept[rows, :] = total[pl.ds(mine, HALF), part, :]
        given[rows, :] = total[pl.ds(HALF - mine, HALF), part, :]


def third_adjoint(
    table, held, other, before, rhs, ineq, side, primal1, primal2, pairs, payload, mine, dual, image, total
):
    half = pl.multiple_of(table[AT_CORE, 0] * HALF, HALF)
    image[pl.ds(half, HALF), :] = held[0:HALF, :]
    image[pl.ds(HALF - half, HALF), :] = other[0:HALF, :]
    dual[...] = clamp_dual(before[...] + STEP * (rhs[...] - image[...]), ineq[...])
    mine[...] = dual[pl.ds(index_col(table) * ROWS_SHARE, ROWS_SHARE), :]
    share = pl.ds(half + table[AT_Z, 0] * ROWS_SHARE, ROWS_SHARE)
    plain = held[HALF : HALF + ROWS_SHARE, :]
    bound, kind, last = rhs[share, :], ineq[share, :], dual[share, :]
    terms = []
    for product in (plain, 0.5 * (3.0 * plain - image[share, :])):
        residual = bound - product
        residual = jnp.where(kind > 0.5, jnp.maximum(residual, 0.0), residual)
        terms.append(jnp.sum(residual * residual, 0, keepdims=True))
    columns = own_columns(table)
    price, final = side[COST:ROW_SIDE, :], primal2[columns, :]
    for primal, value in (
        (final, last),
        (0.5 * (primal1[columns, :] + final), 0.5 * (before[share, :] + last)),
    ):
        gain = jnp.sum(price * primal, 0, keepdims=True)
        terms.append(gain - jnp.sum(bound * value, 0, keepdims=True))
    payload[COL_BLOCKS : COL_BLOCKS + 8, :] = jnp.concatenate(terms + terms, 0)
    adjoint_product(table, lambda slot: pairs[slot], dual, total)
    payload[0:COL_BLOCKS, :] = total[:, 0, :]
    payload[columns, :] -= price


def column_terms(own, right, left, opposite, earlier, free, terms):
    four = (own, right, left, opposite)
    ascent = sum_four(four, slice(0, COL_BLOCKS))
    row_terms = sum_four(four, slice(COL_BLOCKS, COL_BLOCKS + 8))
    kind = free[...]
    squares, gaps = [], []
    for k, reduced in enumerate((-ascent, -0.5 * (earlier[...] + ascent))):
        low = jnp.minimum(reduced, 0.0)
        violation = jnp.where(kind > 0.5, low, 0.0)
        box = jnp.where(kind > 0.5, 0.0, low)
        squares.append(jnp.sum(violation * violation, 0, keepdims=True))
        gaps.append(row_terms[2 + k : 3 + k] - jnp.sum(box, 0, keepdims=True))
    rows = jnp.concatenate([row_terms[0:2]] + squares + gaps + squares, 0)
    sums = jnp.broadcast_to(jnp.sum(rows, 1, keepdims=True), rows.shape)
    places = [lax.broadcasted_iota(jnp.int32, rows.shape, k) for k in range(2)]
    line = jnp.sum(jnp.where(places[0] == places[1], sums, 0.0), 0, keepdims=True)
    terms[...] = jnp.broadcast_to(line[None], terms.shape)


def measures(gathered, primal_residual, dual_residual, gap):
    line = jnp.sum(gathered[...], 0)
    lane = lax.broadcasted_iota(jnp.int32, line.shape, 1)
    for k, (out, size) in enumerate(
        ((primal_residual, NROWS), (dual_residual, NCOLS), (gap, NCOLS))
    ):
        for j in range(2):
            out[j] = jnp.sum(jnp.where(lane == 2 * k + j, line, 0.0)) * (1.0 / size)


def shift(values, axis, step):
    return lax.ppermute(values, axis, [(k, (k + step) % 4) for k in range(4)])


def four_of(values, axis):
    return values, shift(values, axis, 1), shift(values, axis, -1), shift(values, axis, 2)


def four_over_row(values):
    total = call(sums, "sums", [(values.shape, F32)], four_of(values, "x"))
    return four_of(total[0], "y")


def swap_cores(values):
    return lax.ppermute(values, "core", [(0, 1), (1, 0)])


def exchange(copies, axes):
    return lax.all_to_all(copies, axes, 0, 0)


def shards(
    tiles, tile_rows, tile_cols, tile_count, row_types, var_types, rhs, cost, primal_start, dual_start
):
    tiles = tiles.reshape(SLOTS, TILE, TILE)
    blocks, columns, half = (ROW_BLOCKS, TILE), (COL_BLOCKS, TILE), (HALF, TILE)
    row_total = [pltpu.VMEM((ROW_BLOCKS, 8, TILE), F32)]
    col_total = [pltpu.VMEM((COL_BLOCKS, 8, TILE), F32)]

    duals, side = call(
        pack,
        "pack",
        [((N, ROWS_SHARE, TILE), F32), ((SIDE, TILE), F32)],
        (tile_count, tile_rows, tile_cols, row_types, rhs, dual_start, var_types, cost, primal_start),
        smem=1,
        hbm=8,
        scratch=[
            pltpu.VMEM((2, SLOTS), jnp.int32),
            pltpu.VMEM((2 * COLS_SHARE, TILE), jnp.int32),
            pltpu.VMEM((ROWS_SHARE, TILE), F32),
            pltpu.SemaphoreType.DMA((8,)),
        ],
        vmem=PACK_VMEM,
    )

    payload, dual0, table, pairs = call(
        first_adjoint,
        "first_adjoint",
        [
            ((COL_BLOCKS + 2 * COLS_SHARE, TILE), F32),
            (blocks, F32),
            ((8, TILE), jnp.int32),
            ((SLOTS, 2 * TILE, TILE), BF16),
        ],
        (tiles, exchange(duals, ("z", "core")), side),
        hbm=1,
        scratch=[
            pltpu.VMEM((SLOTS, TILE, TILE), F32),
            pltpu.SMEM((8, TILE), jnp.int32),
            pltpu.SemaphoreType.DMA((len(PIECES) + 1,)),
        ]
        + col_total,
        vmem=FIRST_VMEM,
    )
    payload = call(
        x_sums, "x_sums", [((COL_BLOCKS + 8 * COLS_SHARE, TILE), F32)], four_of(payload, "x")
    )

    kept, given, primal1, _, free = call(
        first_forward,
        "first_forward",
        [(half, F32)] * 2 + [(columns, F32)] * 3,
        (table, *four_of(payload[0], "y"), pairs),
        smem=1,
        scratch=[pltpu.VMEM(columns, F32)] + row_total,
    )
    copies = call(
        image_copies,
        "image_copies",
        [((8, HALF + 2 * ROWS_SHARE, TILE), F32)],
        (kept, swap_cores(given), side),
    )
    held = call(
        image_sums, "image_sums", [((3 * HALF, TILE), F32)], (exchange(copies[0], "z"),)
    )[0]

    gradient, dual1, rhs_full, ineq = call(
        second_adjoint,
        "second_adjoint",
        [(columns, F32)] + [(blocks, F32)] * 3,
        (table, held, swap_cores(held), dual0, side, pairs),
        smem=1,
        scratch=[pltpu.VMEM(blocks, F32)] + col_total,
    )

    kept, given, primal2, ascent2, primal_mine = call(
        second_forward,
        "second_forward",
        [(blocks, F32)] * 2 + [(columns, F32)] * 2 + [((COLS_SHARE, TILE), F32)],
        (table, *four_over_row(gradient), primal1, free, pairs),
        smem=1,
        scratch=[pltpu.VMEM(columns, F32)] + row_total,
    )
    copies = call(
        pair_copies, "pair_copies", [((8, HALF + 8, TILE), F32)], (kept, swap_cores(given))
    )
    held = call(pair_sums, "pair_sums", [((HALF + 8, TILE), F32)], (exchange(copies[0], "z"),))[0]

    payload, dual_mine = call(
        third_adjoint,
        "third_adjoint",
        [((COL_BLOCKS + 8, TILE), F32), ((ROWS_SHARE, TILE), F32)],
        (table, held, swap_cores(held), dual1, rhs_full, ineq, side, primal1, primal2, pairs),
        smem=1,
        scratch=[pltpu.VMEM(blocks, F32)] * 2 + col_total,
    )
    terms = call(
        column_terms,
        "column_terms",
        [((N, 1, TILE), F32)],
        (*four_over_row(payload), ascent2, free),
    )
    primal_residual, dual_residual, gap = call(
        measures,
        "measures",
        [((2,), F32)] * 3,
        (exchange(terms[0], ("z", "core")),),
        smem_out=True,
    )
    return primal_mine[None], dual_mine[None], primal_residual, dual_residual, gap


def solution(mesh):
    rings = Mesh(mesh.devices.reshape(4, 4, 8, 2), ("y", "x", "z", "core"))
    row, col = ("y", "x"), ("z", "core")
    in_specs = (
        P(row, col, None, None, None),
        P(row, col, None),
        P(row, col, None),
        P(row, col),
        P(row, col, None),
        P(col, row, None),
        P(row, col, None),
        P(col, row, None),
        P(col, row, None),
        P(row, col, None),
    )
    out_specs = (P(col, row, None), P(row, col, None), P(), P(), P())
    return jax.shard_map(shards, mesh=rings, in_specs=in_specs, out_specs=out_specs, check_vma=False)
```

```python
import jax
import jax.numpy as jnp
from jax import lax
from jax.experimental import pallas as pl
from jax.experimental.pallas import tpu as pltpu
from jax.sharding import Mesh
from jax.sharding import PartitionSpec as P

N = 16
TILE = 128
ROW_BLOCKS = 64
COL_BLOCKS = 128
SLOTS = 64
ROWS_SHARE = ROW_BLOCKS // N
COLS_SHARE = COL_BLOCKS // N
HALF = ROW_BLOCKS // 2
NROWS = float(N * ROW_BLOCKS * TILE)
NCOLS = float(N * COL_BLOCKS * TILE)
PACK_VMEM = 60 * 2**20
FIRST_VMEM = 48 * 2**20
PIECES = (8, 16, 16, 16, 8)
F32, BF16 = jnp.float32, jnp.bfloat16

SLOT_ROWS, SLOT_COLS, COUNT, AT_Y, AT_X, AT_Z, AT_CORE = range(7)
COL_KINDS, COST, ROW_SIDE, TABLE, SIDE = 8, 16, 24, 32, 40
STEP = 0.4

VMEM = pl.BlockSpec(memory_space=pltpu.VMEM)
SMEM = pl.BlockSpec(memory_space=pltpu.SMEM)
HBM = pl.BlockSpec(memory_space=pltpu.HBM)


def call(kernel, name, out_shapes, args, smem=0, hbm=0, smem_out=False, scratch=(), vmem=8 * 2**20, cost=None):
    shapes = tuple(jax.ShapeDtypeStruct(s, d) for s, d in out_shapes)
    return pl.pallas_call(
        kernel,
        name=name,
        out_shape=shapes,
        in_specs=[SMEM] * smem + [HBM] * hbm + [VMEM] * (len(args) - smem - hbm),
        out_specs=tuple([SMEM if smem_out else VMEM] * len(shapes)),
        scratch_shapes=list(scratch),
        compiler_params=pltpu.CompilerParams(vmem_limit_bytes=vmem),
        cost_estimate=cost,
    )(*args)


def split(vector, copies):
    wide = jnp.broadcast_to(vector, (copies, TILE))
    lead = wide.astype(BF16).astype(F32)
    return [lead, wide - lead]


def adjoint_product(table, tile_pair, dual_ref, total):
    total[...] = jnp.zeros_like(total)
    adjoint_slots(table, tile_pair, dual_ref, total, 0, SLOTS)


def adjoint_slots(table, tile_pair, dual_ref, total, first, slots):
    def body(slot, carry):
        lhs = jnp.concatenate(split(dual_ref[pl.ds(table[SLOT_ROWS, slot], 1), :], 8), 0).astype(BF16)
        lhs = jnp.concatenate([lhs, lhs], 1)
        product = jnp.dot(lhs, tile_pair(slot), preferred_element_type=F32)
        total[table[SLOT_COLS, slot]] += product[0:8] + product[8:16]
        return carry

    lax.fori_loop(first, first + slots, body, 0, unroll=slots)


def forward_product(table, tile_pair, primal_refs, total):
    total[...] = jnp.zeros_like(total)
    copies = 8 // len(primal_refs)

    def body(slot, carry):
        parts = [split(ref[pl.ds(table[SLOT_COLS, slot], 1), :], copies) for ref in primal_refs]
        lhs = jnp.concatenate([p[0] for p in parts] + [p[1] for p in parts], 0).astype(BF16)
        lhs = jnp.concatenate([lhs, lhs], 1)
        product = jnp.dot(lhs, tile_pair(slot), preferred_element_type=F32)
        total[table[SLOT_ROWS, slot]] += product[0:8] + product[8:16]
        return carry

    lax.fori_loop(0, SLOTS, body, 0, unroll=SLOTS)


def clamp_primal(values, free):
    floor = jnp.maximum(values, 0.0)
    return jnp.where(free > 0.5, floor, jnp.minimum(floor, 1.0))


def clamp_dual(values, ineq):
    return jnp.where(ineq > 0.5, jnp.maximum(values, 0.0), values)


def own_columns(table):
    index = table[AT_Y, 0] * 4 + table[AT_X, 0]
    return pl.ds(pl.multiple_of(index * COLS_SHARE, COLS_SHARE), COLS_SHARE)


def index_col(table):
    return table[AT_Z, 0] * 2 + table[AT_CORE, 0]


def sum_four(refs, rows):
    own, right, left, opposite = (ref[rows, :] for ref in refs)
    return (own + opposite) + (right + left)


def pack(
    count, rows, cols, row_kinds, rhs, dual, col_kinds, cost, primal, duals, side, places, kinds, start, done
):
    copies = [
        pltpu.make_async_copy(source, target, done.at[k])
        for k, (source, target) in enumerate(
            (
                (rows.at[0], places.at[0:1]),
                (cols.at[0], places.at[1:2]),
                (dual.at[0], start),
                (rhs.at[0], side.at[ROW_SIDE : ROW_SIDE + ROWS_SHARE]),
                (row_kinds.at[0], kinds.at[0:ROWS_SHARE]),
                (primal.at[0], side.at[0:COLS_SHARE]),
                (cost.at[0], side.at[COST:ROW_SIDE]),
                (col_kinds.at[0], kinds.at[COLS_SHARE : 2 * COLS_SHARE]),
            )
        )
    ]
    for copy in copies:
        copy.start()
    side[TABLE + COUNT :, :] = jnp.zeros((SIDE - TABLE - COUNT, TILE), F32)
    for k, value in (
        (COUNT, count[0, 0]),
        (AT_Y, lax.axis_index("y")),
        (AT_X, lax.axis_index("x")),
        (AT_Z, lax.axis_index("z")),
        (AT_CORE, lax.axis_index("core")),
    ):
        side[TABLE + k : TABLE + k + 1, :] = jnp.full((1, TILE), value, jnp.int32).astype(F32)
    side[TABLE : TABLE + COUNT, :] = jnp.zeros((COUNT, TILE), F32)
    for copy in copies:
        copy.wait()
    side[TABLE : TABLE + COUNT, 0:SLOTS] = places[...].astype(F32)
    side[COL_KINDS:COST, :] = kinds[COLS_SHARE:, :].astype(F32)
    side[ROW_SIDE + ROWS_SHARE : TABLE, :] = kinds[0:ROWS_SHARE, :].astype(F32)
    duals[...] = jnp.broadcast_to(start[...][None], duals.shape)


def turn(pairs, turned):
    for slot in range(SLOTS):
        for part in range(2):
            rows = slice(part * TILE, (part + 1) * TILE)
            turned[slot, rows, :] = pairs[slot, rows, :].T


def x_sums(own, right, left, opposite, payload):
    four = (own, right, left, opposite)
    payload[0:COL_BLOCKS, :] = sum_four(four, slice(0, COL_BLOCKS))
    share = 2 * COLS_SHARE
    for k, ref in enumerate(four):
        first = COL_BLOCKS + k * share
        payload[first : first + share, :] = ref[COL_BLOCKS : COL_BLOCKS + share, :]


def sums(own, right, left, opposite, total):
    total[...] = sum_four((own, right, left, opposite), slice(None))


def image_copies(kept, received, side, copies):
    block = jnp.concatenate([kept[...] + received[...], side[ROW_SIDE:TABLE, :]], 0)
    copies[...] = jnp.broadcast_to(block[None], copies.shape)


def image_sums(pieces, held):
    held[0:HALF, :] = jnp.sum(pieces[:, 0:HALF, :], 0)
    for k in range(8):
        for j in range(2):
            first = HALF + j * ROWS_SHARE
            into = HALF * (1 + j) + k * ROWS_SHARE
            held[into : into + ROWS_SHARE, :] = pieces[k, first : first + ROWS_SHARE, :]


def pair_copies(kept, received, copies):
    both = kept[...] + received[...]
    for k in range(8):
        first = HALF + k * ROWS_SHARE
        copies[k, 0:HALF, :] = both[0:HALF]
        copies[k, HALF : HALF + 8, :] = jnp.concatenate(
            [both[first : first + ROWS_SHARE], jnp.zeros((8 - ROWS_SHARE, TILE), F32)], 0
        )


def pair_sums(pieces, held):
    held[...] = jnp.sum(pieces[...], 0)


def first_adjoint(
    tiles, duals, side, payload, dual, table_out, pairs, chunks, table, done, total
):
    copies, first = [], 0
    for k, slots in enumerate(PIECES):
        part = pl.ds(first, slots)
        copies.append(pltpu.make_async_copy(tiles.at[part], chunks.at[part], done.at[k]))
        copies[k].start()
        first += slots
    table_out[...] = side[TABLE:, :].astype(jnp.int32)
    read = pltpu.make_async_copy(table_out, table, done.at[len(PIECES)])
    read.start()
    for k in range(N):
        dual[k * ROWS_SHARE : (k + 1) * ROWS_SHARE, :] = duals[k]
    total[...] = jnp.zeros_like(total)
    payload[COL_BLOCKS:, :] = side[0:COST, :]
    read.wait()

    def tile_pair(slot):
        tile = jnp.where(slot < table[COUNT, 0], chunks[slot], 0.0)
        lead = tile.astype(BF16)
        pair = jnp.concatenate([lead, (tile - lead.astype(F32)).astype(BF16)], 0)
        pairs[slot] = pair
        return pair

    first = 0
    for k, slots in enumerate(PIECES):
        copies[k].wait()
        adjoint_slots(table, tile_pair, dual, total, first, slots)
        first += slots
    payload[0:COL_BLOCKS, :] = total[:, 0, :]
    mine = own_columns(table)
    payload[mine, :] += side[0:COLS_SHARE, :] * (1.0 / STEP) - side[COST:ROW_SIDE, :]


def first_forward(
    table, own, right, left, opposite, turned, kept, given, primal, start, free, extended, total
):
    y, x = table[AT_Y, 0], table[AT_X, 0]
    for j, (ref, dy) in enumerate(((own, 0), (right, 3), (left, 1), (opposite, 2))):
        for k, dx in enumerate((0, 3, 1, 2)):
            device = ((y + dy) & 3) * 4 + ((x + dx) & 3)
            block = pl.ds(pl.multiple_of(device * COLS_SHARE, COLS_SHARE), COLS_SHARE)
            for m, out in enumerate((start, free)):
                first = COL_BLOCKS + (2 * k + m) * COLS_SHARE
                out[block, :] = ref[first : first + COLS_SHARE, :]
    ascent = sum_four((own, right, left, opposite), slice(0, COL_BLOCKS))
    primal[...] = clamp_primal(STEP * ascent, free[...])
    extended[...] = 2.0 * primal[...] - start[...]
    forward_product(table, lambda slot: turned[slot], [extended], total)
    mine = pl.multiple_of(table[AT_CORE, 0] * HALF, HALF)
    kept[...] = total[pl.ds(mine, HALF), 0, :]
    given[...] = total[pl.ds(HALF - mine, HALF), 0, :]


def second_adjoint(table, held, other, start, side, pairs, gradient, dual, rhs, ineq, image, total):
    first = table[AT_CORE, 0] == 0
    mine, theirs = held[...], other[...]
    for core, half in enumerate((jnp.where(first, mine, theirs), jnp.where(first, theirs, mine))):
        image[core * HALF : (core + 1) * HALF, :] = half[0:HALF]
        for k in range(8):
            block = slice((2 * k + core) * ROWS_SHARE, (2 * k + core + 1) * ROWS_SHARE)
            share = slice(k * ROWS_SHARE, (k + 1) * ROWS_SHARE)
            rhs[block, :] = half[HALF : 2 * HALF][share]
            ineq[block, :] = half[2 * HALF :][share]
    dual[...] = clamp_dual(start[...] + STEP * (rhs[...] - image[...]), ineq[...])
    adjoint_product(table, lambda slot: pairs[slot], dual, total)
    gradient[...] = total[:, 0, :]
    gradient[own_columns(table), :] -= side[COST:ROW_SIDE, :]


def second_forward(
    table, own, right, left, opposite, before, free, turned, kept, given, primal, ascent, primal_mine, extended, total
):
    ascent[...] = sum_four((own, right, left, opposite), slice(0, COL_BLOCKS))
    primal[...] = clamp_primal(before[...] + STEP * ascent[...], free[...])
    extended[...] = 2.0 * primal[...] - before[...]
    primal_mine[...] = primal[own_columns(table), :]
    forward_product(table, lambda slot: turned[slot], [extended, primal], total)
    mine = pl.multiple_of(table[AT_CORE, 0] * HALF, HALF)
    for k, part in enumerate((0, 4)):
        rows = slice(k * HALF, (k + 1) * HALF)
        kept[rows, :] = total[pl.ds(mine, HALF), part, :]
        given[rows, :] = total[pl.ds(HALF - mine, HALF), part, :]


def third_adjoint(
    table, held, other, before, rhs, ineq, side, primal1, primal2, pairs, payload, mine, dual, image, total
):
    half = pl.multiple_of(table[AT_CORE, 0] * HALF, HALF)
    image[pl.ds(half, HALF), :] = held[0:HALF, :]
    image[pl.ds(HALF - half, HALF), :] = other[0:HALF, :]
    dual[...] = clamp_dual(before[...] + STEP * (rhs[...] - image[...]), ineq[...])
    mine[...] = dual[pl.ds(index_col(table) * ROWS_SHARE, ROWS_SHARE), :]
    share = pl.ds(half + table[AT_Z, 0] * ROWS_SHARE, ROWS_SHARE)
    plain = held[HALF : HALF + ROWS_SHARE, :]
    bound, kind, last = rhs[share, :], ineq[share, :], dual[share, :]
    terms = []
    for product in (plain, 0.5 * (3.0 * plain - image[share, :])):
        residual = bound - product
        residual = jnp.where(kind > 0.5, jnp.maximum(residual, 0.0), residual)
        terms.append(jnp.sum(residual * residual, 0, keepdims=True))
    columns = own_columns(table)
    price, final = side[COST:ROW_SIDE, :], primal2[columns, :]
    for primal, value in (
        (final, last),
        (0.5 * (primal1[columns, :] + final), 0.5 * (before[share, :] + last)),
    ):
        gain = jnp.sum(price * primal, 0, keepdims=True)
        terms.append(gain - jnp.sum(bound * value, 0, keepdims=True))
    payload[COL_BLOCKS : COL_BLOCKS + 8, :] = jnp.concatenate(terms + terms, 0)
    adjoint_product(table, lambda slot: pairs[slot], dual, total)
    payload[0:COL_BLOCKS, :] = total[:, 0, :]
    payload[columns, :] -= price


def column_terms(own, right, left, opposite, earlier, free, terms):
    four = (own, right, left, opposite)
    ascent = sum_four(four, slice(0, COL_BLOCKS))
    row_terms = sum_four(four, slice(COL_BLOCKS, COL_BLOCKS + 8))
    kind = free[...]
    squares, gaps = [], []
    for k, reduced in enumerate((-ascent, -0.5 * (earlier[...] + ascent))):
        low = jnp.minimum(reduced, 0.0)
        violation = jnp.where(kind > 0.5, low, 0.0)
        box = jnp.where(kind > 0.5, 0.0, low)
        squares.append(jnp.sum(violation * violation, 0, keepdims=True))
        gaps.append(row_terms[2 + k : 3 + k] - jnp.sum(box, 0, keepdims=True))
    rows = jnp.concatenate([row_terms[0:2]] + squares + gaps + squares, 0)
    sums = jnp.broadcast_to(jnp.sum(rows, 1, keepdims=True), rows.shape)
    places = [lax.broadcasted_iota(jnp.int32, rows.shape, k) for k in range(2)]
    line = jnp.sum(jnp.where(places[0] == places[1], sums, 0.0), 0, keepdims=True)
    terms[...] = jnp.broadcast_to(line[None], terms.shape)


def measures(gathered, primal_residual, dual_residual, gap):
    line = jnp.sum(gathered[...], 0)
    lane = lax.broadcasted_iota(jnp.int32, line.shape, 1)
    for k, (out, size) in enumerate(
        ((primal_residual, NROWS), (dual_residual, NCOLS), (gap, NCOLS))
    ):
        for j in range(2):
            out[j] = jnp.sum(jnp.where(lane == 2 * k + j, line, 0.0)) * (1.0 / size)


def shift(values, axis, step):
    return lax.ppermute(values, axis, [(k, (k + step) % 4) for k in range(4)])


def four_of(values, axis):
    return values, shift(values, axis, 1), shift(values, axis, -1), shift(values, axis, 2)


def four_over_row(values):
    total = call(sums, "sums", [(values.shape, F32)], four_of(values, "x"))
    return four_of(total[0], "y")


def swap_cores(values):
    return lax.ppermute(values, "core", [(0, 1), (1, 0)])


def exchange(copies, axes):
    return lax.all_to_all(copies, axes, 0, 0)


def shards(
    tiles, tile_rows, tile_cols, tile_count, row_types, var_types, rhs, cost, primal_start, dual_start
):
    tiles = tiles.reshape(SLOTS, TILE, TILE)
    blocks, columns, half = (ROW_BLOCKS, TILE), (COL_BLOCKS, TILE), (HALF, TILE)
    row_total = [pltpu.VMEM((ROW_BLOCKS, 8, TILE), F32)]
    col_total = [pltpu.VMEM((COL_BLOCKS, 8, TILE), F32)]

    duals, side = call(
        pack,
        "pack",
        [((N, ROWS_SHARE, TILE), F32), ((SIDE, TILE), F32)],
        (tile_count, tile_rows, tile_cols, row_types, rhs, dual_start, var_types, cost, primal_start),
        smem=1,
        hbm=8,
        scratch=[
            pltpu.VMEM((2, SLOTS), jnp.int32),
            pltpu.VMEM((2 * COLS_SHARE, TILE), jnp.int32),
            pltpu.VMEM((ROWS_SHARE, TILE), F32),
            pltpu.SemaphoreType.DMA((8,)),
        ],
        vmem=PACK_VMEM,
    )

    payload, dual0, table, pairs = call(
        first_adjoint,
        "first_adjoint",
        [
            ((COL_BLOCKS + 2 * COLS_SHARE, TILE), F32),
            (blocks, F32),
            ((8, TILE), jnp.int32),
            ((SLOTS, 2 * TILE, TILE), BF16),
        ],
        (tiles, exchange(duals, ("z", "core")), side),
        hbm=1,
        scratch=[
            pltpu.VMEM((SLOTS, TILE, TILE), F32),
            pltpu.SMEM((8, TILE), jnp.int32),
            pltpu.SemaphoreType.DMA((len(PIECES) + 1,)),
        ]
        + col_total,
        vmem=FIRST_VMEM,
    )
    turned = call(
        turn,
        "turn",
        [((SLOTS, 2 * TILE, TILE), BF16)],
        (pairs,),
        cost=pl.CostEstimate(flops=0, bytes_accessed=2**23, transcendentals=0),
    )[0]
    payload = call(
        x_sums, "x_sums", [((COL_BLOCKS + 8 * COLS_SHARE, TILE), F32)], four_of(payload, "x")
    )

    kept, given, primal1, _, free = call(
        first_forward,
        "first_forward",
        [(half, F32)] * 2 + [(columns, F32)] * 3,
        (table, *four_of(payload[0], "y"), turned),
        smem=1,
        scratch=[pltpu.VMEM(columns, F32)] + row_total,
    )
    copies = call(
        image_copies,
        "image_copies",
        [((8, HALF + 2 * ROWS_SHARE, TILE), F32)],
        (kept, swap_cores(given), side),
    )
    held = call(
        image_sums, "image_sums", [((3 * HALF, TILE), F32)], (exchange(copies[0], "z"),)
    )[0]

    gradient, dual1, rhs_full, ineq = call(
        second_adjoint,
        "second_adjoint",
        [(columns, F32)] + [(blocks, F32)] * 3,
        (table, held, swap_cores(held), dual0, side, pairs),
        smem=1,
        scratch=[pltpu.VMEM(blocks, F32)] + col_total,
    )

    kept, given, primal2, ascent2, primal_mine = call(
        second_forward,
        "second_forward",
        [(blocks, F32)] * 2 + [(columns, F32)] * 2 + [((COLS_SHARE, TILE), F32)],
        (table, *four_over_row(gradient), primal1, free, turned),
        smem=1,
        scratch=[pltpu.VMEM(columns, F32)] + row_total,
    )
    copies = call(
        pair_copies, "pair_copies", [((8, HALF + 8, TILE), F32)], (kept, swap_cores(given))
    )
    held = call(pair_sums, "pair_sums", [((HALF + 8, TILE), F32)], (exchange(copies[0], "z"),))[0]

    payload, dual_mine = call(
        third_adjoint,
        "third_adjoint",
        [((COL_BLOCKS + 8, TILE), F32), ((ROWS_SHARE, TILE), F32)],
        (table, held, swap_cores(held), dual1, rhs_full, ineq, side, primal1, primal2, pairs),
        smem=1,
        scratch=[pltpu.VMEM(blocks, F32)] * 2 + col_total,
    )
    terms = call(
        column_terms,
        "column_terms",
        [((N, 1, TILE), F32)],
        (*four_over_row(payload), ascent2, free),
    )
    primal_residual, dual_residual, gap = call(
        measures,
        "measures",
        [((2,), F32)] * 3,
        (exchange(terms[0], ("z", "core")),),
        smem_out=True,
    )
    return primal_mine[None], dual_mine[None], primal_residual, dual_residual, gap


def solution(mesh):
    rings = Mesh(mesh.devices.reshape(4, 4, 8, 2), ("y", "x", "z", "core"))
    row, col = ("y", "x"), ("z", "core")
    in_specs = (
        P(row, col, None, None, None),
        P(row, col, None),
        P(row, col, None),
        P(row, col),
        P(row, col, None),
        P(col, row, None),
        P(row, col, None),
        P(col, row, None),
        P(col, row, None),
        P(row, col, None),
    )
    out_specs = (P(col, row, None), P(row, col, None), P(), P(), P())
    return jax.shard_map(shards, mesh=rings, in_specs=in_specs, out_specs=out_specs, check_vma=False)
```

```python
import jax
import jax.numpy as jnp
from jax import lax
from jax.experimental import pallas as pl
from jax.experimental.pallas import tpu as pltpu
from jax.sharding import Mesh
from jax.sharding import PartitionSpec as P

N = 16
TILE = 128
ROW_BLOCKS = 64
COL_BLOCKS = 128
SLOTS = 64
ROWS_SHARE = ROW_BLOCKS // N
COLS_SHARE = COL_BLOCKS // N
HALF = ROW_BLOCKS // 2
NROWS = float(N * ROW_BLOCKS * TILE)
NCOLS = float(N * COL_BLOCKS * TILE)
PACK_VMEM = 60 * 2**20
FIRST_VMEM = 48 * 2**20
PIECES = (8, 16, 16, 16, 8)
F32, BF16 = jnp.float32, jnp.bfloat16

SLOT_ROWS, SLOT_COLS, COUNT, AT_Y, AT_X, AT_Z, AT_CORE = range(7)
COL_KINDS, COST, ROW_SIDE, TABLE, SIDE = 8, 16, 24, 32, 40
STEP = 0.4

VMEM = pl.BlockSpec(memory_space=pltpu.VMEM)
SMEM = pl.BlockSpec(memory_space=pltpu.SMEM)
HBM = pl.BlockSpec(memory_space=pltpu.HBM)


def call(kernel, name, out_shapes, args, smem=0, hbm=0, smem_out=False, scratch=(), vmem=8 * 2**20, cost=None):
    shapes = tuple(jax.ShapeDtypeStruct(s, d) for s, d in out_shapes)
    return pl.pallas_call(
        kernel,
        name=name,
        out_shape=shapes,
        in_specs=[SMEM] * smem + [HBM] * hbm + [VMEM] * (len(args) - smem - hbm),
        out_specs=tuple([SMEM if smem_out else VMEM] * len(shapes)),
        scratch_shapes=list(scratch),
        compiler_params=pltpu.CompilerParams(vmem_limit_bytes=vmem),
        cost_estimate=cost,
    )(*args)


def split(vector, copies):
    wide = jnp.broadcast_to(vector, (copies, TILE))
    lead = wide.astype(BF16).astype(F32)
    return [lead, wide - lead]


def adjoint_product(table, tile_pair, dual_ref, total):
    total[...] = jnp.zeros_like(total)
    adjoint_slots(table, tile_pair, dual_ref, total, 0, SLOTS)


def adjoint_slots(table, tile_pair, dual_ref, total, first, slots):
    def body(slot, carry):
        lhs = jnp.concatenate(split(dual_ref[pl.ds(table[SLOT_ROWS, slot], 1), :], 8), 0).astype(BF16)
        lhs = jnp.concatenate([lhs, lhs], 1)
        product = jnp.dot(lhs, tile_pair(slot), preferred_element_type=F32)
        total[table[SLOT_COLS, slot]] += product[0:8] + product[8:16]
        return carry

    lax.fori_loop(first, first + slots, body, 0, unroll=slots)


def forward_product(table, tile_pair, primal_refs, total):
    total[...] = jnp.zeros_like(total)
    copies = 8 // len(primal_refs)

    def body(slot, carry):
        parts = [split(ref[pl.ds(table[SLOT_COLS, slot], 1), :], copies) for ref in primal_refs]
        lhs = jnp.concatenate([p[0] for p in parts] + [p[1] for p in parts], 0).astype(BF16)
        lhs = jnp.concatenate([lhs, lhs], 1)
        product = jnp.dot(lhs, tile_pair(slot), preferred_element_type=F32)
        total[table[SLOT_ROWS, slot]] += product[0:8] + product[8:16]
        return carry

    lax.fori_loop(0, SLOTS, body, 0, unroll=SLOTS)


def clamp_primal(values, free):
    floor = jnp.maximum(values, 0.0)
    return jnp.where(free > 0.5, floor, jnp.minimum(floor, 1.0))


def clamp_dual(values, ineq):
    return jnp.where(ineq > 0.5, jnp.maximum(values, 0.0), values)


def own_columns(table):
    index = table[AT_Y, 0] * 4 + table[AT_X, 0]
    return pl.ds(pl.multiple_of(index * COLS_SHARE, COLS_SHARE), COLS_SHARE)


def index_col(table):
    return table[AT_Z, 0] * 2 + table[AT_CORE, 0]


def sum_four(refs, rows):
    own, right, left, opposite = (ref[rows, :] for ref in refs)
    return (own + opposite) + (right + left)


def pack(
    count, rows, cols, row_kinds, rhs, dual, col_kinds, cost, primal, duals, side, places, kinds, start, done
):
    copies = [
        pltpu.make_async_copy(source, target, done.at[k])
        for k, (source, target) in enumerate(
            (
                (rows.at[0], places.at[0:1]),
                (cols.at[0], places.at[1:2]),
                (dual.at[0], start),
                (rhs.at[0], side.at[ROW_SIDE : ROW_SIDE + ROWS_SHARE]),
                (row_kinds.at[0], kinds.at[0:ROWS_SHARE]),
                (primal.at[0], side.at[0:COLS_SHARE]),
                (cost.at[0], side.at[COST:ROW_SIDE]),
                (col_kinds.at[0], kinds.at[COLS_SHARE : 2 * COLS_SHARE]),
            )
        )
    ]
    for copy in copies:
        copy.start()
    side[TABLE + COUNT :, :] = jnp.zeros((SIDE - TABLE - COUNT, TILE), F32)
    for k, value in (
        (COUNT, count[0, 0]),
        (AT_Y, lax.axis_index("y")),
        (AT_X, lax.axis_index("x")),
        (AT_Z, lax.axis_index("z")),
        (AT_CORE, lax.axis_index("core")),
    ):
        side[TABLE + k : TABLE + k + 1, :] = jnp.full((1, TILE), value, jnp.int32).astype(F32)
    side[TABLE : TABLE + COUNT, :] = jnp.zeros((COUNT, TILE), F32)
    for copy in copies:
        copy.wait()
    side[TABLE : TABLE + COUNT, 0:SLOTS] = places[...].astype(F32)
    side[COL_KINDS:COST, :] = kinds[COLS_SHARE:, :].astype(F32)
    side[ROW_SIDE + ROWS_SHARE : TABLE, :] = kinds[0:ROWS_SHARE, :].astype(F32)
    duals[...] = jnp.broadcast_to(start[...][None], duals.shape)


def turn(pairs, turned):
    for slot in range(SLOTS):
        for part in range(2):
            rows = slice(part * TILE, (part + 1) * TILE)
            turned[slot, rows, :] = pairs[slot, rows, :].T


def ring_sums(own, right, left, opposite, payload):
    four = (own, right, left, opposite)
    payload[0:COL_BLOCKS, :] = sum_four(four, slice(0, COL_BLOCKS))
    share = 2 * COLS_SHARE
    for k, ref in enumerate(four):
        first = COL_BLOCKS + k * share
        payload[first : first + share, :] = ref[COL_BLOCKS : COL_BLOCKS + share, :]


def sums(own, right, left, opposite, total):
    total[...] = sum_four((own, right, left, opposite), slice(None))


def image_copies(kept, received, side, copies):
    block = jnp.concatenate([kept[...] + received[...], side[ROW_SIDE:TABLE, :]], 0)
    copies[...] = jnp.broadcast_to(block[None], copies.shape)


def image_sums(pieces, held):
    held[0:HALF, :] = jnp.sum(pieces[:, 0:HALF, :], 0)
    for k in range(8):
        for j in range(2):
            first = HALF + j * ROWS_SHARE
            into = HALF * (1 + j) + k * ROWS_SHARE
            held[into : into + ROWS_SHARE, :] = pieces[k, first : first + ROWS_SHARE, :]


def pair_copies(kept, received, copies):
    both = kept[...] + received[...]
    for k in range(8):
        first = HALF + k * ROWS_SHARE
        copies[k, 0:HALF, :] = both[0:HALF]
        copies[k, HALF : HALF + 8, :] = jnp.concatenate(
            [both[first : first + ROWS_SHARE], jnp.zeros((8 - ROWS_SHARE, TILE), F32)], 0
        )


def pair_sums(pieces, held):
    held[...] = jnp.sum(pieces[...], 0)


def first_adjoint(
    tiles, duals, side, payload, dual, table_out, pairs, chunks, table, done, total
):
    copies, first = [], 0
    for k, slots in enumerate(PIECES):
        part = pl.ds(first, slots)
        copies.append(pltpu.make_async_copy(tiles.at[part], chunks.at[part], done.at[k]))
        copies[k].start()
        first += slots
    table_out[...] = side[TABLE:, :].astype(jnp.int32)
    read = pltpu.make_async_copy(table_out, table, done.at[len(PIECES)])
    read.start()
    for k in range(N):
        dual[k * ROWS_SHARE : (k + 1) * ROWS_SHARE, :] = duals[k]
    total[...] = jnp.zeros_like(total)
    payload[COL_BLOCKS:, :] = side[0:COST, :]
    read.wait()

    def tile_pair(slot):
        tile = jnp.where(slot < table[COUNT, 0], chunks[slot], 0.0)
        lead = tile.astype(BF16)
        pair = jnp.concatenate([lead, (tile - lead.astype(F32)).astype(BF16)], 0)
        pairs[slot] = pair
        return pair

    first = 0
    for k, slots in enumerate(PIECES):
        copies[k].wait()
        adjoint_slots(table, tile_pair, dual, total, first, slots)
        first += slots
    payload[0:COL_BLOCKS, :] = total[:, 0, :]
    mine = own_columns(table)
    payload[mine, :] += side[0:COLS_SHARE, :] * (1.0 / STEP) - side[COST:ROW_SIDE, :]


def first_forward(
    table, own, right, left, opposite, turned, kept, given, primal, start, free, extended, total
):
    y, x, second = table[AT_Y, 0], table[AT_X, 0], table[AT_CORE, 0] == 1
    for j, (ref, late) in enumerate(((own, 0), (right, 3), (left, 1), (opposite, 2))):
        for k, early in enumerate((0, 3, 1, 2)):
            to_y = (y + jnp.where(second, early, late)) & 3
            to_x = (x + jnp.where(second, late, early)) & 3
            device = to_y * 4 + to_x
            block = pl.ds(pl.multiple_of(device * COLS_SHARE, COLS_SHARE), COLS_SHARE)
            for m, out in enumerate((start, free)):
                first = COL_BLOCKS + (2 * k + m) * COLS_SHARE
                out[block, :] = ref[first : first + COLS_SHARE, :]
    ascent = sum_four((own, right, left, opposite), slice(0, COL_BLOCKS))
    primal[...] = clamp_primal(STEP * ascent, free[...])
    extended[...] = 2.0 * primal[...] - start[...]
    forward_product(table, lambda slot: turned[slot], [extended], total)
    mine = pl.multiple_of(table[AT_CORE, 0] * HALF, HALF)
    kept[...] = total[pl.ds(mine, HALF), 0, :]
    given[...] = total[pl.ds(HALF - mine, HALF), 0, :]


def second_adjoint(table, held, other, start, side, pairs, gradient, dual, rhs, ineq, image, total):
    first = table[AT_CORE, 0] == 0
    mine, theirs = held[...], other[...]
    for core, half in enumerate((jnp.where(first, mine, theirs), jnp.where(first, theirs, mine))):
        image[core * HALF : (core + 1) * HALF, :] = half[0:HALF]
        for k in range(8):
            block = slice((2 * k + core) * ROWS_SHARE, (2 * k + core + 1) * ROWS_SHARE)
            share = slice(k * ROWS_SHARE, (k + 1) * ROWS_SHARE)
            rhs[block, :] = half[HALF : 2 * HALF][share]
            ineq[block, :] = half[2 * HALF :][share]
    dual[...] = clamp_dual(start[...] + STEP * (rhs[...] - image[...]), ineq[...])
    adjoint_product(table, lambda slot: pairs[slot], dual, total)
    gradient[...] = total[:, 0, :]
    gradient[own_columns(table), :] -= side[COST:ROW_SIDE, :]


def second_forward(
    table, own, right, left, opposite, before, free, turned, kept, given, primal, ascent, primal_mine, extended, total
):
    ascent[...] = sum_four((own, right, left, opposite), slice(0, COL_BLOCKS))
    primal[...] = clamp_primal(before[...] + STEP * ascent[...], free[...])
    extended[...] = 2.0 * primal[...] - before[...]
    primal_mine[...] = primal[own_columns(table), :]
    forward_product(table, lambda slot: turned[slot], [extended, primal], total)
    mine = pl.multiple_of(table[AT_CORE, 0] * HALF, HALF)
    for k, part in enumerate((0, 4)):
        rows = slice(k * HALF, (k + 1) * HALF)
        kept[rows, :] = total[pl.ds(mine, HALF), part, :]
        given[rows, :] = total[pl.ds(HALF - mine, HALF), part, :]


def third_adjoint(
    table, held, other, before, rhs, ineq, side, primal1, primal2, pairs, payload, mine, dual, image, total
):
    half = pl.multiple_of(table[AT_CORE, 0] * HALF, HALF)
    image[pl.ds(half, HALF), :] = held[0:HALF, :]
    image[pl.ds(HALF - half, HALF), :] = other[0:HALF, :]
    dual[...] = clamp_dual(before[...] + STEP * (rhs[...] - image[...]), ineq[...])
    mine[...] = dual[pl.ds(index_col(table) * ROWS_SHARE, ROWS_SHARE), :]
    share = pl.ds(half + table[AT_Z, 0] * ROWS_SHARE, ROWS_SHARE)
    plain = held[HALF : HALF + ROWS_SHARE, :]
    bound, kind, last = rhs[share, :], ineq[share, :], dual[share, :]
    terms = []
    for product in (plain, 0.5 * (3.0 * plain - image[share, :])):
        residual = bound - product
        residual = jnp.where(kind > 0.5, jnp.maximum(residual, 0.0), residual)
        terms.append(jnp.sum(residual * residual, 0, keepdims=True))
    columns = own_columns(table)
    price, final = side[COST:ROW_SIDE, :], primal2[columns, :]
    for primal, value in (
        (final, last),
        (0.5 * (primal1[columns, :] + final), 0.5 * (before[share, :] + last)),
    ):
        gain = jnp.sum(price * primal, 0, keepdims=True)
        terms.append(gain - jnp.sum(bound * value, 0, keepdims=True))
    payload[COL_BLOCKS : COL_BLOCKS + 8, :] = jnp.concatenate(terms + terms, 0)
    adjoint_product(table, lambda slot: pairs[slot], dual, total)
    payload[0:COL_BLOCKS, :] = total[:, 0, :]
    payload[columns, :] -= price


def column_terms(own, right, left, opposite, earlier, free, terms):
    four = (own, right, left, opposite)
    ascent = sum_four(four, slice(0, COL_BLOCKS))
    row_terms = sum_four(four, slice(COL_BLOCKS, COL_BLOCKS + 8))
    kind = free[...]
    squares, gaps = [], []
    for k, reduced in enumerate((-ascent, -0.5 * (earlier[...] + ascent))):
        low = jnp.minimum(reduced, 0.0)
        violation = jnp.where(kind > 0.5, low, 0.0)
        box = jnp.where(kind > 0.5, 0.0, low)
        squares.append(jnp.sum(violation * violation, 0, keepdims=True))
        gaps.append(row_terms[2 + k : 3 + k] - jnp.sum(box, 0, keepdims=True))
    rows = jnp.concatenate([row_terms[0:2]] + squares + gaps + squares, 0)
    sums = jnp.broadcast_to(jnp.sum(rows, 1, keepdims=True), rows.shape)
    places = [lax.broadcasted_iota(jnp.int32, rows.shape, k) for k in range(2)]
    line = jnp.sum(jnp.where(places[0] == places[1], sums, 0.0), 0, keepdims=True)
    terms[...] = jnp.broadcast_to(line[None], terms.shape)


def measures(gathered, primal_residual, dual_residual, gap):
    line = jnp.sum(gathered[...], 0)
    lane = lax.broadcasted_iota(jnp.int32, line.shape, 1)
    for k, (out, size) in enumerate(
        ((primal_residual, NROWS), (dual_residual, NCOLS), (gap, NCOLS))
    ):
        for j in range(2):
            out[j] = jnp.sum(jnp.where(lane == 2 * k + j, line, 0.0)) * (1.0 / size)


def shift(values, phase, step):
    pairs = []
    for y in range(4):
        for x in range(4):
            for core in range(2):
                to_y, to_x = (y, (x + step) % 4) if core == phase else ((y + step) % 4, x)
                pairs.append(((y * 4 + x) * 2 + core, (to_y * 4 + to_x) * 2 + core))
    return lax.ppermute(values, ("y", "x", "core"), pairs)


def four_of(values, phase):
    return values, shift(values, phase, 1), shift(values, phase, -1), shift(values, phase, 2)


def four_over_row(values):
    total = call(sums, "sums", [(values.shape, F32)], four_of(values, 0))
    return four_of(total[0], 1)


def swap_cores(values):
    return lax.ppermute(values, "core", [(0, 1), (1, 0)])


def exchange(copies, axes):
    return lax.all_to_all(copies, axes, 0, 0)


def shards(
    tiles, tile_rows, tile_cols, tile_count, row_types, var_types, rhs, cost, primal_start, dual_start
):
    tiles = tiles.reshape(SLOTS, TILE, TILE)
    blocks, columns, half = (ROW_BLOCKS, TILE), (COL_BLOCKS, TILE), (HALF, TILE)
    row_total = [pltpu.VMEM((ROW_BLOCKS, 8, TILE), F32)]
    col_total = [pltpu.VMEM((COL_BLOCKS, 8, TILE), F32)]

    duals, side = call(
        pack,
        "pack",
        [((N, ROWS_SHARE, TILE), F32), ((SIDE, TILE), F32)],
        (tile_count, tile_rows, tile_cols, row_types, rhs, dual_start, var_types, cost, primal_start),
        smem=1,
        hbm=8,
        scratch=[
            pltpu.VMEM((2, SLOTS), jnp.int32),
            pltpu.VMEM((2 * COLS_SHARE, TILE), jnp.int32),
            pltpu.VMEM((ROWS_SHARE, TILE), F32),
            pltpu.SemaphoreType.DMA((8,)),
        ],
        vmem=PACK_VMEM,
    )

    payload, dual0, table, pairs = call(
        first_adjoint,
        "first_adjoint",
        [
            ((COL_BLOCKS + 2 * COLS_SHARE, TILE), F32),
            (blocks, F32),
            ((8, TILE), jnp.int32),
            ((SLOTS, 2 * TILE, TILE), BF16),
        ],
        (tiles, exchange(duals, ("z", "core")), side),
        hbm=1,
        scratch=[
            pltpu.VMEM((SLOTS, TILE, TILE), F32),
            pltpu.SMEM((8, TILE), jnp.int32),
            pltpu.SemaphoreType.DMA((len(PIECES) + 1,)),
        ]
        + col_total,
        vmem=FIRST_VMEM,
    )
    turned = call(
        turn,
        "turn",
        [((SLOTS, 2 * TILE, TILE), BF16)],
        (pairs,),
        cost=pl.CostEstimate(flops=0, bytes_accessed=2**23, transcendentals=0),
    )[0]
    payload = call(
        ring_sums, "ring_sums", [((COL_BLOCKS + 8 * COLS_SHARE, TILE), F32)], four_of(payload, 0)
    )

    kept, given, primal1, _, free = call(
        first_forward,
        "first_forward",
        [(half, F32)] * 2 + [(columns, F32)] * 3,
        (table, *four_of(payload[0], 1), turned),
        smem=1,
        scratch=[pltpu.VMEM(columns, F32)] + row_total,
    )
    copies = call(
        image_copies,
        "image_copies",
        [((8, HALF + 2 * ROWS_SHARE, TILE), F32)],
        (kept, swap_cores(given), side),
    )
    held = call(
        image_sums, "image_sums", [((3 * HALF, TILE), F32)], (exchange(copies[0], "z"),)
    )[0]

    gradient, dual1, rhs_full, ineq = call(
        second_adjoint,
        "second_adjoint",
        [(columns, F32)] + [(blocks, F32)] * 3,
        (table, held, swap_cores(held), dual0, side, pairs),
        smem=1,
        scratch=[pltpu.VMEM(blocks, F32)] + col_total,
    )

    kept, given, primal2, ascent2, primal_mine = call(
        second_forward,
        "second_forward",
        [(blocks, F32)] * 2 + [(columns, F32)] * 2 + [((COLS_SHARE, TILE), F32)],
        (table, *four_over_row(gradient), primal1, free, turned),
        smem=1,
        scratch=[pltpu.VMEM(columns, F32)] + row_total,
    )
    copies = call(
        pair_copies, "pair_copies", [((8, HALF + 8, TILE), F32)], (kept, swap_cores(given))
    )
    held = call(pair_sums, "pair_sums", [((HALF + 8, TILE), F32)], (exchange(copies[0], "z"),))[0]

    payload, dual_mine = call(
        third_adjoint,
        "third_adjoint",
        [((COL_BLOCKS + 8, TILE), F32), ((ROWS_SHARE, TILE), F32)],
        (table, held, swap_cores(held), dual1, rhs_full, ineq, side, primal1, primal2, pairs),
        smem=1,
        scratch=[pltpu.VMEM(blocks, F32)] * 2 + col_total,
    )
    terms = call(
        column_terms,
        "column_terms",
        [((N, 1, TILE), F32)],
        (*four_over_row(payload), ascent2, free),
    )
    primal_residual, dual_residual, gap = call(
        measures,
        "measures",
        [((2,), F32)] * 3,
        (exchange(terms[0], ("z", "core")),),
        smem_out=True,
    )
    return primal_mine[None], dual_mine[None], primal_residual, dual_residual, gap


def solution(mesh):
    rings = Mesh(mesh.devices.reshape(4, 4, 8, 2), ("y", "x", "z", "core"))
    row, col = ("y", "x"), ("z", "core")
    in_specs = (
        P(row, col, None, None, None),
        P(row, col, None),
        P(row, col, None),
        P(row, col),
        P(row, col, None),
        P(col, row, None),
        P(row, col, None),
        P(col, row, None),
        P(col, row, None),
        P(row, col, None),
    )
    out_specs = (P(col, row, None), P(row, col, None), P(), P(), P())
    return jax.shard_map(shards, mesh=rings, in_specs=in_specs, out_specs=out_specs, check_vma=False)
```

```python
import jax
import jax.numpy as jnp
from jax import lax
from jax.experimental import pallas as pl
from jax.experimental.pallas import tpu as pltpu
from jax.sharding import Mesh
from jax.sharding import PartitionSpec as P

N = 16
TILE = 128
ROW_BLOCKS = 64
COL_BLOCKS = 128
SLOTS = 64
ROWS_SHARE = ROW_BLOCKS // N
COLS_SHARE = COL_BLOCKS // N
HALF = ROW_BLOCKS // 2
NROWS = float(N * ROW_BLOCKS * TILE)
NCOLS = float(N * COL_BLOCKS * TILE)
PACK_VMEM = 60 * 2**20
FIRST_VMEM = 48 * 2**20
PIECES = (8, 16, 16, 16, 8)
F32, BF16 = jnp.float32, jnp.bfloat16

SLOT_ROWS, SLOT_COLS, COUNT, AT_Y, AT_X, AT_Z, AT_CORE = range(7)
COL_KINDS, COST, ROW_SIDE, TABLE, SIDE = 8, 16, 24, 32, 40
HANDED = 12288
STEP = 0.4

VMEM = pl.BlockSpec(memory_space=pltpu.VMEM)
SMEM = pl.BlockSpec(memory_space=pltpu.SMEM)
HBM = pl.BlockSpec(memory_space=pltpu.HBM)


def call(kernel, name, out_shapes, args, smem=0, hbm=0, smem_out=False, hbm_out=(), scratch=(), vmem=8 * 2**20, cost=None):
    shapes = tuple(jax.ShapeDtypeStruct(s, d) for s, d in out_shapes)
    return pl.pallas_call(
        kernel,
        name=name,
        out_shape=shapes,
        in_specs=[SMEM] * smem + [HBM] * hbm + [VMEM] * (len(args) - smem - hbm),
        out_specs=tuple(
            HBM if k in hbm_out else SMEM if smem_out else VMEM for k in range(len(shapes))
        ),
        scratch_shapes=list(scratch),
        compiler_params=pltpu.CompilerParams(vmem_limit_bytes=vmem),
        cost_estimate=cost,
    )(*args)


def split(vector, copies):
    wide = jnp.broadcast_to(vector, (copies, TILE))
    lead = wide.astype(BF16).astype(F32)
    return [lead, wide - lead]


def adjoint_product(table, tile_pair, dual_ref, total):
    total[...] = jnp.zeros_like(total)
    adjoint_slots(table, tile_pair, dual_ref, total, 0, SLOTS)


def adjoint_slots(table, tile_pair, dual_ref, total, first, slots):
    def body(slot, carry):
        lhs = jnp.concatenate(split(dual_ref[pl.ds(table[SLOT_ROWS, slot], 1), :], 8), 0).astype(BF16)
        lhs = jnp.concatenate([lhs, lhs], 1)
        product = jnp.dot(lhs, tile_pair(slot), preferred_element_type=F32)
        total[table[SLOT_COLS, slot]] += product[0:8] + product[8:16]
        return carry

    lax.fori_loop(first, first + slots, body, 0, unroll=slots)


def forward_product(table, tile_pair, primal_refs, total):
    total[...] = jnp.zeros_like(total)
    copies = 8 // len(primal_refs)

    def body(slot, carry):
        parts = [split(ref[pl.ds(table[SLOT_COLS, slot], 1), :], copies) for ref in primal_refs]
        lhs = jnp.concatenate([p[0] for p in parts] + [p[1] for p in parts], 0).astype(BF16)
        lhs = jnp.concatenate([lhs, lhs], 1)
        product = jnp.dot(lhs, tile_pair(slot), preferred_element_type=F32)
        total[table[SLOT_ROWS, slot]] += product[0:8] + product[8:16]
        return carry

    lax.fori_loop(0, SLOTS, body, 0, unroll=SLOTS)


def clamp_primal(values, free):
    floor = jnp.maximum(values, 0.0)
    return jnp.where(free > 0.5, floor, jnp.minimum(floor, 1.0))


def clamp_dual(values, ineq):
    return jnp.where(ineq > 0.5, jnp.maximum(values, 0.0), values)


def own_columns(table):
    index = table[AT_Y, 0] * 4 + table[AT_X, 0]
    return pl.ds(pl.multiple_of(index * COLS_SHARE, COLS_SHARE), COLS_SHARE)


def index_col(table):
    return table[AT_Z, 0] * 2 + table[AT_CORE, 0]


def sum_four(refs, rows):
    own, right, left, opposite = (ref[rows, :] for ref in refs)
    return (own + opposite) + (right + left)


def pack(
    count, rows, cols, row_kinds, rhs, dual, col_kinds, cost, primal, duals, handed, side, places, kinds, start, done
):
    copies = [
        pltpu.make_async_copy(source, target, done.at[k])
        for k, (source, target) in enumerate(
            (
                (rows.at[0], places.at[0:1]),
                (cols.at[0], places.at[1:2]),
                (dual.at[0], start),
                (rhs.at[0], side.at[ROW_SIDE : ROW_SIDE + ROWS_SHARE]),
                (row_kinds.at[0], kinds.at[0:ROWS_SHARE]),
                (primal.at[0], side.at[0:COLS_SHARE]),
                (cost.at[0], side.at[COST:ROW_SIDE]),
                (col_kinds.at[0], kinds.at[COLS_SHARE : 2 * COLS_SHARE]),
            )
        )
    ]
    for copy in copies:
        copy.start()
    side[TABLE + COUNT :, :] = jnp.zeros((SIDE - TABLE - COUNT, TILE), F32)
    for k, value in (
        (COUNT, count[0, 0]),
        (AT_Y, lax.axis_index("y")),
        (AT_X, lax.axis_index("x")),
        (AT_Z, lax.axis_index("z")),
        (AT_CORE, lax.axis_index("core")),
    ):
        side[TABLE + k : TABLE + k + 1, :] = jnp.full((1, TILE), value, jnp.int32).astype(F32)
    side[TABLE : TABLE + COUNT, :] = jnp.zeros((COUNT, TILE), F32)
    for copy in copies:
        copy.wait()
    side[TABLE : TABLE + COUNT, 0:SLOTS] = places[...].astype(F32)
    side[COL_KINDS:COST, :] = kinds[COLS_SHARE:, :].astype(F32)
    side[ROW_SIDE + ROWS_SHARE : TABLE, :] = kinds[0:ROWS_SHARE, :].astype(F32)
    hand = pltpu.make_async_copy(side, handed.at[0:SIDE], done.at[8])
    hand.start()
    duals[...] = jnp.broadcast_to(start[...][None], duals.shape)
    hand.wait()


def turn(pairs, turned):
    for slot in range(SLOTS):
        for part in range(2):
            rows = slice(part * TILE, (part + 1) * TILE)
            turned[slot, rows, :] = pairs[slot, rows, :].T


def ring_sums(own, right, left, opposite, payload):
    four = (own, right, left, opposite)
    payload[0:COL_BLOCKS, :] = sum_four(four, slice(0, COL_BLOCKS))
    share = 2 * COLS_SHARE
    for k, ref in enumerate(four):
        first = COL_BLOCKS + k * share
        payload[first : first + share, :] = ref[COL_BLOCKS : COL_BLOCKS + share, :]


def sums(own, right, left, opposite, total):
    total[...] = sum_four((own, right, left, opposite), slice(None))


def image_copies(kept, received, side, copies):
    block = jnp.concatenate([kept[...] + received[...], side[ROW_SIDE:TABLE, :]], 0)
    copies[...] = jnp.broadcast_to(block[None], copies.shape)


def image_sums(pieces, held):
    held[0:HALF, :] = jnp.sum(pieces[:, 0:HALF, :], 0)
    for k in range(8):
        for j in range(2):
            first = HALF + j * ROWS_SHARE
            into = HALF * (1 + j) + k * ROWS_SHARE
            held[into : into + ROWS_SHARE, :] = pieces[k, first : first + ROWS_SHARE, :]


def pair_copies(kept, received, copies):
    both = kept[...] + received[...]
    for k in range(8):
        first = HALF + k * ROWS_SHARE
        copies[k, 0:HALF, :] = both[0:HALF]
        copies[k, HALF : HALF + 8, :] = jnp.concatenate(
            [both[first : first + ROWS_SHARE], jnp.zeros((8 - ROWS_SHARE, TILE), F32)], 0
        )


def pair_sums(pieces, held):
    held[...] = jnp.sum(pieces[...], 0)


def first_adjoint(
    tiles, handed, duals, payload, dual, side, table_out, pairs, chunks, table, done, total
):
    share = pltpu.make_async_copy(handed.at[0:SIDE], side, done.at[len(PIECES) + 1])
    share.start()
    copies, first = [], 0
    for k, slots in enumerate(PIECES):
        part = pl.ds(first, slots)
        copies.append(pltpu.make_async_copy(tiles.at[part], chunks.at[part], done.at[k]))
        copies[k].start()
        first += slots
    for k in range(N):
        dual[k * ROWS_SHARE : (k + 1) * ROWS_SHARE, :] = duals[k]
    total[...] = jnp.zeros_like(total)
    share.wait()
    table_out[...] = side[TABLE:, :].astype(jnp.int32)
    read = pltpu.make_async_copy(table_out, table, done.at[len(PIECES)])
    read.start()
    payload[COL_BLOCKS:, :] = side[0:COST, :]
    read.wait()

    def tile_pair(slot):
        tile = jnp.where(slot < table[COUNT, 0], chunks[slot], 0.0)
        lead = tile.astype(BF16)
        pair = jnp.concatenate([lead, (tile - lead.astype(F32)).astype(BF16)], 0)
        pairs[slot] = pair
        return pair

    first = 0
    for k, slots in enumerate(PIECES):
        copies[k].wait()
        adjoint_slots(table, tile_pair, dual, total, first, slots)
        first += slots
    payload[0:COL_BLOCKS, :] = total[:, 0, :]
    mine = own_columns(table)
    payload[mine, :] += side[0:COLS_SHARE, :] * (1.0 / STEP) - side[COST:ROW_SIDE, :]


def first_forward(
    table, own, right, left, opposite, turned, kept, given, primal, start, free, extended, total
):
    y, x, second = table[AT_Y, 0], table[AT_X, 0], table[AT_CORE, 0] == 1
    for j, (ref, late) in enumerate(((own, 0), (right, 3), (left, 1), (opposite, 2))):
        for k, early in enumerate((0, 3, 1, 2)):
            to_y = (y + jnp.where(second, early, late)) & 3
            to_x = (x + jnp.where(second, late, early)) & 3
            device = to_y * 4 + to_x
            block = pl.ds(pl.multiple_of(device * COLS_SHARE, COLS_SHARE), COLS_SHARE)
            for m, out in enumerate((start, free)):
                first = COL_BLOCKS + (2 * k + m) * COLS_SHARE
                out[block, :] = ref[first : first + COLS_SHARE, :]
    ascent = sum_four((own, right, left, opposite), slice(0, COL_BLOCKS))
    primal[...] = clamp_primal(STEP * ascent, free[...])
    extended[...] = 2.0 * primal[...] - start[...]
    forward_product(table, lambda slot: turned[slot], [extended], total)
    mine = pl.multiple_of(table[AT_CORE, 0] * HALF, HALF)
    kept[...] = total[pl.ds(mine, HALF), 0, :]
    given[...] = total[pl.ds(HALF - mine, HALF), 0, :]


def second_adjoint(table, held, other, start, side, pairs, gradient, dual, rhs, ineq, image, total):
    first = table[AT_CORE, 0] == 0
    mine, theirs = held[...], other[...]
    for core, half in enumerate((jnp.where(first, mine, theirs), jnp.where(first, theirs, mine))):
        image[core * HALF : (core + 1) * HALF, :] = half[0:HALF]
        for k in range(8):
            block = slice((2 * k + core) * ROWS_SHARE, (2 * k + core + 1) * ROWS_SHARE)
            share = slice(k * ROWS_SHARE, (k + 1) * ROWS_SHARE)
            rhs[block, :] = half[HALF : 2 * HALF][share]
            ineq[block, :] = half[2 * HALF :][share]
    dual[...] = clamp_dual(start[...] + STEP * (rhs[...] - image[...]), ineq[...])
    adjoint_product(table, lambda slot: pairs[slot], dual, total)
    gradient[...] = total[:, 0, :]
    gradient[own_columns(table), :] -= side[COST:ROW_SIDE, :]


def second_forward(
    table, own, right, left, opposite, before, free, turned, kept, given, primal, ascent, primal_mine, extended, total
):
    ascent[...] = sum_four((own, right, left, opposite), slice(0, COL_BLOCKS))
    primal[...] = clamp_primal(before[...] + STEP * ascent[...], free[...])
    extended[...] = 2.0 * primal[...] - before[...]
    primal_mine[...] = primal[own_columns(table), :]
    forward_product(table, lambda slot: turned[slot], [extended, primal], total)
    mine = pl.multiple_of(table[AT_CORE, 0] * HALF, HALF)
    for k, part in enumerate((0, 4)):
        rows = slice(k * HALF, (k + 1) * HALF)
        kept[rows, :] = total[pl.ds(mine, HALF), part, :]
        given[rows, :] = total[pl.ds(HALF - mine, HALF), part, :]


def row_terms(table, held, before, rhs, ineq, side, primal1, primal2, terms):
    offset = table[AT_Z, 0] * ROWS_SHARE
    share = pl.ds(table[AT_CORE, 0] * HALF + offset, ROWS_SHARE)
    image, plain = held[pl.ds(offset, ROWS_SHARE), :], held[HALF : HALF + ROWS_SHARE, :]
    earlier, bound, kind = before[share, :], rhs[share, :], ineq[share, :]
    last = clamp_dual(earlier + STEP * (bound - image), kind)
    rows = []
    for product in (plain, 0.5 * (3.0 * plain - image)):
        residual = bound - product
        residual = jnp.where(kind > 0.5, jnp.maximum(residual, 0.0), residual)
        rows.append(jnp.sum(residual * residual, 0, keepdims=True))
    columns = own_columns(table)
    price, final = side[COST:ROW_SIDE, :], primal2[columns, :]
    for primal, value in (
        (final, last),
        (0.5 * (primal1[columns, :] + final), 0.5 * (earlier + last)),
    ):
        gain = jnp.sum(price * primal, 0, keepdims=True)
        rows.append(gain - jnp.sum(bound * value, 0, keepdims=True))
    terms[...] = jnp.concatenate(rows + rows, 0)


def third_adjoint(
    table, held, other, before, rhs, ineq, side, terms, pairs, payload, mine, dual, image, total
):
    half = pl.multiple_of(table[AT_CORE, 0] * HALF, HALF)
    image[pl.ds(half, HALF), :] = held[0:HALF, :]
    image[pl.ds(HALF - half, HALF), :] = other[0:HALF, :]
    dual[...] = clamp_dual(before[...] + STEP * (rhs[...] - image[...]), ineq[...])
    mine[...] = dual[pl.ds(index_col(table) * ROWS_SHARE, ROWS_SHARE), :]
    adjoint_product(table, lambda slot: pairs[slot], dual, total)
    payload[0:COL_BLOCKS, :] = total[:, 0, :]
    payload[COL_BLOCKS : COL_BLOCKS + 8, :] = terms[...]
    payload[own_columns(table), :] -= side[COST:ROW_SIDE, :]


def column_terms(own, right, left, opposite, earlier, free, terms):
    four = (own, right, left, opposite)
    ascent = sum_four(four, slice(0, COL_BLOCKS))
    row_terms = sum_four(four, slice(COL_BLOCKS, COL_BLOCKS + 8))
    kind = free[...]
    squares, gaps = [], []
    for k, reduced in enumerate((-ascent, -0.5 * (earlier[...] + ascent))):
        low = jnp.minimum(reduced, 0.0)
        violation = jnp.where(kind > 0.5, low, 0.0)
        box = jnp.where(kind > 0.5, 0.0, low)
        squares.append(jnp.sum(violation * violation, 0, keepdims=True))
        gaps.append(row_terms[2 + k : 3 + k] - jnp.sum(box, 0, keepdims=True))
    rows = jnp.concatenate([row_terms[0:2]] + squares + gaps + squares, 0)
    sums = jnp.broadcast_to(jnp.sum(rows, 1, keepdims=True), rows.shape)
    places = [lax.broadcasted_iota(jnp.int32, rows.shape, k) for k in range(2)]
    line = jnp.sum(jnp.where(places[0] == places[1], sums, 0.0), 0, keepdims=True)
    terms[...] = jnp.broadcast_to(line[None], terms.shape)


def measures(gathered, primal_residual, dual_residual, gap):
    line = jnp.sum(gathered[...], 0)
    lane = lax.broadcasted_iota(jnp.int32, line.shape, 1)
    for k, (out, size) in enumerate(
        ((primal_residual, NROWS), (dual_residual, NCOLS), (gap, NCOLS))
    ):
        for j in range(2):
            out[j] = jnp.sum(jnp.where(lane == 2 * k + j, line, 0.0)) * (1.0 / size)


def shift(values, phase, step):
    pairs = []
    for y in range(4):
        for x in range(4):
            for core in range(2):
                to_y, to_x = (y, (x + step) % 4) if core == phase else ((y + step) % 4, x)
                pairs.append(((y * 4 + x) * 2 + core, (to_y * 4 + to_x) * 2 + core))
    return lax.ppermute(values, ("y", "x", "core"), pairs)


def four_of(values, phase):
    return values, shift(values, phase, 1), shift(values, phase, -1), shift(values, phase, 2)


def four_over_row(values):
    total = call(sums, "sums", [(values.shape, F32)], four_of(values, 0))
    return four_of(total[0], 1)


def swap_cores(values):
    return lax.ppermute(values, "core", [(0, 1), (1, 0)])


def exchange(copies, axes):
    return lax.all_to_all(copies, axes, 0, 0)


def shards(
    tiles, tile_rows, tile_cols, tile_count, row_types, var_types, rhs, cost, primal_start, dual_start
):
    tiles = tiles.reshape(SLOTS, TILE, TILE)
    blocks, columns, half = (ROW_BLOCKS, TILE), (COL_BLOCKS, TILE), (HALF, TILE)
    row_total = [pltpu.VMEM((ROW_BLOCKS, 8, TILE), F32)]
    col_total = [pltpu.VMEM((COL_BLOCKS, 8, TILE), F32)]

    duals, handed = call(
        pack,
        "pack",
        [((N, ROWS_SHARE, TILE), F32), ((HANDED, TILE), F32)],
        (tile_count, tile_rows, tile_cols, row_types, rhs, dual_start, var_types, cost, primal_start),
        smem=1,
        hbm=8,
        hbm_out=(1,),
        scratch=[
            pltpu.VMEM((SIDE, TILE), F32),
            pltpu.VMEM((2, SLOTS), jnp.int32),
            pltpu.VMEM((2 * COLS_SHARE, TILE), jnp.int32),
            pltpu.VMEM((ROWS_SHARE, TILE), F32),
            pltpu.SemaphoreType.DMA((9,)),
        ],
        vmem=PACK_VMEM,
    )

    payload, dual0, side, table, pairs = call(
        first_adjoint,
        "first_adjoint",
        [
            ((COL_BLOCKS + 2 * COLS_SHARE, TILE), F32),
            (blocks, F32),
            ((SIDE, TILE), F32),
            ((8, TILE), jnp.int32),
            ((SLOTS, 2 * TILE, TILE), BF16),
        ],
        (tiles, handed, exchange(duals, ("z", "core"))),
        hbm=2,
        scratch=[
            pltpu.VMEM((SLOTS, TILE, TILE), F32),
            pltpu.SMEM((8, TILE), jnp.int32),
            pltpu.SemaphoreType.DMA((len(PIECES) + 2,)),
        ]
        + col_total,
        vmem=FIRST_VMEM,
    )
    turned = call(
        turn,
        "turn",
        [((SLOTS, 2 * TILE, TILE), BF16)],
        (pairs,),
        cost=pl.CostEstimate(flops=0, bytes_accessed=2**23, transcendentals=0),
    )[0]
    payload = call(
        ring_sums, "ring_sums", [((COL_BLOCKS + 8 * COLS_SHARE, TILE), F32)], four_of(payload, 0)
    )

    kept, given, primal1, _, free = call(
        first_forward,
        "first_forward",
        [(half, F32)] * 2 + [(columns, F32)] * 3,
        (table, *four_of(payload[0], 1), turned),
        smem=1,
        scratch=[pltpu.VMEM(columns, F32)] + row_total,
    )
    copies = call(
        image_copies,
        "image_copies",
        [((8, HALF + 2 * ROWS_SHARE, TILE), F32)],
        (kept, swap_cores(given), side),
    )
    held = call(
        image_sums, "image_sums", [((3 * HALF, TILE), F32)], (exchange(copies[0], "z"),)
    )[0]

    gradient, dual1, rhs_full, ineq = call(
        second_adjoint,
        "second_adjoint",
        [(columns, F32)] + [(blocks, F32)] * 3,
        (table, held, swap_cores(held), dual0, side, pairs),
        smem=1,
        scratch=[pltpu.VMEM(blocks, F32)] + col_total,
    )

    kept, given, primal2, ascent2, primal_mine = call(
        second_forward,
        "second_forward",
        [(blocks, F32)] * 2 + [(columns, F32)] * 2 + [((COLS_SHARE, TILE), F32)],
        (table, *four_over_row(gradient), primal1, free, turned),
        smem=1,
        scratch=[pltpu.VMEM(columns, F32)] + row_total,
    )
    copies = call(
        pair_copies, "pair_copies", [((8, HALF + 8, TILE), F32)], (kept, swap_cores(given))
    )
    held = call(pair_sums, "pair_sums", [((HALF + 8, TILE), F32)], (exchange(copies[0], "z"),))[0]
    other = swap_cores(held)
    terms = call(
        row_terms,
        "row_terms",
        [((8, TILE), F32)],
        (table, held, dual1, rhs_full, ineq, side, primal1, primal2),
        smem=1,
        cost=pl.CostEstimate(flops=0, bytes_accessed=2**21, transcendentals=0),
    )[0]

    payload, dual_mine = call(
        third_adjoint,
        "third_adjoint",
        [((COL_BLOCKS + 8, TILE), F32), ((ROWS_SHARE, TILE), F32)],
        (table, held, other, dual1, rhs_full, ineq, side, terms, pairs),
        smem=1,
        scratch=[pltpu.VMEM(blocks, F32)] * 2 + col_total,
    )
    terms = call(
        column_terms,
        "column_terms",
        [((N, 1, TILE), F32)],
        (*four_over_row(payload), ascent2, free),
    )
    primal_residual, dual_residual, gap = call(
        measures,
        "measures",
        [((2,), F32)] * 3,
        (exchange(terms[0], ("z", "core")),),
        smem_out=True,
    )
    return primal_mine[None], dual_mine[None], primal_residual, dual_residual, gap


def solution(mesh):
    rings = Mesh(mesh.devices.reshape(4, 4, 8, 2), ("y", "x", "z", "core"))
    row, col = ("y", "x"), ("z", "core")
    in_specs = (
        P(row, col, None, None, None),
        P(row, col, None),
        P(row, col, None),
        P(row, col),
        P(row, col, None),
        P(col, row, None),
        P(row, col, None),
        P(col, row, None),
        P(col, row, None),
        P(row, col, None),
    )
    out_specs = (P(col, row, None), P(row, col, None), P(), P(), P())
    return jax.shard_map(shards, mesh=rings, in_specs=in_specs, out_specs=out_specs, check_vma=False)
```

```python
import jax
import jax.numpy as jnp
from jax import lax
from jax.experimental import pallas as pl
from jax.experimental.pallas import tpu as pltpu
from jax.sharding import Mesh
from jax.sharding import PartitionSpec as P

N = 16
TILE = 128
ROW_BLOCKS = 64
COL_BLOCKS = 128
SLOTS = 64
ROWS_SHARE = ROW_BLOCKS // N
COLS_SHARE = COL_BLOCKS // N
HALF = ROW_BLOCKS // 2
NROWS = float(N * ROW_BLOCKS * TILE)
NCOLS = float(N * COL_BLOCKS * TILE)
PACK_VMEM = 60 * 2**20
FIRST_VMEM = 48 * 2**20
PIECES = (8, 16, 16, 16, 8)
F32, BF16 = jnp.float32, jnp.bfloat16

SLOT_ROWS, SLOT_COLS, COUNT, AT_Y, AT_X, AT_Z, AT_CORE = range(7)
COL_KINDS, COST, ROW_SIDE, TABLE, SIDE = 8, 16, 24, 32, 40
STEP = 0.4

VMEM = pl.BlockSpec(memory_space=pltpu.VMEM)
SMEM = pl.BlockSpec(memory_space=pltpu.SMEM)
HBM = pl.BlockSpec(memory_space=pltpu.HBM)


def call(kernel, name, out_shapes, args, smem=0, hbm=0, smem_out=False, hbm_out=(), scratch=(), vmem=8 * 2**20, cost=None):
    shapes = tuple(jax.ShapeDtypeStruct(s, d) for s, d in out_shapes)
    return pl.pallas_call(
        kernel,
        name=name,
        out_shape=shapes,
        in_specs=[SMEM] * smem + [HBM] * hbm + [VMEM] * (len(args) - smem - hbm),
        out_specs=tuple(
            HBM if k in hbm_out else SMEM if smem_out else VMEM for k in range(len(shapes))
        ),
        scratch_shapes=list(scratch),
        compiler_params=pltpu.CompilerParams(vmem_limit_bytes=vmem),
        cost_estimate=cost,
    )(*args)


def split(vector, copies):
    wide = jnp.broadcast_to(vector, (copies, TILE))
    lead = wide.astype(BF16).astype(F32)
    return [lead, wide - lead]


def adjoint_product(table, tile_pair, dual_ref, total):
    total[...] = jnp.zeros_like(total)
    adjoint_slots(table, tile_pair, dual_ref, total, 0, SLOTS)


def adjoint_slots(table, tile_pair, dual_ref, total, first, slots):
    def body(slot, carry):
        lhs = jnp.concatenate(split(dual_ref[pl.ds(table[SLOT_ROWS, slot], 1), :], 8), 0).astype(BF16)
        lhs = jnp.concatenate([lhs, lhs], 1)
        product = jnp.dot(lhs, tile_pair(slot), preferred_element_type=F32)
        total[table[SLOT_COLS, slot]] += product[0:8] + product[8:16]
        return carry

    lax.fori_loop(first, first + slots, body, 0, unroll=slots)


def forward_product(table, tile_pair, primal_refs, total):
    total[...] = jnp.zeros_like(total)
    copies = 8 // len(primal_refs)

    def body(slot, carry):
        parts = [split(ref[pl.ds(table[SLOT_COLS, slot], 1), :], copies) for ref in primal_refs]
        lhs = jnp.concatenate([p[0] for p in parts] + [p[1] for p in parts], 0).astype(BF16)
        lhs = jnp.concatenate([lhs, lhs], 1)
        product = jnp.dot(lhs, tile_pair(slot), preferred_element_type=F32)
        total[table[SLOT_ROWS, slot]] += product[0:8] + product[8:16]
        return carry

    lax.fori_loop(0, SLOTS, body, 0, unroll=SLOTS)


def clamp_primal(values, free):
    floor = jnp.maximum(values, 0.0)
    return jnp.where(free > 0.5, floor, jnp.minimum(floor, 1.0))


def clamp_dual(values, ineq):
    return jnp.where(ineq > 0.5, jnp.maximum(values, 0.0), values)


def own_columns(table):
    index = table[AT_Y, 0] * 4 + table[AT_X, 0]
    return pl.ds(pl.multiple_of(index * COLS_SHARE, COLS_SHARE), COLS_SHARE)


def index_col(table):
    return table[AT_Z, 0] * 2 + table[AT_CORE, 0]


def sum_four(refs, rows):
    own, right, left, opposite = (ref[rows, :] for ref in refs)
    return (own + opposite) + (right + left)


def pack(
    count, rows, cols, row_kinds, rhs, dual, col_kinds, cost, primal, duals, side, places, kinds, start, done
):
    copies = [
        pltpu.make_async_copy(source, target, done.at[k])
        for k, (source, target) in enumerate(
            (
                (rows.at[0], places.at[0:1]),
                (cols.at[0], places.at[1:2]),
                (dual.at[0], start),
                (rhs.at[0], side.at[ROW_SIDE : ROW_SIDE + ROWS_SHARE]),
                (row_kinds.at[0], kinds.at[0:ROWS_SHARE]),
                (primal.at[0], side.at[0:COLS_SHARE]),
                (cost.at[0], side.at[COST:ROW_SIDE]),
                (col_kinds.at[0], kinds.at[COLS_SHARE : 2 * COLS_SHARE]),
            )
        )
    ]
    for copy in copies:
        copy.start()
    side[TABLE + COUNT :, :] = jnp.zeros((SIDE - TABLE - COUNT, TILE), F32)
    for k, value in (
        (COUNT, count[0, 0]),
        (AT_Y, lax.axis_index("y")),
        (AT_X, lax.axis_index("x")),
        (AT_Z, lax.axis_index("z")),
        (AT_CORE, lax.axis_index("core")),
    ):
        side[TABLE + k : TABLE + k + 1, :] = jnp.full((1, TILE), value, jnp.int32).astype(F32)
    side[TABLE : TABLE + COUNT, :] = jnp.zeros((COUNT, TILE), F32)
    for copy in copies:
        copy.wait()
    side[TABLE : TABLE + COUNT, 0:SLOTS] = places[...].astype(F32)
    side[COL_KINDS:COST, :] = kinds[COLS_SHARE:, :].astype(F32)
    side[ROW_SIDE + ROWS_SHARE : TABLE, :] = kinds[0:ROWS_SHARE, :].astype(F32)
    duals[...] = jnp.broadcast_to(start[...][None], duals.shape)


def turn(pairs, turned):
    for slot in range(SLOTS):
        for part in range(2):
            rows = slice(part * TILE, (part + 1) * TILE)
            turned[slot, rows, :] = pairs[slot, rows, :].T


def ring_sums(own, right, left, opposite, payload):
    four = (own, right, left, opposite)
    payload[0:COL_BLOCKS, :] = sum_four(four, slice(0, COL_BLOCKS))
    share = 2 * COLS_SHARE
    for k, ref in enumerate(four):
        first = COL_BLOCKS + k * share
        payload[first : first + share, :] = ref[COL_BLOCKS : COL_BLOCKS + share, :]


def sums(own, right, left, opposite, total):
    total[...] = sum_four((own, right, left, opposite), slice(None))


def image_copies(kept, received, side, copies):
    block = jnp.concatenate([kept[...] + received[...], side[ROW_SIDE:TABLE, :]], 0)
    copies[...] = jnp.broadcast_to(block[None], copies.shape)


def image_sums(pieces, held):
    held[0:HALF, :] = jnp.sum(pieces[:, 0:HALF, :], 0)
    for k in range(8):
        for j in range(2):
            first = HALF + j * ROWS_SHARE
            into = HALF * (1 + j) + k * ROWS_SHARE
            held[into : into + ROWS_SHARE, :] = pieces[k, first : first + ROWS_SHARE, :]


def pair_copies(kept, received, copies):
    both = kept[...] + received[...]
    for k in range(8):
        first = HALF + k * ROWS_SHARE
        copies[k, 0:HALF, :] = both[0:HALF]
        copies[k, HALF : HALF + 8, :] = jnp.concatenate(
            [both[first : first + ROWS_SHARE], jnp.zeros((8 - ROWS_SHARE, TILE), F32)], 0
        )


def pair_sums(pieces, held):
    held[...] = jnp.sum(pieces[...], 0)


def first_adjoint(
    tiles, duals, side, payload, dual, table_out, pairs, chunks, table, done, total
):
    copies, first = [], 0
    for k, slots in enumerate(PIECES):
        part = pl.ds(first, slots)
        copies.append(pltpu.make_async_copy(tiles.at[part], chunks.at[part], done.at[k]))
        copies[k].start()
        first += slots
    table_out[...] = side[TABLE:, :].astype(jnp.int32)
    read = pltpu.make_async_copy(table_out, table, done.at[len(PIECES)])
    read.start()
    for k in range(N):
        dual[k * ROWS_SHARE : (k + 1) * ROWS_SHARE, :] = duals[k]
    total[...] = jnp.zeros_like(total)
    payload[COL_BLOCKS:, :] = side[0:COST, :]
    read.wait()

    def tile_pair(slot):
        tile = jnp.where(slot < table[COUNT, 0], chunks[slot], 0.0)
        lead = tile.astype(BF16)
        pair = jnp.concatenate([lead, (tile - lead.astype(F32)).astype(BF16)], 0)
        pairs[slot] = pair
        return pair

    first = 0
    for k, slots in enumerate(PIECES):
        copies[k].wait()
        adjoint_slots(table, tile_pair, dual, total, first, slots)
        first += slots
    payload[0:COL_BLOCKS, :] = total[:, 0, :]
    mine = own_columns(table)
    payload[mine, :] += side[0:COLS_SHARE, :] * (1.0 / STEP) - side[COST:ROW_SIDE, :]


def first_forward(
    table, own, right, left, opposite, turned, kept, given, primal, free, start, extended, total
):
    y, x, second = table[AT_Y, 0], table[AT_X, 0], table[AT_CORE, 0] == 1
    for j, (ref, late) in enumerate(((own, 0), (right, 3), (left, 1), (opposite, 2))):
        for k, early in enumerate((0, 3, 1, 2)):
            to_y = (y + jnp.where(second, early, late)) & 3
            to_x = (x + jnp.where(second, late, early)) & 3
            device = to_y * 4 + to_x
            block = pl.ds(pl.multiple_of(device * COLS_SHARE, COLS_SHARE), COLS_SHARE)
            for m, out in enumerate((start, free)):
                first = COL_BLOCKS + (2 * k + m) * COLS_SHARE
                out[block, :] = ref[first : first + COLS_SHARE, :]
    ascent = sum_four((own, right, left, opposite), slice(0, COL_BLOCKS))
    primal[...] = clamp_primal(STEP * ascent, free[...])
    extended[...] = 2.0 * primal[...] - start[...]
    forward_product(table, lambda slot: turned[slot], [extended], total)
    mine = pl.multiple_of(table[AT_CORE, 0] * HALF, HALF)
    kept[...] = total[pl.ds(mine, HALF), 0, :]
    given[...] = total[pl.ds(HALF - mine, HALF), 0, :]


def second_adjoint(table, held, other, start, side, pairs, gradient, dual, rhs, ineq, image, total):
    first = table[AT_CORE, 0] == 0
    mine, theirs = held[...], other[...]
    for core, half in enumerate((jnp.where(first, mine, theirs), jnp.where(first, theirs, mine))):
        image[core * HALF : (core + 1) * HALF, :] = half[0:HALF]
        for k in range(8):
            block = slice((2 * k + core) * ROWS_SHARE, (2 * k + core + 1) * ROWS_SHARE)
            share = slice(k * ROWS_SHARE, (k + 1) * ROWS_SHARE)
            rhs[block, :] = half[HALF : 2 * HALF][share]
            ineq[block, :] = half[2 * HALF :][share]
    dual[...] = clamp_dual(start[...] + STEP * (rhs[...] - image[...]), ineq[...])
    adjoint_product(table, lambda slot: pairs[slot], dual, total)
    gradient[...] = total[:, 0, :]
    gradient[own_columns(table), :] -= side[COST:ROW_SIDE, :]


def second_forward(
    table, own, right, left, opposite, before, free, turned, kept, given, primal, ascent, primal_mine, extended, part, done, total
):
    ascent[...] = sum_four((own, right, left, opposite), slice(0, COL_BLOCKS))
    primal[...] = clamp_primal(before[...] + STEP * ascent[...], free[...])
    extended[...] = 2.0 * primal[...] - before[...]
    part[...] = primal[own_columns(table), :]
    copy = pltpu.make_async_copy(part, primal_mine, done)
    copy.start()
    forward_product(table, lambda slot: turned[slot], [extended, primal], total)
    mine = pl.multiple_of(table[AT_CORE, 0] * HALF, HALF)
    for k, part in enumerate((0, 4)):
        rows = slice(k * HALF, (k + 1) * HALF)
        kept[rows, :] = total[pl.ds(mine, HALF), part, :]
        given[rows, :] = total[pl.ds(HALF - mine, HALF), part, :]
    copy.wait()


def row_terms(table, held, before, rhs, ineq, side, primal1, primal2, terms):
    offset = table[AT_Z, 0] * ROWS_SHARE
    share = pl.ds(table[AT_CORE, 0] * HALF + offset, ROWS_SHARE)
    image, plain = held[pl.ds(offset, ROWS_SHARE), :], held[HALF : HALF + ROWS_SHARE, :]
    earlier, bound, kind = before[share, :], rhs[share, :], ineq[share, :]
    last = clamp_dual(earlier + STEP * (bound - image), kind)
    rows = []
    for product in (plain, 0.5 * (3.0 * plain - image)):
        residual = bound - product
        residual = jnp.where(kind > 0.5, jnp.maximum(residual, 0.0), residual)
        rows.append(jnp.sum(residual * residual, 0, keepdims=True))
    columns = own_columns(table)
    price, final = side[COST:ROW_SIDE, :], primal2[columns, :]
    for primal, value in (
        (final, last),
        (0.5 * (primal1[columns, :] + final), 0.5 * (earlier + last)),
    ):
        gain = jnp.sum(price * primal, 0, keepdims=True)
        rows.append(gain - jnp.sum(bound * value, 0, keepdims=True))
    terms[...] = jnp.concatenate(rows + rows, 0)


def third_adjoint(
    table, held, other, before, rhs, ineq, side, terms, pairs, payload, mine, image, dual, part, done, total
):
    half = pl.multiple_of(table[AT_CORE, 0] * HALF, HALF)
    image[pl.ds(half, HALF), :] = held[0:HALF, :]
    image[pl.ds(HALF - half, HALF), :] = other[0:HALF, :]
    dual[...] = clamp_dual(before[...] + STEP * (rhs[...] - image[...]), ineq[...])
    part[...] = dual[pl.ds(index_col(table) * ROWS_SHARE, ROWS_SHARE), :]
    copy = pltpu.make_async_copy(part, mine, done)
    copy.start()
    adjoint_product(table, lambda slot: pairs[slot], dual, total)
    payload[0:COL_BLOCKS, :] = total[:, 0, :]
    payload[COL_BLOCKS : COL_BLOCKS + 8, :] = terms[...]
    payload[own_columns(table), :] -= side[COST:ROW_SIDE, :]
    copy.wait()


def column_terms(own, right, left, opposite, earlier, free, terms):
    four = (own, right, left, opposite)
    ascent = sum_four(four, slice(0, COL_BLOCKS))
    row_terms = sum_four(four, slice(COL_BLOCKS, COL_BLOCKS + 8))
    kind = free[...]
    squares, gaps = [], []
    for k, reduced in enumerate((-ascent, -0.5 * (earlier[...] + ascent))):
        low = jnp.minimum(reduced, 0.0)
        violation = jnp.where(kind > 0.5, low, 0.0)
        box = jnp.where(kind > 0.5, 0.0, low)
        squares.append(jnp.sum(violation * violation, 0, keepdims=True))
        gaps.append(row_terms[2 + k : 3 + k] - jnp.sum(box, 0, keepdims=True))
    rows = jnp.concatenate([row_terms[0:2]] + squares + gaps + squares, 0)
    sums = jnp.broadcast_to(jnp.sum(rows, 1, keepdims=True), rows.shape)
    places = [lax.broadcasted_iota(jnp.int32, rows.shape, k) for k in range(2)]
    line = jnp.sum(jnp.where(places[0] == places[1], sums, 0.0), 0, keepdims=True)
    terms[...] = jnp.broadcast_to(line[None], terms.shape)


def measures(gathered, primal_residual, dual_residual, gap):
    line = jnp.sum(gathered[...], 0)
    lane = lax.broadcasted_iota(jnp.int32, line.shape, 1)
    for k, (out, size) in enumerate(
        ((primal_residual, NROWS), (dual_residual, NCOLS), (gap, NCOLS))
    ):
        for j in range(2):
            out[j] = jnp.sum(jnp.where(lane == 2 * k + j, line, 0.0)) * (1.0 / size)


def shift(values, phase, step):
    pairs = []
    for y in range(4):
        for x in range(4):
            for core in range(2):
                to_y, to_x = (y, (x + step) % 4) if core == phase else ((y + step) % 4, x)
                pairs.append(((y * 4 + x) * 2 + core, (to_y * 4 + to_x) * 2 + core))
    return lax.ppermute(values, ("y", "x", "core"), pairs)


def four_of(values, phase):
    return values, shift(values, phase, 1), shift(values, phase, -1), shift(values, phase, 2)


def four_over_row(values):
    total = call(sums, "sums", [(values.shape, F32)], four_of(values, 0))
    return four_of(total[0], 1)


def swap_cores(values):
    return lax.ppermute(values, "core", [(0, 1), (1, 0)])


def exchange(copies, axes):
    return lax.all_to_all(copies, axes, 0, 0)


def shards(
    tiles, tile_rows, tile_cols, tile_count, row_types, var_types, rhs, cost, primal_start, dual_start
):
    tiles = tiles.reshape(SLOTS, TILE, TILE)
    blocks, columns, half = (ROW_BLOCKS, TILE), (COL_BLOCKS, TILE), (HALF, TILE)
    row_total = [pltpu.VMEM((ROW_BLOCKS, 8, TILE), F32)]
    col_total = [pltpu.VMEM((COL_BLOCKS, 8, TILE), F32)]

    duals, side = call(
        pack,
        "pack",
        [((N, ROWS_SHARE, TILE), F32), ((SIDE, TILE), F32)],
        (tile_count, tile_rows, tile_cols, row_types, rhs, dual_start, var_types, cost, primal_start),
        smem=1,
        hbm=8,
        scratch=[
            pltpu.VMEM((2, SLOTS), jnp.int32),
            pltpu.VMEM((2 * COLS_SHARE, TILE), jnp.int32),
            pltpu.VMEM((ROWS_SHARE, TILE), F32),
            pltpu.SemaphoreType.DMA((8,)),
        ],
        vmem=PACK_VMEM,
    )

    payload, dual0, table, pairs = call(
        first_adjoint,
        "first_adjoint",
        [
            ((COL_BLOCKS + 2 * COLS_SHARE, TILE), F32),
            (blocks, F32),
            ((8, TILE), jnp.int32),
            ((SLOTS, 2 * TILE, TILE), BF16),
        ],
        (tiles, exchange(duals, ("z", "core")), side),
        hbm=1,
        scratch=[
            pltpu.VMEM((SLOTS, TILE, TILE), F32),
            pltpu.SMEM((8, TILE), jnp.int32),
            pltpu.SemaphoreType.DMA((len(PIECES) + 1,)),
        ]
        + col_total,
        vmem=FIRST_VMEM,
    )
    turned = call(
        turn,
        "turn",
        [((SLOTS, 2 * TILE, TILE), BF16)],
        (pairs,),
        cost=pl.CostEstimate(flops=0, bytes_accessed=2**23, transcendentals=0),
    )[0]
    payload = call(
        ring_sums, "ring_sums", [((COL_BLOCKS + 8 * COLS_SHARE, TILE), F32)], four_of(payload, 0)
    )

    kept, given, primal1, free = call(
        first_forward,
        "first_forward",
        [(half, F32)] * 2 + [(columns, F32)] * 2,
        (table, *four_of(payload[0], 1), turned),
        smem=1,
        scratch=[pltpu.VMEM(columns, F32)] * 2 + row_total,
    )
    copies = call(
        image_copies,
        "image_copies",
        [((8, HALF + 2 * ROWS_SHARE, TILE), F32)],
        (kept, swap_cores(given), side),
    )
    held = call(
        image_sums, "image_sums", [((3 * HALF, TILE), F32)], (exchange(copies[0], "z"),)
    )[0]

    gradient, dual1, rhs_full, ineq = call(
        second_adjoint,
        "second_adjoint",
        [(columns, F32)] + [(blocks, F32)] * 3,
        (table, held, swap_cores(held), dual0, side, pairs),
        smem=1,
        scratch=[pltpu.VMEM(blocks, F32)] + col_total,
    )

    kept, given, primal2, ascent2, primal_mine = call(
        second_forward,
        "second_forward",
        [(blocks, F32)] * 2 + [(columns, F32)] * 2 + [((COLS_SHARE, TILE), F32)],
        (table, *four_over_row(gradient), primal1, free, turned),
        smem=1,
        hbm_out=(4,),
        scratch=[pltpu.VMEM(columns, F32), pltpu.VMEM((COLS_SHARE, TILE), F32), pltpu.SemaphoreType.DMA]
        + row_total,
    )
    copies = call(
        pair_copies, "pair_copies", [((8, HALF + 8, TILE), F32)], (kept, swap_cores(given))
    )
    held = call(pair_sums, "pair_sums", [((HALF + 8, TILE), F32)], (exchange(copies[0], "z"),))[0]
    other = swap_cores(held)
    terms = call(
        row_terms,
        "row_terms",
        [((8, TILE), F32)],
        (table, held, dual1, rhs_full, ineq, side, primal1, primal2),
        smem=1,
        cost=pl.CostEstimate(flops=0, bytes_accessed=2**21, transcendentals=0),
    )[0]

    payload, dual_mine = call(
        third_adjoint,
        "third_adjoint",
        [((COL_BLOCKS + 8, TILE), F32), ((ROWS_SHARE, TILE), F32)],
        (table, held, other, dual1, rhs_full, ineq, side, terms, pairs),
        smem=1,
        hbm_out=(1,),
        scratch=[pltpu.VMEM(blocks, F32)] * 2
        + [pltpu.VMEM((ROWS_SHARE, TILE), F32), pltpu.SemaphoreType.DMA]
        + col_total,
    )
    terms = call(
        column_terms,
        "column_terms",
        [((N, 1, TILE), F32)],
        (*four_over_row(payload), ascent2, free),
    )
    primal_residual, dual_residual, gap = call(
        measures,
        "measures",
        [((2,), F32)] * 3,
        (exchange(terms[0], ("z", "core")),),
        smem_out=True,
    )
    return primal_mine[None], dual_mine[None], primal_residual, dual_residual, gap


def solution(mesh):
    rings = Mesh(mesh.devices.reshape(4, 4, 8, 2), ("y", "x", "z", "core"))
    row, col = ("y", "x"), ("z", "core")
    in_specs = (
        P(row, col, None, None, None),
        P(row, col, None),
        P(row, col, None),
        P(row, col),
        P(row, col, None),
        P(col, row, None),
        P(row, col, None),
        P(col, row, None),
        P(col, row, None),
        P(row, col, None),
    )
    out_specs = (P(col, row, None), P(row, col, None), P(), P(), P())
    return jax.shard_map(shards, mesh=rings, in_specs=in_specs, out_specs=out_specs, check_vma=False)
```

```python
import jax
import jax.numpy as jnp
from jax import lax
from jax.experimental import pallas as pl
from jax.experimental.pallas import tpu as pltpu
from jax.sharding import Mesh
from jax.sharding import PartitionSpec as P

N = 16
TILE = 128
ROW_BLOCKS = 64
COL_BLOCKS = 128
SLOTS = 64
ROWS_SHARE = ROW_BLOCKS // N
COLS_SHARE = COL_BLOCKS // N
HALF = ROW_BLOCKS // 2
NROWS = float(N * ROW_BLOCKS * TILE)
NCOLS = float(N * COL_BLOCKS * TILE)
PACK_VMEM = 60 * 2**20
FIRST_VMEM = 48 * 2**20
PIECES = (8, 16, 16, 16, 8)
F32, BF16 = jnp.float32, jnp.bfloat16

SLOT_ROWS, SLOT_COLS, COUNT, AT_Y, AT_X, AT_Z, AT_CORE = range(7)
COL_KINDS, COST, ROW_SIDE, TABLE, SIDE = 8, 16, 24, 32, 40
STEP = 0.4

VMEM = pl.BlockSpec(memory_space=pltpu.VMEM)
SMEM = pl.BlockSpec(memory_space=pltpu.SMEM)
HBM = pl.BlockSpec(memory_space=pltpu.HBM)


def call(kernel, name, out_shapes, args, smem=0, hbm=0, smem_out=0, scratch=(), vmem=8 * 2**20, cost=None):
    shapes = tuple(jax.ShapeDtypeStruct(s, d) for s, d in out_shapes)
    return pl.pallas_call(
        kernel,
        name=name,
        out_shape=shapes,
        in_specs=[SMEM] * smem + [HBM] * hbm + [VMEM] * (len(args) - smem - hbm),
        out_specs=tuple([SMEM] * smem_out + [VMEM] * (len(shapes) - smem_out)),
        scratch_shapes=list(scratch),
        compiler_params=pltpu.CompilerParams(vmem_limit_bytes=vmem),
        cost_estimate=cost,
    )(*args)


def split(vector, copies):
    wide = jnp.broadcast_to(vector, (copies, TILE))
    lead = wide.astype(BF16).astype(F32)
    return [lead, wide - lead]


def adjoint_product(table, tile_pair, dual_ref, total):
    total[...] = jnp.zeros_like(total)
    adjoint_slots(table, tile_pair, dual_ref, total, 0, SLOTS)


def adjoint_slots(table, tile_pair, dual_ref, total, first, slots):
    def body(slot, carry):
        lhs = jnp.concatenate(split(dual_ref[pl.ds(table[SLOT_ROWS, slot], 1), :], 8), 0).astype(BF16)
        lhs = jnp.concatenate([lhs, lhs], 1)
        product = jnp.dot(lhs, tile_pair(slot), preferred_element_type=F32)
        total[table[SLOT_COLS, slot]] += product[0:8] + product[8:16]
        return carry

    lax.fori_loop(first, first + slots, body, 0, unroll=slots)


def forward_product(table, tile_pair, primal_refs, total):
    total[...] = jnp.zeros_like(total)
    copies = 8 // len(primal_refs)

    def body(slot, carry):
        parts = [split(ref[pl.ds(table[SLOT_COLS, slot], 1), :], copies) for ref in primal_refs]
        lhs = jnp.concatenate([p[0] for p in parts] + [p[1] for p in parts], 0).astype(BF16)
        lhs = jnp.concatenate([lhs, lhs], 1)
        product = jnp.dot(lhs, tile_pair(slot), preferred_element_type=F32)
        total[table[SLOT_ROWS, slot]] += product[0:8] + product[8:16]
        return carry

    lax.fori_loop(0, SLOTS, body, 0, unroll=SLOTS)


def clamp_primal(values, free):
    floor = jnp.maximum(values, 0.0)
    return jnp.where(free > 0.5, floor, jnp.minimum(floor, 1.0))


def clamp_dual(values, ineq):
    return jnp.where(ineq > 0.5, jnp.maximum(values, 0.0), values)


def own_columns(table):
    index = table[AT_Y, 0] * 4 + table[AT_X, 0]
    return pl.ds(pl.multiple_of(index * COLS_SHARE, COLS_SHARE), COLS_SHARE)


def index_col(table):
    return table[AT_Z, 0] * 2 + table[AT_CORE, 0]


def sum_four(refs, rows):
    own, right, left, opposite = (ref[rows, :] for ref in refs)
    return (own + opposite) + (right + left)


def pack(
    count, rows, cols, row_kinds, rhs, dual, col_kinds, cost, primal, duals, side, places, kinds, start, done
):
    copies = [
        pltpu.make_async_copy(source, target, done.at[k])
        for k, (source, target) in enumerate(
            (
                (rows.at[0], places.at[0:1]),
                (cols.at[0], places.at[1:2]),
                (dual.at[0], start),
                (rhs.at[0], side.at[ROW_SIDE : ROW_SIDE + ROWS_SHARE]),
                (row_kinds.at[0], kinds.at[0:ROWS_SHARE]),
                (primal.at[0], side.at[0:COLS_SHARE]),
                (cost.at[0], side.at[COST:ROW_SIDE]),
                (col_kinds.at[0], kinds.at[COLS_SHARE : 2 * COLS_SHARE]),
            )
        )
    ]
    for copy in copies:
        copy.start()
    side[TABLE + COUNT :, :] = jnp.zeros((SIDE - TABLE - COUNT, TILE), F32)
    for k, value in (
        (COUNT, count[0, 0]),
        (AT_Y, lax.axis_index("y")),
        (AT_X, lax.axis_index("x")),
        (AT_Z, lax.axis_index("z")),
        (AT_CORE, lax.axis_index("core")),
    ):
        side[TABLE + k : TABLE + k + 1, :] = jnp.full((1, TILE), value, jnp.int32).astype(F32)
    side[TABLE : TABLE + COUNT, :] = jnp.zeros((COUNT, TILE), F32)
    for copy in copies:
        copy.wait()
    side[TABLE : TABLE + COUNT, 0:SLOTS] = places[...].astype(F32)
    side[COL_KINDS:COST, :] = kinds[COLS_SHARE:, :].astype(F32)
    side[ROW_SIDE + ROWS_SHARE : TABLE, :] = kinds[0:ROWS_SHARE, :].astype(F32)
    duals[...] = jnp.broadcast_to(start[...][None], duals.shape)


def turn(pairs, turned):
    for slot in range(SLOTS):
        for part in range(2):
            rows = slice(part * TILE, (part + 1) * TILE)
            turned[slot, rows, :] = pairs[slot, rows, :].T


def ring_sums(own, right, left, opposite, payload):
    four = (own, right, left, opposite)
    payload[0:COL_BLOCKS, :] = sum_four(four, slice(0, COL_BLOCKS))
    share = 2 * COLS_SHARE
    for k, ref in enumerate(four):
        first = COL_BLOCKS + k * share
        payload[first : first + share, :] = ref[COL_BLOCKS : COL_BLOCKS + share, :]


def sums(own, right, left, opposite, total):
    total[...] = sum_four((own, right, left, opposite), slice(None))


def image_copies(kept, received, side, copies):
    block = jnp.concatenate([kept[...] + received[...], side[ROW_SIDE:TABLE, :]], 0)
    copies[...] = jnp.broadcast_to(block[None], copies.shape)


def image_sums(pieces, held):
    held[0:HALF, :] = jnp.sum(pieces[:, 0:HALF, :], 0)
    for k in range(8):
        for j in range(2):
            first = HALF + j * ROWS_SHARE
            into = HALF * (1 + j) + k * ROWS_SHARE
            held[into : into + ROWS_SHARE, :] = pieces[k, first : first + ROWS_SHARE, :]


def pair_copies(kept, received, copies):
    both = kept[...] + received[...]
    for k in range(8):
        first = HALF + k * ROWS_SHARE
        copies[k, 0:HALF, :] = both[0:HALF]
        copies[k, HALF : HALF + 8, :] = jnp.concatenate(
            [both[first : first + ROWS_SHARE], jnp.zeros((8 - ROWS_SHARE, TILE), F32)], 0
        )


def pair_sums(pieces, held):
    held[...] = jnp.sum(pieces[...], 0)


def first_adjoint(
    tiles, duals, side, payload, dual, table_out, pairs, chunks, table, done, total
):
    copies, first = [], 0
    for k, slots in enumerate(PIECES):
        part = pl.ds(first, slots)
        copies.append(pltpu.make_async_copy(tiles.at[part], chunks.at[part], done.at[k]))
        copies[k].start()
        first += slots
    table_out[...] = side[TABLE:, :].astype(jnp.int32)
    read = pltpu.make_async_copy(table_out, table, done.at[len(PIECES)])
    read.start()
    for k in range(N):
        dual[k * ROWS_SHARE : (k + 1) * ROWS_SHARE, :] = duals[k]
    total[...] = jnp.zeros_like(total)
    payload[COL_BLOCKS:, :] = side[0:COST, :]
    read.wait()

    def tile_pair(slot):
        tile = jnp.where(slot < table[COUNT, 0], chunks[slot], 0.0)
        lead = tile.astype(BF16)
        pair = jnp.concatenate([lead, (tile - lead.astype(F32)).astype(BF16)], 0)
        pairs[slot] = pair
        return pair

    first = 0
    for k, slots in enumerate(PIECES):
        copies[k].wait()
        adjoint_slots(table, tile_pair, dual, total, first, slots)
        first += slots
    payload[0:COL_BLOCKS, :] = total[:, 0, :]
    mine = own_columns(table)
    payload[mine, :] += side[0:COLS_SHARE, :] * (1.0 / STEP) - side[COST:ROW_SIDE, :]


def first_forward(
    table, own, right, left, opposite, turned, kept, given, primal, free, start, extended, total
):
    y, x, second = table[AT_Y, 0], table[AT_X, 0], table[AT_CORE, 0] == 1
    for j, (ref, late) in enumerate(((own, 0), (right, 3), (left, 1), (opposite, 2))):
        for k, early in enumerate((0, 3, 1, 2)):
            to_y = (y + jnp.where(second, early, late)) & 3
            to_x = (x + jnp.where(second, late, early)) & 3
            device = to_y * 4 + to_x
            block = pl.ds(pl.multiple_of(device * COLS_SHARE, COLS_SHARE), COLS_SHARE)
            for m, out in enumerate((start, free)):
                first = COL_BLOCKS + (2 * k + m) * COLS_SHARE
                out[block, :] = ref[first : first + COLS_SHARE, :]
    ascent = sum_four((own, right, left, opposite), slice(0, COL_BLOCKS))
    primal[...] = clamp_primal(STEP * ascent, free[...])
    extended[...] = 2.0 * primal[...] - start[...]
    forward_product(table, lambda slot: turned[slot], [extended], total)
    mine = pl.multiple_of(table[AT_CORE, 0] * HALF, HALF)
    kept[...] = total[pl.ds(mine, HALF), 0, :]
    given[...] = total[pl.ds(HALF - mine, HALF), 0, :]


def second_adjoint(table, held, other, start, side, pairs, gradient, dual, rhs, ineq, image, total):
    first = table[AT_CORE, 0] == 0
    mine, theirs = held[...], other[...]
    for core, half in enumerate((jnp.where(first, mine, theirs), jnp.where(first, theirs, mine))):
        image[core * HALF : (core + 1) * HALF, :] = half[0:HALF]
        for k in range(8):
            block = slice((2 * k + core) * ROWS_SHARE, (2 * k + core + 1) * ROWS_SHARE)
            share = slice(k * ROWS_SHARE, (k + 1) * ROWS_SHARE)
            rhs[block, :] = half[HALF : 2 * HALF][share]
            ineq[block, :] = half[2 * HALF :][share]
    dual[...] = clamp_dual(start[...] + STEP * (rhs[...] - image[...]), ineq[...])
    adjoint_product(table, lambda slot: pairs[slot], dual, total)
    gradient[...] = total[:, 0, :]
    gradient[own_columns(table), :] -= side[COST:ROW_SIDE, :]


def second_forward(
    table, own, right, left, opposite, before, free, turned, kept, given, primal, ascent, primal_mine, extended, total
):
    ascent[...] = sum_four((own, right, left, opposite), slice(0, COL_BLOCKS))
    primal[...] = clamp_primal(before[...] + STEP * ascent[...], free[...])
    extended[...] = 2.0 * primal[...] - before[...]
    primal_mine[...] = primal[own_columns(table), :]
    forward_product(table, lambda slot: turned[slot], [extended, primal], total)
    mine = pl.multiple_of(table[AT_CORE, 0] * HALF, HALF)
    for k, part in enumerate((0, 4)):
        rows = slice(k * HALF, (k + 1) * HALF)
        kept[rows, :] = total[pl.ds(mine, HALF), part, :]
        given[rows, :] = total[pl.ds(HALF - mine, HALF), part, :]


def row_terms(table, held, before, rhs, ineq, side, primal1, primal2, terms):
    offset = table[AT_Z, 0] * ROWS_SHARE
    share = pl.ds(table[AT_CORE, 0] * HALF + offset, ROWS_SHARE)
    image, plain = held[pl.ds(offset, ROWS_SHARE), :], held[HALF : HALF + ROWS_SHARE, :]
    earlier, bound, kind = before[share, :], rhs[share, :], ineq[share, :]
    last = clamp_dual(earlier + STEP * (bound - image), kind)
    rows = []
    for product in (plain, 0.5 * (3.0 * plain - image)):
        residual = bound - product
        residual = jnp.where(kind > 0.5, jnp.maximum(residual, 0.0), residual)
        rows.append(jnp.sum(residual * residual, 0, keepdims=True))
    columns = own_columns(table)
    price, final = side[COST:ROW_SIDE, :], primal2[columns, :]
    for primal, value in (
        (final, last),
        (0.5 * (primal1[columns, :] + final), 0.5 * (earlier + last)),
    ):
        gain = jnp.sum(price * primal, 0, keepdims=True)
        rows.append(gain - jnp.sum(bound * value, 0, keepdims=True))
    terms[...] = jnp.concatenate(rows + rows, 0)


def third_adjoint(
    table, held, other, before, rhs, ineq, side, terms, pairs, payload, mine, dual, image, total
):
    half = pl.multiple_of(table[AT_CORE, 0] * HALF, HALF)
    image[pl.ds(half, HALF), :] = held[0:HALF, :]
    image[pl.ds(HALF - half, HALF), :] = other[0:HALF, :]
    dual[...] = clamp_dual(before[...] + STEP * (rhs[...] - image[...]), ineq[...])
    mine[...] = dual[pl.ds(index_col(table) * ROWS_SHARE, ROWS_SHARE), :]
    adjoint_product(table, lambda slot: pairs[slot], dual, total)
    payload[0:COL_BLOCKS, :] = total[:, 0, :]
    payload[COL_BLOCKS : COL_BLOCKS + 8, :] = terms[...]
    payload[own_columns(table), :] -= side[COST:ROW_SIDE, :]


def column_terms(own, right, left, opposite, earlier, free, terms):
    four = (own, right, left, opposite)
    ascent = sum_four(four, slice(0, COL_BLOCKS))
    row_terms = sum_four(four, slice(COL_BLOCKS, COL_BLOCKS + 8))
    kind = free[...]
    squares, gaps = [], []
    for k, reduced in enumerate((-ascent, -0.5 * (earlier[...] + ascent))):
        low = jnp.minimum(reduced, 0.0)
        violation = jnp.where(kind > 0.5, low, 0.0)
        box = jnp.where(kind > 0.5, 0.0, low)
        squares.append(jnp.sum(violation * violation, 0, keepdims=True))
        gaps.append(row_terms[2 + k : 3 + k] - jnp.sum(box, 0, keepdims=True))
    rows = jnp.concatenate([row_terms[0:2]] + squares + gaps + squares, 0)
    sums = jnp.broadcast_to(jnp.sum(rows, 1, keepdims=True), rows.shape)
    places = [lax.broadcasted_iota(jnp.int32, rows.shape, k) for k in range(2)]
    line = jnp.sum(jnp.where(places[0] == places[1], sums, 0.0), 0, keepdims=True)
    terms[...] = jnp.broadcast_to(line[None], terms.shape)


def measures(
    gathered, primal_part, dual_part, primal_residual, dual_residual, gap, primal_mine, dual_mine
):
    primal_mine[...] = primal_part[...]
    dual_mine[...] = dual_part[...]
    line = jnp.sum(gathered[...], 0)
    lane = lax.broadcasted_iota(jnp.int32, line.shape, 1)
    for k, (out, size) in enumerate(
        ((primal_residual, NROWS), (dual_residual, NCOLS), (gap, NCOLS))
    ):
        for j in range(2):
            out[j] = jnp.sum(jnp.where(lane == 2 * k + j, line, 0.0)) * (1.0 / size)


def shift(values, phase, step):
    pairs = []
    for y in range(4):
        for x in range(4):
            for core in range(2):
                to_y, to_x = (y, (x + step) % 4) if core == phase else ((y + step) % 4, x)
                pairs.append(((y * 4 + x) * 2 + core, (to_y * 4 + to_x) * 2 + core))
    return lax.ppermute(values, ("y", "x", "core"), pairs)


def four_of(values, phase):
    return values, shift(values, phase, 1), shift(values, phase, -1), shift(values, phase, 2)


def four_over_row(values):
    total = call(sums, "sums", [(values.shape, F32)], four_of(values, 0))
    return four_of(total[0], 1)


def swap_cores(values):
    return lax.ppermute(values, "core", [(0, 1), (1, 0)])


def exchange(copies, axes):
    return lax.all_to_all(copies, axes, 0, 0)


def shards(
    tiles, tile_rows, tile_cols, tile_count, row_types, var_types, rhs, cost, primal_start, dual_start
):
    tiles = tiles.reshape(SLOTS, TILE, TILE)
    blocks, columns, half = (ROW_BLOCKS, TILE), (COL_BLOCKS, TILE), (HALF, TILE)
    row_total = [pltpu.VMEM((ROW_BLOCKS, 8, TILE), F32)]
    col_total = [pltpu.VMEM((COL_BLOCKS, 8, TILE), F32)]

    duals, side = call(
        pack,
        "pack",
        [((N, ROWS_SHARE, TILE), F32), ((SIDE, TILE), F32)],
        (tile_count, tile_rows, tile_cols, row_types, rhs, dual_start, var_types, cost, primal_start),
        smem=1,
        hbm=8,
        scratch=[
            pltpu.VMEM((2, SLOTS), jnp.int32),
            pltpu.VMEM((2 * COLS_SHARE, TILE), jnp.int32),
            pltpu.VMEM((ROWS_SHARE, TILE), F32),
            pltpu.SemaphoreType.DMA((8,)),
        ],
        vmem=PACK_VMEM,
    )

    payload, dual0, table, pairs = call(
        first_adjoint,
        "first_adjoint",
        [
            ((COL_BLOCKS + 2 * COLS_SHARE, TILE), F32),
            (blocks, F32),
            ((8, TILE), jnp.int32),
            ((SLOTS, 2 * TILE, TILE), BF16),
        ],
        (tiles, exchange(duals, ("z", "core")), side),
        hbm=1,
        scratch=[
            pltpu.VMEM((SLOTS, TILE, TILE), F32),
            pltpu.SMEM((8, TILE), jnp.int32),
            pltpu.SemaphoreType.DMA((len(PIECES) + 1,)),
        ]
        + col_total,
        vmem=FIRST_VMEM,
    )
    turned = call(
        turn,
        "turn",
        [((SLOTS, 2 * TILE, TILE), BF16)],
        (pairs,),
        cost=pl.CostEstimate(flops=0, bytes_accessed=2**23, transcendentals=0),
    )[0]
    payload = call(
        ring_sums, "ring_sums", [((COL_BLOCKS + 8 * COLS_SHARE, TILE), F32)], four_of(payload, 0)
    )

    kept, given, primal1, free = call(
        first_forward,
        "first_forward",
        [(half, F32)] * 2 + [(columns, F32)] * 2,
        (table, *four_of(payload[0], 1), turned),
        smem=1,
        scratch=[pltpu.VMEM(columns, F32)] * 2 + row_total,
    )
    copies = call(
        image_copies,
        "image_copies",
        [((8, HALF + 2 * ROWS_SHARE, TILE), F32)],
        (kept, swap_cores(given), side),
    )
    held = call(
        image_sums, "image_sums", [((3 * HALF, TILE), F32)], (exchange(copies[0], "z"),)
    )[0]

    gradient, dual1, rhs_full, ineq = call(
        second_adjoint,
        "second_adjoint",
        [(columns, F32)] + [(blocks, F32)] * 3,
        (table, held, swap_cores(held), dual0, side, pairs),
        smem=1,
        scratch=[pltpu.VMEM(blocks, F32)] + col_total,
    )

    kept, given, primal2, ascent2, primal_part = call(
        second_forward,
        "second_forward",
        [(blocks, F32)] * 2 + [(columns, F32)] * 2 + [((COLS_SHARE, TILE), F32)],
        (table, *four_over_row(gradient), primal1, free, turned),
        smem=1,
        scratch=[pltpu.VMEM(columns, F32)] + row_total,
    )
    copies = call(
        pair_copies, "pair_copies", [((8, HALF + 8, TILE), F32)], (kept, swap_cores(given))
    )
    held = call(pair_sums, "pair_sums", [((HALF + 8, TILE), F32)], (exchange(copies[0], "z"),))[0]
    other = swap_cores(held)
    terms = call(
        row_terms,
        "row_terms",
        [((8, TILE), F32)],
        (table, held, dual1, rhs_full, ineq, side, primal1, primal2),
        smem=1,
        cost=pl.CostEstimate(flops=0, bytes_accessed=2**21, transcendentals=0),
    )[0]

    payload, dual_part = call(
        third_adjoint,
        "third_adjoint",
        [((COL_BLOCKS + 8, TILE), F32), ((ROWS_SHARE, TILE), F32)],
        (table, held, other, dual1, rhs_full, ineq, side, terms, pairs),
        smem=1,
        scratch=[pltpu.VMEM(blocks, F32)] * 2 + col_total,
    )
    terms = call(
        column_terms,
        "column_terms",
        [((N, 1, TILE), F32)],
        (*four_over_row(payload), ascent2, free),
    )
    primal_residual, dual_residual, gap, primal_mine, dual_mine = call(
        measures,
        "measures",
        [((2,), F32)] * 3 + [((COLS_SHARE, TILE), F32), ((ROWS_SHARE, TILE), F32)],
        (exchange(terms[0], ("z", "core")), primal_part, dual_part),
        smem_out=3,
    )
    return primal_mine[None], dual_mine[None], primal_residual, dual_residual, gap


def solution(mesh):
    rings = Mesh(mesh.devices.reshape(4, 4, 8, 2), ("y", "x", "z", "core"))
    row, col = ("y", "x"), ("z", "core")
    in_specs = (
        P(row, col, None, None, None),
        P(row, col, None),
        P(row, col, None),
        P(row, col),
        P(row, col, None),
        P(col, row, None),
        P(row, col, None),
        P(col, row, None),
        P(col, row, None),
        P(row, col, None),
    )
    out_specs = (P(col, row, None), P(row, col, None), P(), P(), P())
    return jax.shard_map(shards, mesh=rings, in_specs=in_specs, out_specs=out_specs, check_vma=False)
```
